128 devices in a mesh: gx: 16 (over y, x), gy: 8 (over z, core).
Axes of the slice: x: 4, y: 4, z: 4, core: 2. Of those that a mesh axis runs over, the one named last changes fastest.
Arguments:
- velocity: float32 [3, 32, 512, 4096], P(None, None, 'gx', 'gy'), may hold values from -6 to 6
- fiber_points: float32 [1024, 3, 128], P(('gx', 'gy')), may hold values from -6 to 6
- stiffness: float32 [1024], P(('gx', 'gy')), may hold values from 0.5 to 2
- links: int32 [1024, 128], P(('gx', 'gy')), may hold values from 1 to 127
- delta_weights: bfloat16 [1024, 8, 128, 512], P(('gx', 'gy')), may hold values from -0.5 to 0.5
- owners: int32 [1024, 8, 1], P(('gx', 'gy')), may hold values from 0 to 127; in each aligned block of 64 rows (0 to 63, 64 to 127, ..., all dimensions but the last counted through in order) at most 2 rows name the same one
- patch_slots: int32 [1024, 8], P(('gx', 'gy')), may hold values from 0 to 1023
Outputs:
- fluid: float32 [3, 32, 512, 4096], P(None, None, 'gx', 'gy')
- moved_points: float32 [1024, 3, 128], P(('gx', 'gy'))
The draws below stay inside these ranges and needn't reach their ends.
Inputs may be any that keep to these rules, and one draw needn't show every extreme that they name: owners counts devices in the order gx slower, gy faster; among the rows of one device, no owner is named more than 2 times, a bound that some block reaches.
All inputs are finite; a program needn't handle non-finite values.
Results may differ from the reference program's by a relative error of at most 0.0037.
Values may be sent and summed in bfloat16 or wider, within the bound.
No kernel may reach another device: no remote copies, remote signals or barrier semaphores. Data moves between devices by JAX's collectives and lax.ppermute only.
A program may use at most 128 MiB of HBM per device.

```python
import math
import jax
import jax.numpy as jnp
import numpy as np
from jax import lax

CX = 32
CY = 512
NZ = 32
PATCH = 512
FBP = 128
FBD = 8
INTERSECTION = 8
STEPS = 2
NX = 512
NY = 4096
CAP = 2
P_DEV = 1024
FIBERS_B = 1024
N_GX = 16
N_GY = 8
DEVICES = 128


def set_ends(drawn, own_key, smallest, high):
    longest = drawn.shape.index(max(drawn.shape))
    spots = []
    for shift in (0, 1):
        where = [jax.random.randint(jax.random.fold_in(own_key, axis), (), 0, length) for axis, length in enumerate(drawn.shape)]
        where[longest] = (where[longest] + shift) % drawn.shape[longest]
        spots.append(tuple(where))
    return drawn.at[spots[0]].set(smallest).at[spots[1]].set(high)


def steps_of(own_key, shape, split, least, largest):
    gain, own = 1.0, jax.random.fold_in(own_key, 6)
    for axis_at, blocks in split:
        draws = jnp.exp(jax.random.uniform(jax.random.fold_in(own, axis_at), (blocks,), jnp.float32, least / len(split), largest / len(split)))
        gain = gain * jnp.repeat(draws, shape[axis_at] // blocks).reshape([-1 if axis == axis_at else 1 for axis in range(len(shape))])
    return gain


def deal_out(key, own, number, rows, amount, top, most, slope):
    order = jax.random.permutation(key, amount)
    crowded, common = load_shares(amount, rows * top, most, slope, True), load_shares(amount, rows * top, most, slope, False)
    places = jnp.arange(amount)

    def named(lengths, turn):
        used = int((lengths > 0).sum())
        fixed = max(1, used // 4)
        passed = fixed + (places - fixed + turn * (used - fixed)) % max(1, amount - fixed)
        return jnp.zeros((amount,), jnp.int32).at[order[jnp.where(places < fixed, places, passed)]].set(jnp.asarray(lengths, jnp.int32))

    lengths = jnp.where(number % 4 == 0, named(crowded, number // 4), named(common, number - number // 4 - 1))
    mixed = jax.random.permutation(jax.random.fold_in(own, 3), amount)
    donor, taker = mixed[0:amount // 2 * 2:2], mixed[1:amount // 2 * 2:2]
    margin = jnp.minimum(lengths[donor] - 1, most - lengths[taker]) // 2
    margin = jnp.where((donor == order[0]) | (taker == order[0]) | (lengths[taker] == 0), 0, jnp.maximum(margin, 0))
    passed = jax.random.randint(jax.random.fold_in(own, 4), (amount // 2,), 0, 1 << 20) % (margin + 1)
    lengths = lengths.at[donor].add(-passed).at[taker].add(passed)
    labels = jnp.searchsorted(jnp.cumsum(lengths), jnp.arange(rows * top), side="right").astype(jnp.int32)
    grid = labels.reshape(top, rows).T
    grid = grid[jax.random.permutation(jax.random.fold_in(own, 1), rows)]
    turn = jax.random.randint(jax.random.fold_in(own, 2), (rows, 1), 0, top)
    return jnp.take_along_axis(grid, (jnp.arange(top)[None, :] + turn) % top, axis=1)


def load_shares(amount, total, limit, slope, full):
    portions = [(1 << 20) // math.isqrt(rank ** slope) + 1 for rank in range(1, amount + 1)]
    largest = limit if full else min(limit, max(-(-total // amount), total * portions[0] // sum(portions)))
    least = 1 if total - largest >= amount - 1 else 0
    given, surplus = [largest] + [least] * (amount - 1), total - largest - least * (amount - 1)
    while surplus > 0:
        candidates = [i for i in range(1, amount) if given[i] < largest] or [i for i in range(1, amount) if given[i] < limit]
        mass, left = sum([portions[i] for i in candidates]), surplus
        for i in candidates:
            more = min(limit - given[i], max(1, left * portions[i] // mass), surplus)
            given[i] = given[i] + more
            surplus = surplus - more
    return np.array(given)


def bell_draw(stream_key, dims, deviation, bound, shards=(), kind=jnp.bfloat16):
    entries = jax.random.normal(stream_key, dims, jnp.float32) * deviation
    if len(shards) > 0:
        entries = steps_of(stream_key, dims, shards, -0.22, 0.18) * entries
    return jnp.clip(entries, min=-bound, max=bound).astype(kind)


def setup_inputs(seed: int = 0) -> dict:
    seeds = jax.random.split(jax.random.key(seed), 8)
    velocity = bell_draw(seeds[0], (3, NZ, NX, NY), 1.0, 6.0, ((2, 16), (3, 8)), jnp.float32)
    fiber_points = bell_draw(seeds[1], (FIBERS_B, 3, FBP), 1.0, 6.0, ((0, 128),), jnp.float32)
    stiffness = jnp.clip(jnp.exp(math.log(2.0) - 1.3862944 * jax.random.uniform(seeds[2], (FIBERS_B,), jnp.float32) ** steps_of(seeds[2], (FIBERS_B,), ((0, 128),), -0.2, 0.2)), 0.5, 2.0)
    links = set_ends(jax.random.randint(seeds[3], (FIBERS_B, FBP), 1, FBP), jax.random.fold_in(seeds[3], 1), 1, FBP - 1).astype(jnp.int32)
    delta_weights = bell_draw(seeds[4], (FIBERS_B, INTERSECTION, FBP, PATCH), FBP ** -0.5, 0.5, ((0, 128),))
    owners_keys = jax.random.split(jax.random.fold_in(seeds[5], 1), FIBERS_B * INTERSECTION // (FBD * INTERSECTION))
    owners_turns = jax.random.permutation(jax.random.fold_in(seeds[5], 3), FIBERS_B * INTERSECTION // (FBD * INTERSECTION))
    owners = jax.vmap(lambda own, number: deal_out(jax.random.fold_in(seeds[5], 2), own, number, FBD * INTERSECTION, DEVICES, 1, CAP, 2))(owners_keys, owners_turns).reshape((FIBERS_B, INTERSECTION, 1))
    patch_slots = set_ends(jax.random.randint(seeds[6], (FIBERS_B, INTERSECTION), 0, P_DEV), jax.random.fold_in(seeds[6], 1), 0, P_DEV - 1).astype(jnp.int32)
    return dict(velocity=velocity, fiber_points=fiber_points, stiffness=stiffness, links=links, delta_weights=delta_weights, owners=owners, patch_slots=patch_slots)


viscosity = 0.1
transport_rate = 0.1
force_step = 0.5
fiber_step = 0.25


def advance(extended):
    middle = extended[:, :, 1:-1, 1:-1]
    east_cells = extended[:, :, 2:, 1:-1]
    west_cells = extended[:, :, :-2, 1:-1]
    north_cells = extended[:, :, 1:-1, 2:]
    south_cells = extended[:, :, 1:-1, :-2]
    above_cells = jnp.roll(middle, -1, axis=1)
    below_cells = jnp.roll(middle, 1, axis=1)
    laplace = east_cells + west_cells + north_cells + south_cells + above_cells + below_cells - 6.0 * middle
    transport = middle[0:1] * (east_cells - west_cells) + middle[1:2] * (north_cells - south_cells) + middle[2:3] * (above_cells - below_cells)
    return middle + viscosity * laplace - transport_rate * transport


def reference(velocity, fiber_points, stiffness, links, delta_weights, owners, patch_slots):
    device_count = N_GX * N_GY
    patch_count = CX * CY * NZ // PATCH
    partner = (jnp.arange(FBP, dtype=jnp.int32)[None, :] + links) % FBP
    partner_full = jnp.broadcast_to(partner[:, None, :], fiber_points.shape)
    partner_points = jnp.take_along_axis(fiber_points, partner_full, axis=2)
    fiber_force = stiffness[:, None, None] * (partner_points - fiber_points)
    force_bf = fiber_force.astype(jnp.bfloat16)
    contrib = jnp.einsum("bcp,bkpq->bkcq", force_bf.astype(jnp.float32), delta_weights.astype(jnp.float32), precision=lax.Precision.HIGHEST)
    target = (owners[:, :, 0] * patch_count + patch_slots).reshape(-1).astype(jnp.int32)
    patches = jnp.zeros((device_count * patch_count, 3, PATCH), jnp.float32)
    patches = patches.at[target].add(contrib.reshape(-1, 3, PATCH))
    field = patches.reshape(N_GX, N_GY, patch_count, 3, PATCH).transpose(3, 0, 1, 2, 4)
    field = field.reshape(3, N_GX, N_GY, NZ, CX, CY).transpose(0, 3, 1, 4, 2, 5).reshape(3, NZ, NX, NY)
    moving = velocity + force_step * field
    for step_index in range(STEPS):
        moving = advance(jnp.pad(moving, ((0, 0), (0, 0), (1, 1), (1, 1))))
    fluid_bf = moving.astype(jnp.bfloat16)
    patch_view = fluid_bf.reshape(3, NZ, N_GX, CX, N_GY, CY).transpose(2, 4, 0, 1, 3, 5)
    patch_view = patch_view.reshape(device_count, 3, patch_count, PATCH).transpose(0, 2, 1, 3)
    patch_view = patch_view.reshape(device_count * patch_count, 3, PATCH)
    picked = patch_view[target].reshape(FIBERS_B, INTERSECTION, 3, PATCH)
    interp = jnp.einsum("bkcq,bkpq->bcp", picked.astype(jnp.float32), delta_weights.astype(jnp.float32), precision=lax.Precision.HIGHEST)
    return moving, fiber_points + fiber_step * interp
```

```python
import functools

import jax
import jax.numpy as jnp
from jax import lax
from jax.experimental import pallas as pl
from jax.experimental.pallas import tpu as pltpu
from jax.sharding import PartitionSpec as P

viscosity = 0.1
transport_rate = 0.1
force_step = 0.5
fiber_step = 0.25

F32 = jnp.float32
BF16 = jnp.bfloat16
LANES = 128
BELOW, ABOVE = 2, 10


def dot(a, b):
    return jnp.dot(a, b, preferred_element_type=F32)


def iota(shape, axis):
    return lax.broadcasted_iota(jnp.int32, shape, axis)


def spread_kernel(gy_size, slots, pts, stiff, links, owners, patch_slots, dw, out, dest_out, force, rows):
    b = pl.program_id(0)
    blocks, points = links.shape
    inter = owners.shape[1]
    entries = blocks * inter

    @pl.when(b == 0)
    def _():
        partner = lax.rem(iota((blocks, points), 1) + links[...], points)
        for c in range(3):
            own = pts[c]
            force[c] = jnp.take_along_axis(own, partner, axis=1) - own

    stiffness = stiff[b]
    group = iota((inter, inter * points), 0)
    column = iota((inter, inter * points), 1) // points
    parts = []
    for c in range(3):
        row = (stiffness * force[c, pl.ds(b, 1), :]).astype(BF16).astype(F32)
        wide = jnp.concatenate([jnp.broadcast_to(row, (inter, points))] * inter, axis=1)
        parts.append(jnp.where(group == column, wide, 0.0))
    parts.append(jnp.zeros_like(parts[0]))
    spread = dot(jnp.concatenate(parts, axis=0).astype(BF16), dw[0])
    for c in range(3):
        rows[c, pl.ds(pl.multiple_of(b * inter, inter), inter), :] = spread[c * inter : (c + 1) * inter]

    @pl.when(b == blocks - 1)
    def _():
        pick_block = (iota((entries, blocks), 0) // inter == iota((entries, blocks), 1)).astype(BF16)
        pick_k = lax.rem(iota((entries, inter), 0), inter) == iota((entries, inter), 1)

        def as_column(table):
            spread_rows = dot(pick_block, table.astype(F32).astype(BF16))
            return jnp.sum(jnp.where(pick_k, spread_rows, 0.0), axis=1, keepdims=True)

        owner = as_column(owners[...])
        code = patch_slots[...] + 1
        high, low = as_column(code // 32), as_column(lax.rem(code, 32))
        owner_wide = jnp.broadcast_to(owner, (entries, LANES))
        owner_row = jnp.transpose(
            jnp.concatenate([owner_wide, jnp.zeros((LANES - entries, LANES), F32)], axis=0)
        )[:entries, :entries]
        same = (owner_wide[:, :entries] == owner_row) & (iota((entries, entries), 1) < iota((entries, entries), 0))
        rank = jnp.sum(jnp.where(same, 1.0, 0.0), axis=1, keepdims=True)
        dest = owner * 2.0 + rank
        dest_wide = jnp.broadcast_to(dest, (entries, LANES))
        dest_out[...] = dest_wide
        padded = jnp.concatenate([dest_wide, jnp.full((LANES - entries, LANES), -8.0, F32)], axis=0)
        dest_row = jnp.transpose(padded)[0:1, :entries].astype(jnp.int32)
        position = lax.rem(dest_row // 2, gy_size)
        slot = iota((slots, entries), 0)
        here = (slot == dest_row).astype(F32).astype(BF16)
        to_above = ((slot == dest_row + 2) & (position < gy_size - 1)).astype(F32).astype(BF16)
        to_below = ((slot == dest_row - 2) & (position > 0)).astype(F32).astype(BF16)
        lane = iota((entries, LANES), 1)

        def digits(at):
            return jnp.where(lane == at, high, 0.0) + jnp.where(lane == at + 1, low, 0.0)

        own_head, above_head, below_head = digits(0), digits(BELOW), digits(ABOVE)
        patch = rows.shape[2]
        for c in range(3):
            tail = pltpu.roll(rows[c, :, patch - LANES :], BELOW + 4 + 2 * c, axis=1)
            at = BELOW + 2 + 2 * c
            above_head += jnp.where((lane == at) | (lane == at + 1), tail, 0.0)
            at = ABOVE + 2 + 2 * c
            start = pltpu.roll(rows[c, :, :LANES], at, axis=1)
            below_head += jnp.where((lane == at) | (lane == at + 1), start, 0.0)
            out[:, c * patch : (c + 1) * patch] = dot(here, rows[c].astype(BF16)).astype(BF16)
        head = dot(here, own_head.astype(BF16))
        head += dot(to_above, above_head.astype(BF16))
        head += dot(to_below, below_head.astype(BF16))
        out[:, 3 * patch : 3 * patch + LANES] = head.astype(BF16)
        out[:, 3 * patch + LANES :] = jnp.zeros((slots, patch - LANES), BF16)


def place_kernel(layer_rows, velocity, edge, received, out, low_rows, high_rows, low_f, high_f):
    step = pl.program_id(0)
    rows, patch = velocity.shape[1], velocity.shape[2]
    slots = received.shape[0]
    layers = rows // layer_rows
    head = received[:, 3 * patch : 3 * patch + LANES].astype(F32)
    head_t = jnp.transpose(head)
    lane = iota((slots, LANES), 1)

    def onehot(at):
        slot = (head_t[at : at + 1] * 32.0 + head_t[at + 1 : at + 2] - 1.0).astype(jnp.int32)
        return (iota((rows, slots), 0) + step * rows == slot).astype(F32).astype(BF16)

    here, below, above = onehot(0), onehot(BELOW), onehot(ABOVE)
    for c in range(3):
        placed = dot(here, received[:, c * patch : (c + 1) * patch])
        out[c, :, :patch] = velocity[c] + force_step * placed
        tail = pltpu.roll(head, LANES - 4 - BELOW - 2 * c, axis=1)
        tail = jnp.where(lane >= LANES - 2, tail, 0.0).astype(BF16)
        start = pltpu.roll(head, LANES - (ABOVE + 2 + 2 * c), axis=1)
        start = jnp.where(lane < 2, start, 0.0).astype(BF16)
        out[c, :, patch:] = edge[c] + force_step * (dot(below, tail) + dot(above, start))
        for j in range(2):
            for z in range(layers):
                at = pl.ds(step * layers + z, 1)
                low_f[c, j, at, :] = out[c, z * layer_rows + j : z * layer_rows + j + 1, :]
                top = (z + 1) * layer_rows - 2 + j
                high_f[c, j, at, :] = out[c, top : top + 1, :]

    @pl.when(step == pl.num_programs(0) - 1)
    def _():
        low_rows[...] = low_f[...].astype(BF16)
        high_rows[...] = high_f[...].astype(BF16)


def update(centre, weights, c, east, west, north, south, up, down):
    (px, mx), (py, my), (pz, mz) = weights
    keep = 1.0 - 6.0 * viscosity
    return keep * centre[c] + px * east + mx * west + py * north + my * south + pz * up + mz * down


def mix(centre):
    return [(viscosity - transport_rate * v, viscosity + transport_rate * v) for v in centre]


def sweep_kernel(sides, u0, below_x, above_x, head, fluid, replies, u1, halo, mid):
    layers, rows, wide = u0.shape[1:]
    patch = wide - LANES
    slots = head.shape[0]
    lane = iota((8, LANES), 1)
    mask = jnp.where(lane == 0, sides[3], 0.0) + jnp.where(lane == LANES - 1, sides[2], 0.0)
    sub = iota((8, wide), 0)

    for c in range(3):
        for j in range(2):
            halo[0, c, j] = below_x[c, j].astype(F32)
            halo[1, c, j] = above_x[c, j].astype(F32)
    mask_all = mask[0:1]
    for side in range(2):
        near = 1 - side
        centre = [halo[side, c, near] for c in range(3)]
        weights = mix(centre)
        for c in range(3):
            inner = u0[c, :, 0 if side == 0 else rows - 1, :]
            outer = halo[side, c, 1 - near]
            east, west = (inner, outer) if side == 0 else (outer, inner)
            v = centre[c]
            new = update(
                centre, weights, c, east, west,
                pltpu.roll(v, wide - 1, axis=1), pltpu.roll(v, 1, axis=1),
                pltpu.roll(v, layers - 1, axis=0), pltpu.roll(v, 1, axis=0),
            ) * sides[side]
            mid[side, c, :, :patch] = new[:, :patch]
            mid[side, c, :, patch:] = new[:, patch:] * mask_all

    def sweep(source, low_row, high_row, store, keep):
        @pl.loop(0, layers)
        def _(z):
            z_up = jnp.where(z == layers - 1, 0, z + 1)
            z_down = jnp.where(z == 0, layers - 1, z - 1)
            for x in range(0, rows, 8):
                centre = [source[c, z, x : x + 8, :] for c in range(3)]
                weights = mix([v[:, :keep] for v in centre])
                for c in range(3):
                    v = centre[c]
                    if x + 8 < rows:
                        east = source[c, z, x + 1 : x + 9, :keep]
                    else:
                        east = jnp.where(sub[:, :keep] == 7, high_row(c, z), pltpu.roll(v[:, :keep], 7, axis=0))
                    if x > 0:
                        west = source[c, z, x - 1 : x + 7, :keep]
                    else:
                        west = jnp.where(sub[:, :keep] == 0, low_row(c, z), pltpu.roll(v[:, :keep], 1, axis=0))
                    new = update(
                        [w[:, :keep] for w in centre], weights, c, east, west,
                        pltpu.roll(v, wide - 1, axis=1)[:, :keep], pltpu.roll(v, 1, axis=1)[:, :keep],
                        source[c, z_up, x : x + 8, :keep], source[c, z_down, x : x + 8, :keep],
                    )
                    store(c, z, x, new)

    def store_first(c, z, x, new):
        u1[c, z, x : x + 8, :patch] = new[:, :patch]
        u1[c, z, x : x + 8, patch:] = new[:, patch:] * mask

    def store_last(c, z, x, new):
        fluid[c, pl.ds(pl.multiple_of(z * rows + x, 8), 8), :] = new

    sweep(
        u0,
        lambda c, z: halo[0, c, 1, pl.ds(z, 1), :],
        lambda c, z: halo[1, c, 0, pl.ds(z, 1), :],
        store_first,
        wide,
    )
    sweep(
        u1,
        lambda c, z: mid[0, c, pl.ds(z, 1), :patch],
        lambda c, z: mid[1, c, pl.ds(z, 1), :patch],
        store_last,
        patch,
    )

    heads = head[...].astype(F32)
    slot = (heads[:, 0:1] * 32.0 + heads[:, 1:2] - 1.0).astype(jnp.int32)
    chunk = 256
    for c in range(3):
        total = jnp.zeros((slots, patch), F32)
        for first in range(0, layers * rows, chunk):
            pick = (iota((slots, chunk), 1) + first == slot).astype(F32).astype(BF16)
            total += dot(pick, fluid[c, first : first + chunk, :].astype(BF16))
        replies[:, c * patch : (c + 1) * patch] = total.astype(BF16)


def gather_kernel(pts, dest, returned, dw, out, picked, moved):
    b = pl.program_id(0)
    entries, slots = dest.shape[0], returned.shape[0]
    inter = entries // pl.num_programs(0)
    patch, points = dw.shape[2], pts.shape[2]

    @pl.when(b == 0)
    def _():
        to = dest[:, 0:1].astype(jnp.int32)
        pick = (iota((entries, slots), 1) == to).astype(F32).astype(BF16)
        for c in range(3):
            picked[c] = dot(pick, returned[:, c * patch : (c + 1) * patch])

    at = pl.ds(pl.multiple_of(b * inter, inter), inter)
    parts = [picked[c, at, :] for c in range(3)]
    parts.append(jnp.zeros_like(parts[0]))
    every = lax.dot_general(
        jnp.concatenate(parts, axis=0).astype(BF16), dw[0], (((1,), (1,)), ((), ())), preferred_element_type=F32
    )
    group = iota((inter, inter * points), 0)
    column = iota((inter, inter * points), 1) // points
    for c in range(3):
        own = jnp.where(group == column, every[c * inter : (c + 1) * inter], 0.0)
        folded = own[:, :points]
        for k in range(1, inter):
            folded = folded + own[:, k * points : (k + 1) * points]
        moved[c, pl.ds(b, 1), :] = jnp.sum(folded, axis=0, keepdims=True)

    @pl.when(b == pl.num_programs(0) - 1)
    def _():
        for c in range(3):
            out[c] = pts[c] + fiber_step * moved[c]


def whole(shape):
    return pl.BlockSpec(shape, lambda *_: (0,) * len(shape))


def shards(velocity, fiber_points, stiffness, links, delta_weights, owners, patch_slots):
    blocks, inter, points, patch = delta_weights.shape
    layers, rows, columns = velocity.shape[1:]
    gx_size, gy_size = lax.axis_size("gx"), lax.axis_size("gy")
    devices = gx_size * gy_size
    entries, slots, cells = blocks * inter, devices * 2, layers * rows
    wide = patch + LANES
    mb = 1 << 20
    pts = fiber_points.transpose(1, 0, 2)
    dw = delta_weights.reshape(blocks, inter * points, patch)
    smem = pl.BlockSpec(memory_space=pltpu.SMEM)

    outgoing, dest = pl.pallas_call(
        functools.partial(spread_kernel, gy_size, slots),
        grid=(blocks,),
        in_specs=[
            whole((3, blocks, points)),
            smem,
            whole((blocks, points)),
            whole((blocks, inter)),
            whole((blocks, inter)),
            pl.BlockSpec((1, inter * points, patch), lambda b: (b, 0, 0)),
        ],
        out_specs=[whole((slots, 4 * patch)), whole((entries, LANES))],
        out_shape=[
            jax.ShapeDtypeStruct((slots, 4 * patch), BF16),
            jax.ShapeDtypeStruct((entries, LANES), F32),
        ],
        scratch_shapes=[pltpu.VMEM((3, blocks, points), F32), pltpu.VMEM((3, entries, patch), F32)],
        compiler_params=pltpu.CompilerParams(vmem_limit_bytes=16 * mb),
        cost_estimate=pl.CostEstimate(flops=10**9, bytes_accessed=9 * mb, transcendentals=0),
        name="spread",
    )(pts, stiffness, links, owners.reshape(blocks, inter), patch_slots, dw)

    def exchange(rows_out):
        width = rows_out.shape[1]
        return lax.all_to_all(
            rows_out.reshape(devices, 2, width), ("gx", "gy"), split_axis=0, concat_axis=0, tiled=True
        ).reshape(slots, width)

    received = exchange(outgoing)

    ahead = [(i + 1, i) for i in range(gy_size - 1)]
    behind = [(i, i + 1) for i in range(gy_size - 1)]
    flat = velocity.reshape(3, cells, columns)
    first = lax.ppermute(flat[:, :, :2].transpose(0, 2, 1), "gy", ahead)
    last = lax.ppermute(flat[:, :, columns - 2 :].transpose(0, 2, 1), "gy", behind)
    edge = jnp.concatenate(
        [first.transpose(0, 2, 1), jnp.zeros((3, cells, LANES - 4), F32), last.transpose(0, 2, 1)], axis=2
    )

    steps = 4
    part = cells // steps
    u0, low_rows, high_rows = pl.pallas_call(
        functools.partial(place_kernel, rows),
        grid=(steps,),
        in_specs=[
            pl.BlockSpec((3, part, patch), lambda s: (0, s, 0)),
            pl.BlockSpec((3, part, LANES), lambda s: (0, s, 0)),
            whole((slots, 4 * patch)),
        ],
        out_specs=[
            pl.BlockSpec((3, part, wide), lambda s: (0, s, 0)),
            whole((3, 2, layers, wide)),
            whole((3, 2, layers, wide)),
        ],
        out_shape=[
            jax.ShapeDtypeStruct((3, cells, wide), F32),
            jax.ShapeDtypeStruct((3, 2, layers, wide), BF16),
            jax.ShapeDtypeStruct((3, 2, layers, wide), BF16),
        ],
        scratch_shapes=[pltpu.VMEM((3, 2, layers, wide), F32)] * 2,
        compiler_params=pltpu.CompilerParams(vmem_limit_bytes=24 * mb),
        cost_estimate=pl.CostEstimate(flops=10**9, bytes_accessed=17 * mb, transcendentals=0),
        name="place",
    )(flat, edge, received)

    up = [(i, i + 1) for i in range(gx_size - 1)]
    below_x = lax.ppermute(high_rows, "gx", up)
    above_x = lax.ppermute(low_rows, "gx", [(b, a) for a, b in up])

    gx, gy = lax.axis_index("gx"), lax.axis_index("gy")
    sides = jnp.stack([gx > 0, gx < gx_size - 1, gy > 0, gy < gy_size - 1]).astype(F32)
    vmem = pl.BlockSpec(memory_space=pltpu.VMEM)
    fluid, replies = pl.pallas_call(
        sweep_kernel,
        in_specs=[smem, vmem, vmem, vmem, vmem],
        out_specs=[vmem, vmem],
        out_shape=[
            jax.ShapeDtypeStruct((3, cells, patch), F32),
            jax.ShapeDtypeStruct((slots, 3 * patch), BF16),
        ],
        scratch_shapes=[
            pltpu.VMEM((3, layers, rows, wide), F32),
            pltpu.VMEM((2, 3, 2, layers, wide), F32),
            pltpu.VMEM((2, 3, layers, wide), F32),
        ],
        compiler_params=pltpu.CompilerParams(vmem_limit_bytes=48 * mb),
        cost_estimate=pl.CostEstimate(flops=2 * 10**9, bytes_accessed=16 * mb, transcendentals=0),
        name="sweeps",
    )(sides, u0.reshape(3, layers, rows, wide), below_x, above_x, received[:, 3 * patch : 3 * patch + LANES])

    returned = exchange(replies)
    moved = pl.pallas_call(
        gather_kernel,
        grid=(blocks,),
        in_specs=[
            whole((3, blocks, points)),
            whole((entries, LANES)),
            whole((slots, 3 * patch)),
            pl.BlockSpec((1, inter * points, patch), lambda b: (b, 0, 0)),
        ],
        out_specs=whole((3, blocks, points)),
        out_shape=jax.ShapeDtypeStruct((3, blocks, points), F32),
        scratch_shapes=[pltpu.VMEM((3, entries, patch), F32), pltpu.VMEM((3, blocks, points), F32)],
        compiler_params=pltpu.CompilerParams(vmem_limit_bytes=16 * mb),
        cost_estimate=pl.CostEstimate(flops=10**9, bytes_accessed=9 * mb, transcendentals=0),
        name="interp",
    )(pts, dest, returned, dw)
    return fluid.reshape(3, layers, rows, columns), moved.transpose(1, 0, 2)


def solution(mesh):
    placed = (
        P(None, None, "gx", "gy"),
        P(("gx", "gy"), None, None),
        P(("gx", "gy")),
        P(("gx", "gy"), None),
        P(("gx", "gy"), None, None, None),
        P(("gx", "gy"), None, None),
        P(("gx", "gy"), None),
    )
    return jax.shard_map(
        shards,
        mesh=mesh,
        in_specs=placed,
        out_specs=(P(None, None, "gx", "gy"), P(("gx", "gy"), None, None)),
        check_vma=False,
    )
```

```python
import functools

import jax
import jax.numpy as jnp
from jax import lax
from jax.experimental import pallas as pl
from jax.experimental.pallas import tpu as pltpu
from jax.sharding import PartitionSpec as P

viscosity = 0.1
transport_rate = 0.1
force_step = 0.5
fiber_step = 0.25

F32 = jnp.float32
BF16 = jnp.bfloat16
LANES = 128
BELOW, ABOVE = 2, 10


def dot(a, b):
    return jnp.dot(a, b, preferred_element_type=F32)


def iota(shape, axis):
    return lax.broadcasted_iota(jnp.int32, shape, axis)


def spread_kernel(
    gy_size, slots, pts_hbm, stiff, links_hbm, owners_hbm, patch_slots_hbm, dw_hbm, out, dest_out, dw,
    force, rows, pts, links, owners, patch_slots, sems,
):
    blocks, points = links.shape
    inter = owners.shape[1]
    entries = blocks * inter
    loads = [
        pltpu.make_async_copy(dw_hbm.at[b], dw.at[b], sems.at[b]) for b in range(blocks)
    ]
    small = [(pts_hbm, pts), (links_hbm, links), (owners_hbm, owners), (patch_slots_hbm, patch_slots)]
    small = [pltpu.make_async_copy(a, b, sems.at[blocks + i]) for i, (a, b) in enumerate(small)]
    for copy in small + loads:
        copy.start()
    for copy in small:
        copy.wait()
    partner = lax.rem(iota((blocks, points), 1) + links[...], points)
    for c in range(3):
        own = pts[c]
        force[c] = jnp.take_along_axis(own, partner, axis=1) - own
    group = iota((inter, inter * points), 0)
    column = iota((inter, inter * points), 1) // points

    @pl.loop(0, blocks)
    def _(b):
        stiffness = stiff[b]
        parts = []
        for c in range(3):
            row = (stiffness * force[c, pl.ds(b, 1), :]).astype(BF16).astype(F32)
            wide = jnp.concatenate([jnp.broadcast_to(row, (inter, points))] * inter, axis=1)
            parts.append(jnp.where(group == column, wide, 0.0))
        parts.append(jnp.zeros_like(parts[0]))
        pltpu.make_async_copy(dw_hbm.at[b], dw.at[b], sems.at[b]).wait()
        spread = dot(jnp.concatenate(parts, axis=0).astype(BF16), dw[b])
        for c in range(3):
            rows[c, pl.ds(pl.multiple_of(b * inter, inter), inter), :] = spread[c * inter : (c + 1) * inter]

    pick_block = (iota((entries, blocks), 0) // inter == iota((entries, blocks), 1)).astype(BF16)
    pick_k = lax.rem(iota((entries, inter), 0), inter) == iota((entries, inter), 1)

    def as_column(table):
        spread_rows = dot(pick_block, table.astype(F32).astype(BF16))
        return jnp.sum(jnp.where(pick_k, spread_rows, 0.0), axis=1, keepdims=True)

    owner = as_column(owners[...])
    code = patch_slots[...] + 1
    high, low = as_column(code // 32), as_column(lax.rem(code, 32))
    owner_wide = jnp.broadcast_to(owner, (entries, LANES))
    owner_row = jnp.transpose(
        jnp.concatenate([owner_wide, jnp.zeros((LANES - entries, LANES), F32)], axis=0)
    )[:entries, :entries]
    same = (owner_wide[:, :entries] == owner_row) & (iota((entries, entries), 1) < iota((entries, entries), 0))
    rank = jnp.sum(jnp.where(same, 1.0, 0.0), axis=1, keepdims=True)
    dest = owner * 2.0 + rank
    dest_wide = jnp.broadcast_to(dest, (entries, LANES))
    dest_out[...] = dest_wide
    padded = jnp.concatenate([dest_wide, jnp.full((LANES - entries, LANES), -8.0, F32)], axis=0)
    dest_row = jnp.transpose(padded)[0:1, :entries].astype(jnp.int32)
    position = lax.rem(dest_row // 2, gy_size)
    slot = iota((slots, entries), 0)
    here = (slot == dest_row).astype(F32).astype(BF16)
    to_above = ((slot == dest_row + 2) & (position < gy_size - 1)).astype(F32).astype(BF16)
    to_below = ((slot == dest_row - 2) & (position > 0)).astype(F32).astype(BF16)
    lane = iota((entries, LANES), 1)

    def digits(at):
        return jnp.where(lane == at, high, 0.0) + jnp.where(lane == at + 1, low, 0.0)

    own_head, above_head, below_head = digits(0), digits(BELOW), digits(ABOVE)
    patch = rows.shape[2]
    for c in range(3):
        tail = pltpu.roll(rows[c, :, patch - LANES :], BELOW + 4 + 2 * c, axis=1)
        at = BELOW + 2 + 2 * c
        above_head += jnp.where((lane == at) | (lane == at + 1), tail, 0.0)
        at = ABOVE + 2 + 2 * c
        start = pltpu.roll(rows[c, :, :LANES], at, axis=1)
        below_head += jnp.where((lane == at) | (lane == at + 1), start, 0.0)
        out[:, c * patch : (c + 1) * patch] = dot(here, rows[c].astype(BF16)).astype(BF16)
    head = dot(here, own_head.astype(BF16))
    head += dot(to_above, above_head.astype(BF16))
    head += dot(to_below, below_head.astype(BF16))
    out[:, 3 * patch :] = head.astype(BF16)


def stage_kernel(velocity, edge, out, sems):
    patch = velocity.shape[2]
    main = pltpu.make_async_copy(velocity, out.at[:, :, :patch], sems.at[0])
    side = pltpu.make_async_copy(edge, out.at[:, :, patch:], sems.at[1])
    main.start()
    side.start()
    main.wait()
    side.wait()


def place_kernel(layer_rows, staged, received, out, low_rows, high_rows, low_f, high_f):
    cells, wide = staged.shape[1:]
    patch = wide - LANES
    slots = received.shape[0]
    part = 256
    layers = part // layer_rows
    head = received[:, 3 * patch :].astype(F32)
    head_t = jnp.transpose(head)
    lane = iota((slots, LANES), 1)
    tails, starts = [], []
    for c in range(3):
        tail = pltpu.roll(head, LANES - 4 - BELOW - 2 * c, axis=1)
        tails.append(jnp.where(lane >= LANES - 2, tail, 0.0).astype(BF16))
        start = pltpu.roll(head, LANES - (ABOVE + 2 + 2 * c), axis=1)
        starts.append(jnp.where(lane < 2, start, 0.0).astype(BF16))

    def slot_at(at):
        return (head_t[at : at + 1] * 32.0 + head_t[at + 1 : at + 2] - 1.0).astype(jnp.int32)

    slot_here, slot_below, slot_above = slot_at(0), slot_at(BELOW), slot_at(ABOVE)

    @pl.loop(0, cells // part)
    def _(step):
        row = iota((part, slots), 0) + step * part
        here = (row == slot_here).astype(F32).astype(BF16)
        below = (row == slot_below).astype(F32).astype(BF16)
        above = (row == slot_above).astype(F32).astype(BF16)
        at = pl.ds(pl.multiple_of(step * part, part), part)
        for c in range(3):
            main = staged[c, at, :patch] + force_step * dot(here, received[:, c * patch : (c + 1) * patch])
            edge = staged[c, at, patch:] + force_step * (dot(below, tails[c]) + dot(above, starts[c]))
            out[c, at, :patch] = main
            out[c, at, patch:] = edge
            to = pl.ds(pl.multiple_of(step * layers, layers), layers)
            for j in range(2):
                for side, offset in ((low_f, j), (high_f, layer_rows - 2 + j)):
                    picks = range(offset, part, layer_rows)
                    side[c, j, to, :patch] = jnp.concatenate([main[i : i + 1] for i in picks], axis=0)
                    side[c, j, to, patch:] = jnp.concatenate([edge[i : i + 1] for i in picks], axis=0)

    low_rows[...] = low_f[...].astype(BF16)
    high_rows[...] = high_f[...].astype(BF16)


def update(centre, weights, c, east, west, north, south, up, down):
    (px, mx), (py, my), (pz, mz) = weights
    keep = 1.0 - 6.0 * viscosity
    return keep * centre[c] + px * east + mx * west + py * north + my * south + pz * up + mz * down


def mix(centre):
    return [(viscosity - transport_rate * v, viscosity + transport_rate * v) for v in centre]


def edge_mask(sides):
    lane = iota((8, LANES), 1)
    return jnp.where(lane == 0, sides[3], 0.0) + jnp.where(lane == LANES - 1, sides[2], 0.0)


def sweep(source, low_row, high_row, store, keep):
    layers, rows, wide = source.shape[1:]
    sub = iota((8, keep), 0)

    @pl.loop(0, layers)
    def _(z):
        z_up = jnp.where(z == layers - 1, 0, z + 1)
        z_down = jnp.where(z == 0, layers - 1, z - 1)
        for x in range(0, rows, 8):
            centre = [source[c, z, x : x + 8, :] for c in range(3)]
            weights = mix([v[:, :keep] for v in centre])
            for c in range(3):
                v = centre[c]
                if x + 8 < rows:
                    east = source[c, z, x + 1 : x + 9, :keep]
                else:
                    east = jnp.where(sub == 7, high_row(c, z), pltpu.roll(v[:, :keep], 7, axis=0))
                if x > 0:
                    west = source[c, z, x - 1 : x + 7, :keep]
                else:
                    west = jnp.where(sub == 0, low_row(c, z), pltpu.roll(v[:, :keep], 1, axis=0))
                new = update(
                    [w[:, :keep] for w in centre], weights, c, east, west,
                    pltpu.roll(v, wide - 1, axis=1)[:, :keep], pltpu.roll(v, 1, axis=1)[:, :keep],
                    source[c, z_up, x : x + 8, :keep], source[c, z_down, x : x + 8, :keep],
                )
                store(c, z, x, new)


def first_kernel(sides, u0, u1):
    patch = u0.shape[3] - LANES
    mask = edge_mask(sides)

    def store(c, z, x, new):
        u1[c, z, x : x + 8, :patch] = new[:, :patch]
        u1[c, z, x : x + 8, patch:] = new[:, patch:] * mask

    sweep(u0, lambda c, z: 0.0, lambda c, z: 0.0, store, u0.shape[3])


def last_kernel(sides, u1_in, low_f, high_f, below_x, above_x, received, fluid_hbm, replies, u1, mid, fluid, sems):
    layers, rows, wide = u1.shape[1:]
    patch = wide - LANES
    slots = received.shape[0]
    mask = edge_mask(sides)[0:1]

    for side in range(2):
        halo, inner, row = (below_x, low_f, 0) if side == 0 else (above_x, high_f, rows - 1)
        near = 1 - side
        centre = [halo[c, near].astype(F32) for c in range(3)]
        weights = mix(centre)
        slope = transport_rate if side == 0 else -transport_rate
        own = viscosity + slope * inner[0, side]
        for c in range(3):
            outer = halo[c, side].astype(F32)
            inside = inner[c, side]
            east, west = (inside, outer) if side == 0 else (outer, inside)
            v = centre[c]
            new = update(
                centre, weights, c, east, west,
                pltpu.roll(v, wide - 1, axis=1), pltpu.roll(v, 1, axis=1),
                pltpu.roll(v, layers - 1, axis=0), pltpu.roll(v, 1, axis=0),
            ) * sides[side]
            mid[side, c, :, :patch] = new[:, :patch]
            mid[side, c, :, patch:] = new[:, patch:] * mask
            term = own * v
            tail = term[:, patch:] * mask
            for z in range(layers):
                u1[c, z, row : row + 1, :patch] += term[z : z + 1, :patch]
                u1[c, z, row : row + 1, patch:] += tail[z : z + 1]

    def store(c, z, x, new):
        fluid[c, pl.ds(pl.multiple_of(z * rows + x, 8), 8), :] = new

    sweep(
        u1,
        lambda c, z: mid[0, c, pl.ds(z, 1), :patch],
        lambda c, z: mid[1, c, pl.ds(z, 1), :patch],
        store,
        patch,
    )
    write = pltpu.make_async_copy(fluid, fluid_hbm, sems.at[0])
    write.start()

    heads = received[:, 3 * patch :].astype(F32)
    slot = (heads[:, 0:1] * 32.0 + heads[:, 1:2] - 1.0).astype(jnp.int32)
    chunk = 256
    for c in range(3):
        total = jnp.zeros((slots, patch), F32)
        for first in range(0, layers * rows, chunk):
            pick = (iota((slots, chunk), 1) + first == slot).astype(F32).astype(BF16)
            total += dot(pick, fluid[c, first : first + chunk, :].astype(BF16))
        replies[:, c * patch : (c + 1) * patch] = total.astype(BF16)
    write.wait()


def gather_kernel(pts, dest, returned, dw, out, picked, moved):
    entries, slots = dest.shape[0], returned.shape[0]
    blocks, patch, points = dw.shape[0], dw.shape[2], pts.shape[2]
    inter = entries // blocks
    to = dest[:, 0:1].astype(jnp.int32)
    pick = (iota((entries, slots), 1) == to).astype(F32).astype(BF16)
    for c in range(3):
        picked[c] = dot(pick, returned[:, c * patch : (c + 1) * patch])
    group = iota((inter, inter * points), 0)
    column = iota((inter, inter * points), 1) // points

    @pl.loop(0, blocks)
    def _(b):
        at = pl.ds(pl.multiple_of(b * inter, inter), inter)
        parts = [picked[c, at, :] for c in range(3)]
        parts.append(jnp.zeros_like(parts[0]))
        every = lax.dot_general(
            jnp.concatenate(parts, axis=0).astype(BF16), dw[b], (((1,), (1,)), ((), ())), preferred_element_type=F32
        )
        for c in range(3):
            own = jnp.where(group == column, every[c * inter : (c + 1) * inter], 0.0)
            folded = own[:, :points]
            for k in range(1, inter):
                folded = folded + own[:, k * points : (k + 1) * points]
            moved[c, pl.ds(b, 1), :] = jnp.sum(folded, axis=0, keepdims=True)

    for c in range(3):
        out[c] = pts[c] + fiber_step * moved[c]


def shards(velocity, fiber_points, stiffness, links, delta_weights, owners, patch_slots):
    blocks, inter, points, patch = delta_weights.shape
    layers, rows, columns = velocity.shape[1:]
    gx_size, gy_size = lax.axis_size("gx"), lax.axis_size("gy")
    devices = gx_size * gy_size
    entries, slots, cells = blocks * inter, devices * 2, layers * rows
    wide, width = patch + LANES, 3 * patch + LANES
    mb = 1 << 20
    pts = fiber_points.transpose(1, 0, 2)
    dw = delta_weights.reshape(blocks, inter * points, patch)
    smem = pl.BlockSpec(memory_space=pltpu.SMEM)
    vmem = pl.BlockSpec(memory_space=pltpu.VMEM)
    hbm = pl.BlockSpec(memory_space=pltpu.HBM)
    anywhere = pl.BlockSpec(memory_space=pl.ANY)

    def params(limit):
        return pltpu.CompilerParams(vmem_limit_bytes=limit * mb)

    def cost(flops, size):
        return pl.CostEstimate(flops=flops, bytes_accessed=size * mb, transcendentals=0)

    outgoing, dest, dw_near = pl.pallas_call(
        functools.partial(spread_kernel, gy_size, slots),
        in_specs=[hbm, smem, hbm, hbm, hbm, hbm],
        out_specs=[vmem, vmem, vmem],
        out_shape=[
            jax.ShapeDtypeStruct((slots, width), BF16),
            jax.ShapeDtypeStruct((entries, LANES), F32),
            jax.ShapeDtypeStruct(dw.shape, BF16),
        ],
        scratch_shapes=[
            pltpu.VMEM((3, blocks, points), F32),
            pltpu.VMEM((3, entries, patch), F32),
            pltpu.VMEM((3, blocks, points), F32),
            pltpu.VMEM((blocks, points), jnp.int32),
            pltpu.VMEM((blocks, inter), jnp.int32),
            pltpu.VMEM((blocks, inter), jnp.int32),
            pltpu.SemaphoreType.DMA((blocks + 4,)),
        ],
        compiler_params=params(16),
        cost_estimate=cost(10**9, 9),
        name="spread",
    )(pts, stiffness, links, owners.reshape(blocks, inter), patch_slots, dw)

    def exchange(rows_out):
        size = rows_out.shape[1]
        return lax.all_to_all(
            rows_out.reshape(devices, 2, size), ("gx", "gy"), split_axis=0, concat_axis=0, tiled=True
        ).reshape(slots, size)

    received = exchange(outgoing)

    ahead = [(i + 1, i) for i in range(gy_size - 1)]
    behind = [(i, i + 1) for i in range(gy_size - 1)]
    flat = velocity.reshape(3, cells, columns)
    first = lax.ppermute(flat[:, :, :2].transpose(0, 2, 1), "gy", ahead)
    last = lax.ppermute(flat[:, :, columns - 2 :].transpose(0, 2, 1), "gy", behind)
    edge = jnp.concatenate(
        [first.transpose(0, 2, 1), jnp.zeros((3, cells, LANES - 4), F32), last.transpose(0, 2, 1)], axis=2
    )
    staged = pl.pallas_call(
        stage_kernel,
        in_specs=[hbm, anywhere],
        out_specs=vmem,
        out_shape=jax.ShapeDtypeStruct((3, cells, wide), F32),
        scratch_shapes=[pltpu.SemaphoreType.DMA((2,))],
        compiler_params=params(16),
        cost_estimate=cost(0, 8),
        name="stage",
    )(flat, edge)

    side = (3, 2, layers, wide)
    u0, low_rows, high_rows, low_f, high_f = pl.pallas_call(
        functools.partial(place_kernel, rows),
        in_specs=[vmem, vmem],
        out_specs=[vmem] * 5,
        out_shape=[
            jax.ShapeDtypeStruct((3, cells, wide), F32),
            jax.ShapeDtypeStruct(side, BF16),
            jax.ShapeDtypeStruct(side, BF16),
            jax.ShapeDtypeStruct(side, F32),
            jax.ShapeDtypeStruct(side, F32),
        ],
        input_output_aliases={0: 0},
        compiler_params=params(24),
        cost_estimate=cost(10**9, 10),
        name="place",
    )(staged, received)

    up = [(i, i + 1) for i in range(gx_size - 1)]
    below_x = lax.ppermute(high_rows, "gx", up)
    above_x = lax.ppermute(low_rows, "gx", [(b, a) for a, b in up])

    gx, gy = lax.axis_index("gx"), lax.axis_index("gy")
    sides = jnp.stack([gx > 0, gx < gx_size - 1, gy > 0, gy < gy_size - 1]).astype(F32)
    u1 = pl.pallas_call(
        first_kernel,
        in_specs=[smem, vmem],
        out_specs=vmem,
        out_shape=jax.ShapeDtypeStruct((3, layers, rows, wide), F32),
        compiler_params=params(24),
        cost_estimate=cost(2 * 10**9, 16),
        name="sweep_first",
    )(sides, u0.reshape(3, layers, rows, wide))
    fluid, replies, _ = pl.pallas_call(
        last_kernel,
        in_specs=[smem] + [vmem] * 6,
        out_specs=[hbm, vmem, vmem],
        out_shape=[
            jax.ShapeDtypeStruct((3, cells, patch), F32),
            jax.ShapeDtypeStruct((slots, 3 * patch), BF16),
            jax.ShapeDtypeStruct((3, layers, rows, wide), F32),
        ],
        scratch_shapes=[
            pltpu.VMEM((2, 3, layers, wide), F32),
            pltpu.VMEM((3, cells, patch), F32),
            pltpu.SemaphoreType.DMA((1,)),
        ],
        input_output_aliases={1: 2},
        compiler_params=params(24),
        cost_estimate=cost(2 * 10**9, 16),
        name="sweep_last",
    )(sides, u1, low_f, high_f, below_x, above_x, received)

    returned = exchange(replies)
    moved = pl.pallas_call(
        gather_kernel,
        in_specs=[vmem] * 4,
        out_specs=vmem,
        out_shape=jax.ShapeDtypeStruct((3, blocks, points), F32),
        scratch_shapes=[pltpu.VMEM((3, entries, patch), F32), pltpu.VMEM((3, blocks, points), F32)],
        compiler_params=params(16),
        cost_estimate=cost(10**9, 9),
        name="interp",
    )(pts, dest, returned, dw_near)
    return fluid.reshape(3, layers, rows, columns), moved.transpose(1, 0, 2)


def solution(mesh):
    placed = (
        P(None, None, "gx", "gy"),
        P(("gx", "gy"), None, None),
        P(("gx", "gy")),
        P(("gx", "gy"), None),
        P(("gx", "gy"), None, None, None),
        P(("gx", "gy"), None, None),
        P(("gx", "gy"), None),
    )
    return jax.shard_map(
        shards,
        mesh=mesh,
        in_specs=placed,
        out_specs=(P(None, None, "gx", "gy"), P(("gx", "gy"), None, None)),
        check_vma=False,
    )
```

```python
import functools

import jax
import jax.numpy as jnp
from jax import lax
from jax.experimental import pallas as pl
from jax.experimental.pallas import tpu as pltpu
from jax.sharding import PartitionSpec as P

viscosity = 0.1
transport_rate = 0.1
force_step = 0.5
fiber_step = 0.25

F32 = jnp.float32
BF16 = jnp.bfloat16
LANES = 128
BELOW, ABOVE = 2, 10


def dot(a, b):
    return jnp.dot(a, b, preferred_element_type=F32)


def iota(shape, axis):
    return lax.broadcasted_iota(jnp.int32, shape, axis)


def spread_kernel(
    gy_size, slots, pts_hbm, stiff, links_hbm, owners_hbm, patch_slots_hbm, dw_hbm, out, dest_out,
    dw, force, rows, pts, links, owners, patch_slots, sems,
):
    blocks, points = links.shape
    inter = owners.shape[1]
    entries = blocks * inter
    loads = [
        pltpu.make_async_copy(dw_hbm.at[b], dw.at[b], sems.at[b]) for b in range(blocks)
    ]
    small = [(pts_hbm, pts), (links_hbm, links), (owners_hbm, owners), (patch_slots_hbm, patch_slots)]
    small = [pltpu.make_async_copy(a, b, sems.at[blocks + i]) for i, (a, b) in enumerate(small)]
    for copy in small + loads:
        copy.start()
    for copy in small:
        copy.wait()
    partner = lax.rem(iota((blocks, points), 1) + links[...], points)
    for c in range(3):
        own = pts[c]
        force[c] = jnp.take_along_axis(own, partner, axis=1) - own
    group = iota((inter, inter * points), 0)
    column = iota((inter, inter * points), 1) // points

    @pl.loop(0, blocks)
    def _(b):
        stiffness = stiff[b]
        parts = []
        for c in range(3):
            row = (stiffness * force[c, pl.ds(b, 1), :]).astype(BF16).astype(F32)
            wide = jnp.concatenate([jnp.broadcast_to(row, (inter, points))] * inter, axis=1)
            parts.append(jnp.where(group == column, wide, 0.0))
        parts.append(jnp.zeros_like(parts[0]))
        pltpu.make_async_copy(dw_hbm.at[b], dw.at[b], sems.at[b]).wait()
        spread = dot(jnp.concatenate(parts, axis=0).astype(BF16), dw[b])
        for c in range(3):
            rows[c, pl.ds(pl.multiple_of(b * inter, inter), inter), :] = spread[c * inter : (c + 1) * inter]

    pick_block = (iota((entries, blocks), 0) // inter == iota((entries, blocks), 1)).astype(BF16)
    pick_k = lax.rem(iota((entries, inter), 0), inter) == iota((entries, inter), 1)

    def as_column(table):
        spread_rows = dot(pick_block, table.astype(F32).astype(BF16))
        return jnp.sum(jnp.where(pick_k, spread_rows, 0.0), axis=1, keepdims=True)

    owner = as_column(owners[...])
    code = patch_slots[...] + 1
    high, low = as_column(code // 32), as_column(lax.rem(code, 32))
    owner_wide = jnp.broadcast_to(owner, (entries, LANES))
    owner_row = jnp.transpose(
        jnp.concatenate([owner_wide, jnp.zeros((LANES - entries, LANES), F32)], axis=0)
    )[:entries, :entries]
    same = (owner_wide[:, :entries] == owner_row) & (iota((entries, entries), 1) < iota((entries, entries), 0))
    rank = jnp.sum(jnp.where(same, 1.0, 0.0), axis=1, keepdims=True)
    dest = owner * 2.0 + rank
    dest_wide = jnp.broadcast_to(dest, (entries, LANES))
    dest_out[...] = dest_wide
    padded = jnp.concatenate([dest_wide, jnp.full((LANES - entries, LANES), -8.0, F32)], axis=0)
    dest_row = jnp.transpose(padded)[0:1, :entries].astype(jnp.int32)
    position = lax.rem(dest_row // 2, gy_size)
    slot = iota((slots, entries), 0)
    here = (slot == dest_row).astype(F32).astype(BF16)
    to_above = ((slot == dest_row + 2) & (position < gy_size - 1)).astype(F32).astype(BF16)
    to_below = ((slot == dest_row - 2) & (position > 0)).astype(F32).astype(BF16)
    lane = iota((entries, LANES), 1)

    def digits(at):
        return jnp.where(lane == at, high, 0.0) + jnp.where(lane == at + 1, low, 0.0)

    own_head, above_head, below_head = digits(0), digits(BELOW), digits(ABOVE)
    patch = rows.shape[2]
    for c in range(3):
        tail = pltpu.roll(rows[c, :, patch - LANES :], BELOW + 4 + 2 * c, axis=1)
        at = BELOW + 2 + 2 * c
        above_head += jnp.where((lane == at) | (lane == at + 1), tail, 0.0)
        at = ABOVE + 2 + 2 * c
        start = pltpu.roll(rows[c, :, :LANES], at, axis=1)
        below_head += jnp.where((lane == at) | (lane == at + 1), start, 0.0)
        out[:, c * patch : (c + 1) * patch] = dot(here, rows[c].astype(BF16)).astype(BF16)
    head = dot(here, own_head.astype(BF16))
    head += dot(to_above, above_head.astype(BF16))
    head += dot(to_below, below_head.astype(BF16))
    out[:, 3 * patch :] = head.astype(BF16)


class Arrived:
    def __init__(self, received, patch):
        self.received, self.patch = received, patch
        slots = received.shape[0]
        head = received[:, 3 * patch :].astype(F32)
        head_t = jnp.transpose(head)
        lane = iota((slots, LANES), 1)
        self.tails, self.starts = [], []
        for c in range(3):
            tail = pltpu.roll(head, LANES - 4 - BELOW - 2 * c, axis=1)
            self.tails.append(jnp.where(lane >= LANES - 2, tail, 0.0).astype(BF16))
            start = pltpu.roll(head, LANES - (ABOVE + 2 + 2 * c), axis=1)
            self.starts.append(jnp.where(lane < 2, start, 0.0).astype(BF16))
        self.slots = [
            (head_t[at : at + 1] * 32.0 + head_t[at + 1 : at + 2] - 1.0).astype(jnp.int32) for at in (0, BELOW, ABOVE)
        ]

    def choose(self, row):
        return [(row == slot).astype(F32).astype(BF16) for slot in self.slots]

    def force(self, chosen, c):
        here, below, above = chosen
        main = dot(here, self.received[:, c * self.patch : (c + 1) * self.patch])
        return force_step * main, force_step * (dot(below, self.tails[c]) + dot(above, self.starts[c]))


def rim_kernel(layer_rows, velocity, edges, received, low_rows, high_rows, rim):
    layers, patch = low_rows.shape[2], velocity.shape[2]
    slots = received.shape[0]
    arrived = Arrived(received, patch)
    row = iota((4 * layers, slots), 0)
    line, z = row // layers, lax.rem(row, layers)
    chosen = arrived.choose(z * layer_rows + jnp.where(line < 2, line, layer_rows - 4 + line))
    for c in range(3):
        main, edge = arrived.force(chosen, c)
        main, edge = velocity[c] + main, edges[c] + edge
        for j in range(4):
            at = slice(j * layers, (j + 1) * layers)
            to = low_rows if j < 2 else high_rows
            to[c, j % 2, :, :patch] = main[at].astype(BF16)
            to[c, j % 2, :, patch:] = edge[at].astype(BF16)
        for side, at in ((0, slice(0, layers)), (1, slice(3 * layers, 4 * layers))):
            rim[side, c, :, :patch] = main[at]
            rim[side, c, :, patch:] = edge[at]


def update(centre, weights, c, east, west, north, south, up, down):
    (px, mx), (py, my), (pz, mz) = weights
    keep = 1.0 - 6.0 * viscosity
    return keep * centre[c] + px * east + mx * west + py * north + my * south + pz * up + mz * down


def mix(centre):
    return [(viscosity - transport_rate * v, viscosity + transport_rate * v) for v in centre]


def edge_mask(sides):
    lane = iota((8, LANES), 1)
    return jnp.where(lane == 0, sides[3], 0.0) + jnp.where(lane == LANES - 1, sides[2], 0.0)


def sweep(source, low_row, high_row, store, keep, after=None):
    layers, rows, wide = source.shape[1:]
    sub = iota((8, keep), 0)

    @pl.loop(0, layers)
    def _(z):
        z_up = jnp.where(z == layers - 1, 0, z + 1)
        z_down = jnp.where(z == 0, layers - 1, z - 1)
        for x in range(0, rows, 8):
            centre = [source[c, z, x : x + 8, :] for c in range(3)]
            weights = mix([v[:, :keep] for v in centre])
            for c in range(3):
                v = centre[c]
                if x + 8 < rows:
                    east = source[c, z, x + 1 : x + 9, :keep]
                else:
                    east = jnp.where(sub == 7, high_row(c, z), pltpu.roll(v[:, :keep], 7, axis=0))
                if x > 0:
                    west = source[c, z, x - 1 : x + 7, :keep]
                else:
                    west = jnp.where(sub == 0, low_row(c, z), pltpu.roll(v[:, :keep], 1, axis=0))
                new = update(
                    [w[:, :keep] for w in centre], weights, c, east, west,
                    pltpu.roll(v, wide - 1, axis=1)[:, :keep], pltpu.roll(v, 1, axis=1)[:, :keep],
                    source[c, z_up, x : x + 8, :keep], source[c, z_down, x : x + 8, :keep],
                )
                store(c, z, x, new)
        if after is not None:
            after(z)


def first_kernel(sides, velocity, edges, received, u1, u0, sems):
    layers, rows, wide = u0.shape[1:]
    patch = wide - LANES
    part = 8
    slots = received.shape[0]

    def load(step):
        at = pl.ds(step * part, part)
        return pltpu.make_async_copy(velocity.at[:, at], u0.at[:, at, :, pl.ds(0, patch)], sems.at[step])

    for step in range(layers // part):
        load(step).start()
    arrived = Arrived(received, patch)

    @pl.loop(0, layers // part)
    def _(step):
        at = pl.ds(step * part, part)
        chosen = arrived.choose(iota((part * rows, slots), 0) + step * (part * rows))
        load(step).wait()
        for c in range(3):
            main, edge = arrived.force(chosen, c)
            u0[c, at, :, :patch] += main.reshape(part, rows, patch)
            u0[c, at, :, patch:] = edges[c, at] + edge.reshape(part, rows, LANES)

    mask = edge_mask(sides)

    def store(c, z, x, new):
        u1[c, z, x : x + 8, :patch] = new[:, :patch]
        u1[c, z, x : x + 8, patch:] = new[:, patch:] * mask

    sweep(u0, lambda c, z: 0.0, lambda c, z: 0.0, store, wide)


def last_kernel(sides, u1_in, rim, below_x, above_x, received, fluid_hbm, replies, u1, mid, fluid, sems):
    layers, rows, wide = u1.shape[1:]
    patch = wide - LANES
    slots = received.shape[0]
    mask = edge_mask(sides)[0:1]

    for side in range(2):
        halo, row = (below_x, 0) if side == 0 else (above_x, rows - 1)
        near = 1 - side
        centre = [halo[c, near].astype(F32) for c in range(3)]
        weights = mix(centre)
        slope = transport_rate if side == 0 else -transport_rate
        own = viscosity + slope * rim[side, 0]
        for c in range(3):
            outer = halo[c, side].astype(F32)
            inside = rim[side, c]
            east, west = (inside, outer) if side == 0 else (outer, inside)
            v = centre[c]
            new = update(
                centre, weights, c, east, west,
                pltpu.roll(v, wide - 1, axis=1), pltpu.roll(v, 1, axis=1),
                pltpu.roll(v, layers - 1, axis=0), pltpu.roll(v, 1, axis=0),
            ) * sides[side]
            mid[side, c, :, :patch] = new[:, :patch]
            mid[side, c, :, patch:] = new[:, patch:] * mask
            term = own * v
            tail = term[:, patch:] * mask
            for z in range(layers):
                u1[c, z, row : row + 1, :patch] += term[z : z + 1, :patch]
                u1[c, z, row : row + 1, patch:] += tail[z : z + 1]

    part = 8

    def write(step):
        at = pl.ds(pl.multiple_of(step * part * rows, part * rows), part * rows)
        return pltpu.make_async_copy(fluid.at[:, at], fluid_hbm.at[:, at], sems.at[step])

    def after(z):
        @pl.when(lax.rem(z, part) == part - 1)
        def _():
            write(z // part).start()

    def store(c, z, x, new):
        fluid[c, pl.ds(pl.multiple_of(z * rows + x, 8), 8), :] = new

    sweep(
        u1,
        lambda c, z: mid[0, c, pl.ds(z, 1), :patch],
        lambda c, z: mid[1, c, pl.ds(z, 1), :patch],
        store,
        patch,
        after,
    )

    heads = received[:, 3 * patch :].astype(F32)
    slot = (heads[:, 0:1] * 32.0 + heads[:, 1:2] - 1.0).astype(jnp.int32)
    chunk = 256
    for c in range(3):
        total = jnp.zeros((slots, patch), F32)
        for first in range(0, layers * rows, chunk):
            pick = (iota((slots, chunk), 1) + first == slot).astype(F32).astype(BF16)
            total += dot(pick, fluid[c, first : first + chunk, :].astype(BF16))
        replies[:, c * patch : (c + 1) * patch] = total.astype(BF16)
    for step in range(layers // part):
        write(step).wait()


def gather_kernel(pts, dest, returned, dw_hbm, out, dw, picked, moved, sems):
    entries, slots = dest.shape[0], returned.shape[0]
    blocks, patch, points = dw.shape[0], dw.shape[2], pts.shape[2]
    inter = entries // blocks
    for b in range(blocks):
        pltpu.make_async_copy(dw_hbm.at[b], dw.at[b], sems.at[b]).start()
    to = dest[:, 0:1].astype(jnp.int32)
    pick = (iota((entries, slots), 1) == to).astype(F32).astype(BF16)
    for c in range(3):
        picked[c] = dot(pick, returned[:, c * patch : (c + 1) * patch])
    group = iota((inter, inter * points), 0)
    column = iota((inter, inter * points), 1) // points

    @pl.loop(0, blocks)
    def _(b):
        at = pl.ds(pl.multiple_of(b * inter, inter), inter)
        parts = [picked[c, at, :] for c in range(3)]
        parts.append(jnp.zeros_like(parts[0]))
        pltpu.make_async_copy(dw_hbm.at[b], dw.at[b], sems.at[b]).wait()
        every = lax.dot_general(
            jnp.concatenate(parts, axis=0).astype(BF16), dw[b], (((1,), (1,)), ((), ())), preferred_element_type=F32
        )
        for c in range(3):
            own = jnp.where(group == column, every[c * inter : (c + 1) * inter], 0.0)
            folded = own[:, :points]
            for k in range(1, inter):
                folded = folded + own[:, k * points : (k + 1) * points]
            moved[c, pl.ds(b, 1), :] = jnp.sum(folded, axis=0, keepdims=True)

    for c in range(3):
        out[c] = pts[c] + fiber_step * moved[c]


def shards(velocity, fiber_points, stiffness, links, delta_weights, owners, patch_slots):
    blocks, inter, points, patch = delta_weights.shape
    layers, rows, columns = velocity.shape[1:]
    gx_size, gy_size = lax.axis_size("gx"), lax.axis_size("gy")
    devices = gx_size * gy_size
    entries, slots, cells = blocks * inter, devices * 2, layers * rows
    wide, width = patch + LANES, 3 * patch + LANES
    mb = 1 << 20
    pts = fiber_points.transpose(1, 0, 2)
    dw = delta_weights.reshape(blocks, inter * points, patch)
    smem = pl.BlockSpec(memory_space=pltpu.SMEM)
    vmem = pl.BlockSpec(memory_space=pltpu.VMEM)
    hbm = pl.BlockSpec(memory_space=pltpu.HBM)
    anywhere = pl.BlockSpec(memory_space=pl.ANY)

    def params(limit):
        return pltpu.CompilerParams(vmem_limit_bytes=limit * mb)

    def cost(flops, size):
        return pl.CostEstimate(flops=flops, bytes_accessed=size * mb, transcendentals=0)

    outgoing, dest = pl.pallas_call(
        functools.partial(spread_kernel, gy_size, slots),
        in_specs=[hbm, smem, hbm, hbm, hbm, hbm],
        out_specs=[vmem, vmem],
        out_shape=[
            jax.ShapeDtypeStruct((slots, width), BF16),
            jax.ShapeDtypeStruct((entries, LANES), F32),
        ],
        scratch_shapes=[
            pltpu.VMEM(dw.shape, BF16),
            pltpu.VMEM((3, blocks, points), F32),
            pltpu.VMEM((3, entries, patch), F32),
            pltpu.VMEM((3, blocks, points), F32),
            pltpu.VMEM((blocks, points), jnp.int32),
            pltpu.VMEM((blocks, inter), jnp.int32),
            pltpu.VMEM((blocks, inter), jnp.int32),
            pltpu.SemaphoreType.DMA((blocks + 4,)),
        ],
        compiler_params=params(60),
        cost_estimate=cost(10**9, 9),
        name="spread",
    )(pts, stiffness, links, owners.reshape(blocks, inter), patch_slots, dw)

    def exchange(rows_out):
        size = rows_out.shape[1]
        return lax.all_to_all(
            rows_out.reshape(devices, 2, size), ("gx", "gy"), split_axis=0, concat_axis=0, tiled=True
        ).reshape(slots, size)

    received = exchange(outgoing)

    ahead = [(i + 1, i) for i in range(gy_size - 1)]
    behind = [(i, i + 1) for i in range(gy_size - 1)]
    flat = velocity.reshape(3, cells, columns)
    first = lax.ppermute(flat[:, :, :2].transpose(0, 2, 1), "gy", ahead)
    last = lax.ppermute(flat[:, :, columns - 2 :].transpose(0, 2, 1), "gy", behind)
    edge = jnp.concatenate(
        [first.transpose(0, 2, 1), jnp.zeros((3, cells, LANES - 4), F32), last.transpose(0, 2, 1)], axis=2
    )
    lines = (0, 1, rows - 2, rows - 1)
    rim_velocity = jnp.stack([velocity[:, :, x, :] for x in lines], axis=1).reshape(3, 4 * layers, patch)
    edge = edge.reshape(3, layers, rows, LANES)
    rim_edge = jnp.stack([edge[:, :, x, :] for x in lines], axis=1).reshape(3, 4 * layers, LANES)

    side = (3, 2, layers, wide)
    low_rows, high_rows, rim = pl.pallas_call(
        functools.partial(rim_kernel, rows),
        in_specs=[vmem] * 3,
        out_specs=[vmem] * 3,
        out_shape=[
            jax.ShapeDtypeStruct(side, BF16),
            jax.ShapeDtypeStruct(side, BF16),
            jax.ShapeDtypeStruct((2, 3, layers, wide), F32),
        ],
        compiler_params=params(24),
        cost_estimate=cost(10**8, 3),
        name="rim",
    )(rim_velocity, rim_edge, received)

    up = [(i, i + 1) for i in range(gx_size - 1)]
    below_x = lax.ppermute(high_rows, "gx", up)
    above_x = lax.ppermute(low_rows, "gx", [(b, a) for a, b in up])

    gx, gy = lax.axis_index("gx"), lax.axis_index("gy")
    sides = jnp.stack([gx > 0, gx < gx_size - 1, gy > 0, gy < gy_size - 1]).astype(F32)
    u1 = pl.pallas_call(
        first_kernel,
        in_specs=[smem, hbm, vmem, vmem],
        out_specs=vmem,
        out_shape=jax.ShapeDtypeStruct((3, layers, rows, wide), F32),
        scratch_shapes=[pltpu.VMEM((3, layers, rows, wide), F32), pltpu.SemaphoreType.DMA((layers // 8,))],
        compiler_params=params(24),
        cost_estimate=cost(2 * 10**9, 24),
        name="sweep_first",
    )(sides, pltpu.with_memory_space_constraint(velocity, pltpu.HBM), edge, received)
    fluid, replies, _ = pl.pallas_call(
        last_kernel,
        in_specs=[smem] + [vmem] * 5,
        out_specs=[hbm, vmem, vmem],
        out_shape=[
            jax.ShapeDtypeStruct((3, cells, patch), F32),
            jax.ShapeDtypeStruct((slots, 3 * patch), BF16),
            jax.ShapeDtypeStruct((3, layers, rows, wide), F32),
        ],
        scratch_shapes=[
            pltpu.VMEM((2, 3, layers, wide), F32),
            pltpu.VMEM((3, cells, patch), F32),
            pltpu.SemaphoreType.DMA((layers // 8,)),
        ],
        input_output_aliases={1: 2},
        compiler_params=params(24),
        cost_estimate=cost(2 * 10**9, 16),
        name="sweep_last",
    )(sides, u1, rim, below_x, above_x, received)

    returned = exchange(replies)
    moved = pl.pallas_call(
        gather_kernel,
        in_specs=[vmem] * 3 + [hbm],
        out_specs=vmem,
        out_shape=jax.ShapeDtypeStruct((3, blocks, points), F32),
        scratch_shapes=[
            pltpu.VMEM(dw.shape, BF16),
            pltpu.VMEM((3, entries, patch), F32),
            pltpu.VMEM((3, blocks, points), F32),
            pltpu.SemaphoreType.DMA((blocks,)),
        ],
        compiler_params=params(56),
        cost_estimate=cost(10**9, 9),
        name="interp",
    )(pts, dest, returned, dw)
    return fluid.reshape(3, layers, rows, columns), moved.transpose(1, 0, 2)


def solution(mesh):
    placed = (
        P(None, None, "gx", "gy"),
        P(("gx", "gy"), None, None),
        P(("gx", "gy")),
        P(("gx", "gy"), None),
        P(("gx", "gy"), None, None, None),
        P(("gx", "gy"), None, None),
        P(("gx", "gy"), None),
    )
    return jax.shard_map(
        shards,
        mesh=mesh,
        in_specs=placed,
        out_specs=(P(None, None, "gx", "gy"), P(("gx", "gy"), None, None)),
        check_vma=False,
    )
```

```python
import functools

import jax
import jax.numpy as jnp
from jax import lax
from jax.experimental import pallas as pl
from jax.experimental.pallas import tpu as pltpu
from jax.sharding import PartitionSpec as P

viscosity = 0.1
transport_rate = 0.1
force_step = 0.5
fiber_step = 0.25

F32 = jnp.float32
BF16 = jnp.bfloat16
LANES = 128
BELOW, ABOVE = 2, 10


def dot(a, b):
    return jnp.dot(a, b, preferred_element_type=F32)


def iota(shape, axis):
    return lax.broadcasted_iota(jnp.int32, shape, axis)


def spread_kernel(
    gy_size, slots, pts_hbm, stiff_hbm, links_hbm, owners_hbm, patch_slots_hbm, dw_hbm, out, dest_out,
    dw, force, rows, choose, pts, stiff, links, owners, patch_slots, sems,
):
    blocks, points = links.shape
    inter = owners.shape[1]
    entries = blocks * inter
    patch = rows.shape[2]
    small = [
        (pts_hbm, pts), (stiff_hbm, stiff), (links_hbm, links), (owners_hbm, owners), (patch_slots_hbm, patch_slots)
    ]
    small = [pltpu.make_async_copy(a, b, sems.at[blocks + i]) for i, (a, b) in enumerate(small)]
    for copy in small + [pltpu.make_async_copy(dw_hbm.at[b], dw.at[b], sems.at[b]) for b in range(blocks)]:
        copy.start()
    for copy in small:
        copy.wait()
    partner = lax.rem(iota((blocks, points), 1) + links[...], points)
    for c in range(3):
        own = pts[c]
        force[c] = jnp.take_along_axis(own, partner, axis=1) - own

    pick_block = (iota((entries, blocks), 0) // inter == iota((entries, blocks), 1)).astype(F32).astype(BF16)
    pick_k = lax.rem(iota((entries, inter), 0), inter) == iota((entries, inter), 1)

    def as_column(table):
        spread_rows = dot(pick_block, table.astype(F32).astype(BF16))
        return jnp.sum(jnp.where(pick_k, spread_rows, 0.0), axis=1, keepdims=True)

    owner = as_column(owners[...])
    code = patch_slots[...] + 1
    high, low = as_column(code // 32), as_column(lax.rem(code, 32))
    owner_wide = jnp.broadcast_to(owner, (entries, LANES))
    owner_row = jnp.transpose(
        jnp.concatenate([owner_wide, jnp.zeros((LANES - entries, LANES), F32)], axis=0)
    )[:entries, :entries]
    same = (owner_wide[:, :entries] == owner_row) & (iota((entries, entries), 1) < iota((entries, entries), 0))
    rank = jnp.sum(jnp.where(same, 1.0, 0.0), axis=1, keepdims=True)
    dest_wide = jnp.broadcast_to(owner * 2.0 + rank, (entries, LANES))
    dest_out[...] = dest_wide
    padded = jnp.concatenate([dest_wide, jnp.full((LANES - entries, LANES), -8.0, F32)], axis=0)
    dest_row = jnp.transpose(padded)[0:1, :entries].astype(jnp.int32)
    position = lax.rem(dest_row // 2, gy_size)
    slot = iota((slots, entries), 0)
    choose[0] = (slot == dest_row).astype(F32).astype(BF16)
    choose[1] = ((slot == dest_row + 2) & (position < gy_size - 1)).astype(F32).astype(BF16)
    choose[2] = ((slot == dest_row - 2) & (position > 0)).astype(F32).astype(BF16)
    lane = iota((entries, LANES), 1)

    def digits(at):
        return jnp.where(lane == at, high, 0.0) + jnp.where(lane == at + 1, low, 0.0)

    own_head, above_head, below_head = digits(0), digits(BELOW), digits(ABOVE)
    group = iota((inter, inter * points), 0)
    column = iota((inter, inter * points), 1) // points

    @pl.loop(0, blocks)
    def _(b):
        stiffness = stiff[b]
        parts = []
        for c in range(3):
            row = (stiffness * force[c, pl.ds(b, 1), :]).astype(BF16).astype(F32)
            wide = jnp.concatenate([jnp.broadcast_to(row, (inter, points))] * inter, axis=1)
            parts.append(jnp.where(group == column, wide, 0.0))
        parts.append(jnp.zeros_like(parts[0]))
        pltpu.make_async_copy(dw_hbm.at[b], dw.at[b], sems.at[b]).wait()
        spread = dot(jnp.concatenate(parts, axis=0).astype(BF16), dw[b])
        for c in range(3):
            rows[c, pl.ds(pl.multiple_of(b * inter, inter), inter), :] = spread[c * inter : (c + 1) * inter]

    for c in range(3):
        tail = pltpu.roll(rows[c, :, patch - LANES :], BELOW + 4 + 2 * c, axis=1)
        at = BELOW + 2 + 2 * c
        above_head += jnp.where((lane == at) | (lane == at + 1), tail, 0.0)
        at = ABOVE + 2 + 2 * c
        start = pltpu.roll(rows[c, :, :LANES], at, axis=1)
        below_head += jnp.where((lane == at) | (lane == at + 1), start, 0.0)
        out[:, c * patch : (c + 1) * patch] = dot(choose[0], rows[c].astype(BF16)).astype(BF16)
    head = dot(choose[0], own_head.astype(BF16))
    head += dot(choose[1], above_head.astype(BF16))
    head += dot(choose[2], below_head.astype(BF16))
    out[:, 3 * patch :] = head.astype(BF16)


class Arrived:
    def __init__(self, received, patch):
        self.received, self.patch = received, patch
        slots = received.shape[0]
        head = received[:, 3 * patch :].astype(F32)
        head_t = jnp.transpose(head)
        lane = iota((slots, LANES), 1)
        self.tails, self.starts = [], []
        for c in range(3):
            tail = pltpu.roll(head, LANES - 4 - BELOW - 2 * c, axis=1)
            self.tails.append(jnp.where(lane >= LANES - 2, tail, 0.0).astype(BF16))
            start = pltpu.roll(head, LANES - (ABOVE + 2 + 2 * c), axis=1)
            self.starts.append(jnp.where(lane < 2, start, 0.0).astype(BF16))
        self.slots = [
            (head_t[at : at + 1] * 32.0 + head_t[at + 1 : at + 2] - 1.0).astype(jnp.int32) for at in (0, BELOW, ABOVE)
        ]

    def choose(self, row):
        return [(row == slot).astype(F32).astype(BF16) for slot in self.slots]

    def force(self, chosen, c):
        here, below, above = chosen
        main = dot(here, self.received[:, c * self.patch : (c + 1) * self.patch])
        return force_step * main, force_step * (dot(below, self.tails[c]) + dot(above, self.starts[c]))


def rim_kernel(layer_rows, velocity, edges, received, low_rows, high_rows, rim):
    layers, patch = low_rows.shape[2], velocity.shape[2]
    slots = received.shape[0]
    arrived = Arrived(received, patch)
    row = iota((4 * layers, slots), 0)
    line, z = row // layers, lax.rem(row, layers)
    chosen = arrived.choose(z * layer_rows + jnp.where(line < 2, line, layer_rows - 4 + line))
    for c in range(3):
        main, edge = arrived.force(chosen, c)
        main, edge = velocity[c] + main, edges[c] + edge
        for j in range(4):
            at = slice(j * layers, (j + 1) * layers)
            to = low_rows if j < 2 else high_rows
            to[c, j % 2, :, :patch] = main[at].astype(BF16)
            to[c, j % 2, :, patch:] = edge[at].astype(BF16)
        for side, at in ((0, slice(0, layers)), (1, slice(3 * layers, 4 * layers))):
            rim[side, c, :, :patch] = main[at]
            rim[side, c, :, patch:] = edge[at]


def update(centre, weights, c, east, west, north, south, up, down):
    (px, mx), (py, my), (pz, mz) = weights
    keep = 1.0 - 6.0 * viscosity
    return keep * centre[c] + px * east + mx * west + py * north + my * south + pz * up + mz * down


def mix(centre):
    return [(viscosity - transport_rate * v, viscosity + transport_rate * v) for v in centre]


def edge_mask(sides):
    lane = iota((8, LANES), 1)
    return jnp.where(lane == 0, sides[3], 0.0) + jnp.where(lane == LANES - 1, sides[2], 0.0)


def sweep(source, low_row, high_row, store, tiles, after=None):
    layers, rows, wide = source.shape[1:]
    count = wide // LANES
    sub, lane = iota((8, LANES), 0), iota((8, LANES), 1)
    first_sub, last_sub, first_lane, last_lane = sub == 0, sub == 7, lane == 0, lane == LANES - 1

    @pl.loop(0, layers, step=2)
    def _(even):
        for z, up, down in (
            (even, even + 1, jnp.where(even == 0, layers - 1, even - 1)),
            (even + 1, jnp.where(even == layers - 2, 0, even + 2), even),
        ):
            below = [low_row(c, z) for c in range(3)]
            above = [high_row(c, z) for c in range(3)]
            for x in range(0, rows, 8):
                for t in range(tiles):
                    at = slice(t * LANES, (t + 1) * LANES)
                    centre = [source[c, z, x : x + 8, at] for c in range(3)]
                    weights = mix(centre)
                    for c in range(3):
                        v = centre[c]
                        ahead = source[c, z, x + 8 : x + 16, at] if x + 8 < rows else above[c][:, at]
                        behind = source[c, z, x - 8 : x, at] if x > 0 else below[c][:, at]
                        right = (t + 1) % count * LANES
                        left = (t - 1) % count * LANES
                        right = source[c, z, x : x + 8, right : right + LANES]
                        left = source[c, z, x : x + 8, left : left + LANES]
                        new = update(
                            centre, weights, c,
                            pltpu.roll(jnp.where(first_sub, ahead, v), 7, axis=0),
                            pltpu.roll(jnp.where(last_sub, behind, v), 1, axis=0),
                            pltpu.roll(jnp.where(first_lane, right, v), LANES - 1, axis=1),
                            pltpu.roll(jnp.where(last_lane, left, v), 1, axis=1),
                            source[c, up, x : x + 8, at],
                            source[c, down, x : x + 8, at],
                        )
                        store(c, z, x, at, new)
        if after is not None:
            after(even + 1)


def first_kernel(sides, velocity, edges, received, u1, u0, sems):
    layers, rows, wide = u0.shape[1:]
    patch = wide - LANES
    part = 8
    slots = received.shape[0]

    def load(step):
        at = pl.ds(step * part, part)
        return pltpu.make_async_copy(velocity.at[:, at], u0.at[:, at, :, pl.ds(0, patch)], sems.at[step])

    for step in range(layers // part):
        load(step).start()
    arrived = Arrived(received, patch)

    @pl.loop(0, layers // part)
    def _(step):
        at = pl.ds(step * part, part)
        chosen = arrived.choose(iota((part * rows, slots), 0) + step * (part * rows))
        load(step).wait()
        for c in range(3):
            main, edge = arrived.force(chosen, c)
            u0[c, at, :, :patch] += main.reshape(part, rows, patch)
            u0[c, at, :, patch:] = edges[c, at] + edge.reshape(part, rows, LANES)

    mask = edge_mask(sides)

    def store(c, z, x, at, new):
        u1[c, z, x : x + 8, at] = new * mask if at.start == patch else new

    nothing = jnp.zeros((1, wide), F32)
    sweep(u0, lambda c, z: nothing, lambda c, z: nothing, store, wide // LANES)


def last_kernel(sides, u1_in, rim, below_x, above_x, received, fluid_hbm, replies, u1, mid, fluid, sems):
    layers, rows, wide = u1.shape[1:]
    patch = wide - LANES
    slots = received.shape[0]
    mask = edge_mask(sides)[0:1]

    for side in range(2):
        halo, row = (below_x, 0) if side == 0 else (above_x, rows - 1)
        near = 1 - side
        centre = [halo[c, near].astype(F32) for c in range(3)]
        weights = mix(centre)
        slope = transport_rate if side == 0 else -transport_rate
        own = viscosity + slope * rim[side, 0]
        for c in range(3):
            outer = halo[c, side].astype(F32)
            inside = rim[side, c]
            east, west = (inside, outer) if side == 0 else (outer, inside)
            v = centre[c]
            new = update(
                centre, weights, c, east, west,
                pltpu.roll(v, wide - 1, axis=1), pltpu.roll(v, 1, axis=1),
                pltpu.roll(v, layers - 1, axis=0), pltpu.roll(v, 1, axis=0),
            ) * sides[side]
            mid[side, c, :, :patch] = new[:, :patch]
            mid[side, c, :, patch:] = new[:, patch:] * mask
            term = own * v
            tail = term[:, patch:] * mask
            for z in range(layers):
                u1[c, z, row : row + 1, :patch] += term[z : z + 1, :patch]
                u1[c, z, row : row + 1, patch:] += tail[z : z + 1]

    part = 8

    def write(step):
        at = pl.ds(pl.multiple_of(step * part * rows, part * rows), part * rows)
        return pltpu.make_async_copy(fluid.at[:, at], fluid_hbm.at[:, at], sems.at[step])

    def after(z):
        @pl.when(lax.rem(z, part) == part - 1)
        def _():
            write(z // part).start()

    def store(c, z, x, at, new):
        fluid[c, pl.ds(pl.multiple_of(z * rows + x, 8), 8), at] = new

    sweep(
        u1,
        lambda c, z: mid[0, c, pl.ds(z, 1), :patch],
        lambda c, z: mid[1, c, pl.ds(z, 1), :patch],
        store,
        patch // LANES,
        after,
    )

    heads = received[:, 3 * patch :].astype(F32)
    slot = (heads[:, 0:1] * 32.0 + heads[:, 1:2] - 1.0).astype(jnp.int32)
    chunk = 256
    for c in range(3):
        total = jnp.zeros((slots, patch), F32)
        for first in range(0, layers * rows, chunk):
            pick = (iota((slots, chunk), 1) + first == slot).astype(F32).astype(BF16)
            total += dot(pick, fluid[c, first : first + chunk, :].astype(BF16))
        replies[:, c * patch : (c + 1) * patch] = total.astype(BF16)
    for step in range(layers // part):
        write(step).wait()


def gather_kernel(pts, dest, returned, dw_hbm, out, dw, picked, moved, sems):
    entries, slots = dest.shape[0], returned.shape[0]
    blocks, patch, points = dw.shape[0], dw.shape[2], pts.shape[2]
    inter = entries // blocks
    for b in range(blocks):
        pltpu.make_async_copy(dw_hbm.at[b], dw.at[b], sems.at[b]).start()
    to = dest[:, 0:1].astype(jnp.int32)
    pick = (iota((entries, slots), 1) == to).astype(F32).astype(BF16)
    for c in range(3):
        picked[c] = dot(pick, returned[:, c * patch : (c + 1) * patch])
    k_of_lane = lax.rem(iota((points, LANES), 1), inter)

    @pl.loop(0, blocks)
    def _(b):
        at = pl.ds(pl.multiple_of(b * inter, inter), inter)
        parts = [picked[c, at, :] for c in range(3)]
        parts.append(jnp.zeros((LANES - 3 * inter, patch), F32))
        cells = jnp.concatenate(parts, axis=0).astype(BF16)
        pltpu.make_async_copy(dw_hbm.at[b], dw.at[b], sems.at[b]).wait()
        every = lax.dot_general(dw[b], cells, (((1,), (1,)), ((), ())), preferred_element_type=F32)
        folded = jnp.zeros((points, LANES), F32)
        for k in range(inter):
            folded += jnp.where(k_of_lane == k, every[k * points : (k + 1) * points], 0.0)
        turned = jnp.transpose(folded)
        for c in range(3):
            moved[c, pl.ds(b, 1), :] = jnp.sum(turned[c * inter : (c + 1) * inter], axis=0, keepdims=True)

    for c in range(3):
        out[c] = pts[c] + fiber_step * moved[c]


def in_hbm(x):
    return pltpu.with_memory_space_constraint(x, pltpu.HBM)


def params(limit):
    return pltpu.CompilerParams(vmem_limit_bytes=limit << 20)


def cost(flops, size):
    return pl.CostEstimate(flops=flops, bytes_accessed=size << 20, transcendentals=0)


SMEM = pl.BlockSpec(memory_space=pltpu.SMEM)
VMEM = pl.BlockSpec(memory_space=pltpu.VMEM)
HBM = pl.BlockSpec(memory_space=pltpu.HBM)


def run_spread(gy_size, slots, pts, stiffness, links, owners, patch_slots, dw):
    blocks, points = links.shape
    inter, patch = owners.shape[1], dw.shape[2]
    entries = blocks * inter
    return pl.pallas_call(
        functools.partial(spread_kernel, gy_size, slots),
        in_specs=[HBM] * 6,
        out_specs=[VMEM, VMEM],
        out_shape=[
            jax.ShapeDtypeStruct((slots, 3 * patch + LANES), BF16),
            jax.ShapeDtypeStruct((entries, LANES), F32),
        ],
        scratch_shapes=[
            pltpu.VMEM(dw.shape, BF16),
            pltpu.VMEM((3, blocks, points), F32),
            pltpu.VMEM((3, entries, patch), F32),
            pltpu.VMEM((3, slots, entries), BF16),
            pltpu.VMEM((3, blocks, points), F32),
            pltpu.SMEM((blocks,), F32),
            pltpu.VMEM((blocks, points), jnp.int32),
            pltpu.VMEM((blocks, inter), jnp.int32),
            pltpu.VMEM((blocks, inter), jnp.int32),
            pltpu.SemaphoreType.DMA((blocks + 5,)),
        ],
        compiler_params=params(24),
        cost_estimate=cost(10**9, 9),
        name="spread",
    )(*[in_hbm(x) for x in (pts, stiffness, links, owners, patch_slots, dw)])


def run_rim(layer_rows, layers, rim_velocity, rim_edge, received):
    patch = rim_velocity.shape[2]
    wide = patch + LANES
    side = (3, 2, layers, wide)
    return pl.pallas_call(
        functools.partial(rim_kernel, layer_rows),
        in_specs=[VMEM] * 3,
        out_specs=[VMEM] * 3,
        out_shape=[
            jax.ShapeDtypeStruct(side, BF16),
            jax.ShapeDtypeStruct(side, BF16),
            jax.ShapeDtypeStruct((2, 3, layers, wide), F32),
        ],
        compiler_params=params(24),
        cost_estimate=cost(10**8, 3),
        name="rim",
    )(rim_velocity, rim_edge, received)


def run_first(sides, velocity, edge, received):
    layers, rows, patch = velocity.shape[1:]
    block = (3, layers, rows, patch + LANES)
    return pl.pallas_call(
        first_kernel,
        in_specs=[SMEM, HBM, VMEM, VMEM],
        out_specs=VMEM,
        out_shape=jax.ShapeDtypeStruct(block, F32),
        scratch_shapes=[pltpu.VMEM(block, F32), pltpu.SemaphoreType.DMA((layers // 8,))],
        compiler_params=params(24),
        cost_estimate=cost(2 * 10**9, 24),
        name="sweep_first",
    )(sides, in_hbm(velocity), edge, received)


def run_last(sides, u1, rim, below_x, above_x, received):
    layers, rows, wide = u1.shape[1:]
    patch, slots = wide - LANES, received.shape[0]
    return pl.pallas_call(
        last_kernel,
        in_specs=[SMEM] + [VMEM] * 5,
        out_specs=[HBM, VMEM, VMEM],
        out_shape=[
            jax.ShapeDtypeStruct((3, layers * rows, patch), F32),
            jax.ShapeDtypeStruct((slots, 3 * patch), BF16),
            jax.ShapeDtypeStruct(u1.shape, F32),
        ],
        scratch_shapes=[
            pltpu.VMEM((2, 3, layers, wide), F32),
            pltpu.VMEM((3, layers * rows, patch), F32),
            pltpu.SemaphoreType.DMA((layers // 8,)),
        ],
        input_output_aliases={1: 2},
        compiler_params=params(24),
        cost_estimate=cost(2 * 10**9, 16),
        name="sweep_last",
    )(sides, u1, rim, below_x, above_x, received)[:2]


def run_gather(pts, dest, returned, dw):
    blocks, patch = dw.shape[0], dw.shape[2]
    return pl.pallas_call(
        gather_kernel,
        in_specs=[VMEM] * 3 + [HBM],
        out_specs=VMEM,
        out_shape=jax.ShapeDtypeStruct(pts.shape, F32),
        scratch_shapes=[
            pltpu.VMEM(dw.shape, BF16),
            pltpu.VMEM((3, dest.shape[0], patch), F32),
            pltpu.VMEM(pts.shape, F32),
            pltpu.SemaphoreType.DMA((blocks,)),
        ],
        compiler_params=params(24),
        cost_estimate=cost(10**9, 9),
        name="interp",
    )(pts, dest, returned, in_hbm(dw))


def shards(velocity, fiber_points, stiffness, links, delta_weights, owners, patch_slots):
    blocks, inter, points, patch = delta_weights.shape
    layers, rows, columns = velocity.shape[1:]
    gx_size, gy_size = lax.axis_size("gx"), lax.axis_size("gy")
    devices = gx_size * gy_size
    slots, cells = devices * 2, layers * rows
    pts = fiber_points.transpose(1, 0, 2)
    dw = delta_weights.reshape(blocks, inter * points, patch)
    outgoing, dest = run_spread(
        gy_size, slots, pts, stiffness, links, owners.reshape(blocks, inter), patch_slots, dw
    )

    def exchange(rows_out):
        size = rows_out.shape[1]
        return lax.all_to_all(
            rows_out.reshape(devices, 2, size), ("gx", "gy"), split_axis=0, concat_axis=0, tiled=True
        ).reshape(slots, size)

    received = exchange(outgoing)

    ahead = [(i + 1, i) for i in range(gy_size - 1)]
    behind = [(i, i + 1) for i in range(gy_size - 1)]
    flat = velocity.reshape(3, cells, columns)
    first = lax.ppermute(flat[:, :, :2].transpose(0, 2, 1), "gy", ahead)
    last = lax.ppermute(flat[:, :, columns - 2 :].transpose(0, 2, 1), "gy", behind)
    edge = jnp.concatenate(
        [first.transpose(0, 2, 1), jnp.zeros((3, cells, LANES - 4), F32), last.transpose(0, 2, 1)], axis=2
    ).reshape(3, layers, rows, LANES)
    lines = (0, 1, rows - 2, rows - 1)
    rim_velocity = jnp.stack([velocity[:, :, x, :] for x in lines], axis=1).reshape(3, 4 * layers, patch)
    rim_edge = jnp.stack([edge[:, :, x, :] for x in lines], axis=1).reshape(3, 4 * layers, LANES)
    low_rows, high_rows, rim = run_rim(rows, layers, rim_velocity, rim_edge, received)

    up = [(i, i + 1) for i in range(gx_size - 1)]
    below_x = lax.ppermute(high_rows, "gx", up)
    above_x = lax.ppermute(low_rows, "gx", [(b, a) for a, b in up])
    gx, gy = lax.axis_index("gx"), lax.axis_index("gy")
    sides = jnp.stack([gx > 0, gx < gx_size - 1, gy > 0, gy < gy_size - 1]).astype(F32)
    u1 = run_first(sides, velocity, edge, received)
    fluid, replies = run_last(sides, u1, rim, below_x, above_x, received)
    moved = run_gather(pts, dest, exchange(replies), dw)
    return fluid.reshape(3, layers, rows, columns), moved.transpose(1, 0, 2)


def solution(mesh):
    placed = (
        P(None, None, "gx", "gy"),
        P(("gx", "gy"), None, None),
        P(("gx", "gy")),
        P(("gx", "gy"), None),
        P(("gx", "gy"), None, None, None),
        P(("gx", "gy"), None, None),
        P(("gx", "gy"), None),
    )
    return jax.shard_map(
        shards,
        mesh=mesh,
        in_specs=placed,
        out_specs=(P(None, None, "gx", "gy"), P(("gx", "gy"), None, None)),
        check_vma=False,
    )
```

```python
import functools

import jax
import jax.numpy as jnp
from jax import lax
from jax.experimental import pallas as pl
from jax.experimental.pallas import tpu as pltpu
from jax.sharding import PartitionSpec as P

viscosity = 0.1
transport_rate = 0.1
force_step = 0.5
fiber_step = 0.25

F32 = jnp.float32
BF16 = jnp.bfloat16
LANES = 128
BELOW, ABOVE = 2, 10


def dot(a, b):
    return jnp.dot(a, b, preferred_element_type=F32)


def iota(shape, axis):
    return lax.broadcasted_iota(jnp.int32, shape, axis)


def spread_kernel(
    gy_size, slots, pts_hbm, stiff_hbm, links_hbm, owners_hbm, patch_slots_hbm, dw_hbm, out, dest_out,
    dw, force, rows, choose, pts, stiff, links, owners, patch_slots, sems,
):
    blocks, points = links.shape
    inter = owners.shape[1]
    entries = blocks * inter
    patch = rows.shape[2]
    small = [
        (pts_hbm, pts), (stiff_hbm, stiff), (links_hbm, links), (owners_hbm, owners), (patch_slots_hbm, patch_slots)
    ]
    small = [pltpu.make_async_copy(a, b, sems.at[blocks + i]) for i, (a, b) in enumerate(small)]
    for copy in small + [pltpu.make_async_copy(dw_hbm.at[b], dw.at[b], sems.at[b]) for b in range(blocks)]:
        copy.start()
    for copy in small:
        copy.wait()
    partner = lax.rem(iota((blocks, points), 1) + links[...], points)
    for c in range(3):
        own = pts[c]
        force[c] = jnp.take_along_axis(own, partner, axis=1) - own

    pick_block = (iota((entries, blocks), 0) // inter == iota((entries, blocks), 1)).astype(F32).astype(BF16)
    pick_k = lax.rem(iota((entries, inter), 0), inter) == iota((entries, inter), 1)

    def as_column(table):
        spread_rows = dot(pick_block, table.astype(F32).astype(BF16))
        return jnp.sum(jnp.where(pick_k, spread_rows, 0.0), axis=1, keepdims=True)

    owner = as_column(owners[...])
    code = patch_slots[...] + 1
    high, low = as_column(code // 32), as_column(lax.rem(code, 32))
    owner_wide = jnp.broadcast_to(owner, (entries, LANES))
    owner_row = jnp.transpose(
        jnp.concatenate([owner_wide, jnp.zeros((LANES - entries, LANES), F32)], axis=0)
    )[:entries, :entries]
    same = (owner_wide[:, :entries] == owner_row) & (iota((entries, entries), 1) < iota((entries, entries), 0))
    rank = jnp.sum(jnp.where(same, 1.0, 0.0), axis=1, keepdims=True)
    dest_wide = jnp.broadcast_to(owner * 2.0 + rank, (entries, LANES))
    dest_out[...] = dest_wide
    padded = jnp.concatenate([dest_wide, jnp.full((LANES - entries, LANES), -8.0, F32)], axis=0)
    dest_row = jnp.transpose(padded)[0:1, :entries].astype(jnp.int32)
    position = lax.rem(dest_row // 2, gy_size)
    slot = iota((slots, entries), 0)
    choose[0] = (slot == dest_row).astype(F32).astype(BF16)
    choose[1] = ((slot == dest_row + 2) & (position < gy_size - 1)).astype(F32).astype(BF16)
    choose[2] = ((slot == dest_row - 2) & (position > 0)).astype(F32).astype(BF16)
    lane = iota((entries, LANES), 1)

    def digits(at):
        return jnp.where(lane == at, high, 0.0) + jnp.where(lane == at + 1, low, 0.0)

    own_head, above_head, below_head = digits(0), digits(BELOW), digits(ABOVE)
    group = iota((inter, inter * points), 0)
    column = iota((inter, inter * points), 1) // points

    @pl.loop(0, blocks)
    def _(b):
        stiffness = stiff[b]
        parts = []
        for c in range(3):
            row = (stiffness * force[c, pl.ds(b, 1), :]).astype(BF16).astype(F32)
            wide = jnp.concatenate([jnp.broadcast_to(row, (inter, points))] * inter, axis=1)
            parts.append(jnp.where(group == column, wide, 0.0))
        parts.append(jnp.zeros_like(parts[0]))
        pltpu.make_async_copy(dw_hbm.at[b], dw.at[b], sems.at[b]).wait()
        spread = dot(jnp.concatenate(parts, axis=0).astype(BF16), dw[b])
        for c in range(3):
            rows[c, pl.ds(pl.multiple_of(b * inter, inter), inter), :] = spread[c * inter : (c + 1) * inter]

    for c in range(3):
        tail = pltpu.roll(rows[c, :, patch - LANES :], BELOW + 4 + 2 * c, axis=1)
        at = BELOW + 2 + 2 * c
        above_head += jnp.where((lane == at) | (lane == at + 1), tail, 0.0)
        at = ABOVE + 2 + 2 * c
        start = pltpu.roll(rows[c, :, :LANES], at, axis=1)
        below_head += jnp.where((lane == at) | (lane == at + 1), start, 0.0)
        out[:, c * patch : (c + 1) * patch] = dot(choose[0], rows[c].astype(BF16)).astype(BF16)
    head = dot(choose[0], own_head.astype(BF16))
    head += dot(choose[1], above_head.astype(BF16))
    head += dot(choose[2], below_head.astype(BF16))
    out[:, 3 * patch :] = head.astype(BF16)


class Arrived:
    def __init__(self, received, patch):
        self.received, self.patch = received, patch
        slots = received.shape[0]
        head = received[:, 3 * patch :].astype(F32)
        head_t = jnp.transpose(head)
        lane = iota((slots, LANES), 1)
        self.tails, self.starts = [], []
        for c in range(3):
            tail = pltpu.roll(head, LANES - 4 - BELOW - 2 * c, axis=1)
            self.tails.append(jnp.where(lane >= LANES - 2, tail, 0.0).astype(BF16))
            start = pltpu.roll(head, LANES - (ABOVE + 2 + 2 * c), axis=1)
            self.starts.append(jnp.where(lane < 2, start, 0.0).astype(BF16))
        self.slots = [
            (head_t[at : at + 1] * 32.0 + head_t[at + 1 : at + 2] - 1.0).astype(jnp.int32) for at in (0, BELOW, ABOVE)
        ]

    def choose(self, row):
        return [(row == slot).astype(F32).astype(BF16) for slot in self.slots]

    def force(self, chosen, c):
        here, below, above = chosen
        main = dot(here, self.received[:, c * self.patch : (c + 1) * self.patch])
        return force_step * main, force_step * (dot(below, self.tails[c]) + dot(above, self.starts[c]))


def rim_kernel(layer_rows, velocity, edges, received, low_rows, high_rows, rim):
    layers, patch = low_rows.shape[2], velocity.shape[2]
    slots = received.shape[0]
    arrived = Arrived(received, patch)
    row = iota((4 * layers, slots), 0)
    line, z = row // layers, lax.rem(row, layers)
    chosen = arrived.choose(z * layer_rows + jnp.where(line < 2, line, layer_rows - 4 + line))
    for c in range(3):
        main, edge = arrived.force(chosen, c)
        main, edge = velocity[c] + main, edges[c] + edge
        for j in range(4):
            at = slice(j * layers, (j + 1) * layers)
            to = low_rows if j < 2 else high_rows
            to[c, j % 2, :, :patch] = main[at].astype(BF16)
            to[c, j % 2, :, patch:] = edge[at].astype(BF16)
        for side, at in ((0, slice(0, layers)), (1, slice(3 * layers, 4 * layers))):
            for t in range(patch // LANES):
                rim[side, c, t] = main[at, t * LANES : (t + 1) * LANES]
            rim[side, c, patch // LANES] = edge[at]


def update(centre, weights, c, east, west, north, south, up, down):
    (px, mx), (py, my), (pz, mz) = weights
    keep = 1.0 - 6.0 * viscosity
    return keep * centre[c] + px * east + mx * west + py * north + my * south + pz * up + mz * down


def mix(centre):
    return [(viscosity - transport_rate * v, viscosity + transport_rate * v) for v in centre]


def beside():
    flags = []
    for axis in ("gx", "gy"):
        at, size = lax.axis_index(axis), lax.axis_size(axis)
        flags += [jnp.where(at > 0, 1.0, 0.0).astype(F32), jnp.where(at < size - 1, 1.0, 0.0).astype(F32)]
    return flags


def edge_mask(sides):
    lane = iota((8, LANES), 1)
    return jnp.where(lane == 0, sides[3], 0.0) + jnp.where(lane == LANES - 1, sides[2], 0.0)


def rows_at(z, x, rows):
    return pl.ds(pl.multiple_of(z * rows + x, 8), 8)


def shifted(v, ahead, behind, axis):
    size = v.shape[axis]
    at = iota(v.shape, axis)
    return (
        pltpu.roll(jnp.where(at == 0, ahead, v), size - 1, axis=axis),
        pltpu.roll(jnp.where(at == size - 1, behind, v), 1, axis=axis),
    )


def sweep_pair(source, layers, z, low_row, high_row, store, tiles):
    count, rows = source.shape[1], source.shape[2] // layers
    z1 = lax.rem(z + 1, layers)
    for z, up, down in ((z, z1, lax.rem(z + layers - 1, layers)), (z1, lax.rem(z + 2, layers), z)):
        for x in range(0, rows, 8):
            for t in range(tiles):
                here = rows_at(z, x, rows)
                centre = [source[c, t, here, :] for c in range(3)]
                weights = mix(centre)
                for c in range(3):
                    v = centre[c]
                    ahead = source[c, t, rows_at(z, x + 8, rows), :] if x + 8 < rows else high_row(c, t, z)
                    behind = source[c, t, rows_at(z, x - 8, rows), :] if x > 0 else low_row(c, t, z)
                    east, west = shifted(v, ahead, behind, 0)
                    north, south = shifted(v, source[c, (t + 1) % count, here, :], source[c, (t - 1) % count, here, :], 1)
                    above, below = source[c, t, rows_at(up, x, rows), :], source[c, t, rows_at(down, x, rows), :]
                    store(c, t, here, update(centre, weights, c, east, west, north, south, above, below))


def first_kernel(layers, velocity, edges, received, u1, u0, sems):
    count, cells = u0.shape[1:3]
    rows, tiles = cells // layers, count - 1
    depth, slots = 8, received.shape[0]
    part, steps = depth * rows, layers // depth

    def load(step, t):
        at = pl.ds(pl.multiple_of(step * part, part), part)
        return pltpu.make_async_copy(
            velocity.at[:, at, pl.ds(t * LANES, LANES)], u0.at[:, t, at], sems.at[step * tiles + t]
        )

    for step in range(steps):
        for t in range(tiles):
            load(step, t).start()
    arrived = Arrived(received, tiles * LANES)
    mask = edge_mask(beside())

    def store(c, t, here, new):
        u1[c, t, here, :] = new * mask if t == tiles else new

    def nothing(c, t, z):
        return 0.0

    @pl.loop(0, steps)
    def _(step):
        at = pl.ds(pl.multiple_of(step * part, part), part)
        chosen = arrived.choose(iota((part, slots), 0) + step * part)
        for t in range(tiles):
            load(step, t).wait()
        for c in range(3):
            main, edge = arrived.force(chosen, c)
            for t in range(tiles):
                u0[c, t, at, :] += main[:, t * LANES : (t + 1) * LANES]
            u0[c, tiles, at, :] = edges[c, at, :] + edge

        @pl.loop(jnp.where(step == 0, 1, 0), jnp.where(step == steps - 1, depth // 2 + 1, depth // 2))
        def _(i):
            sweep_pair(u0, layers, step * depth - 1 + 2 * i, nothing, nothing, store, count)


def last_kernel(layers, u1_in, rim, below_x, above_x, received, fluid_hbm, replies, u1, mid, halo, fluid, pick, sems):
    count, cells = u1.shape[1:3]
    rows, tiles = cells // layers, count - 1
    patch, slots = tiles * LANES, received.shape[0]
    sides = beside()
    mask = edge_mask(sides)

    heads = received[:, 3 * patch :].astype(F32)
    slot = (heads[:, 0:1] * 32.0 + heads[:, 1:2] - 1.0).astype(jnp.int32)
    for first in range(0, cells, 256):
        pick[:, first : first + 256] = (iota((slots, 256), 1) + first == slot).astype(F32).astype(BF16)

    for side, source in enumerate((below_x, above_x)):
        for c in range(3):
            for j in range(2):
                for t in range(count):
                    halo[side, c, j, t] = source[c, j, :, t * LANES : (t + 1) * LANES].astype(F32)
    for side in range(2):
        near, row = 1 - side, (rows - 1) * side
        slope = -transport_rate if side else transport_rate
        for t in range(count):
            scale = sides[side] * mask if t == tiles else sides[side]
            for g in range(0, layers, 8):
                at = slice(g, g + 8)
                after, before = (g + 8) % layers, (g - 8) % layers
                centre = [halo[side, c, near, t, at, :] for c in range(3)]
                weights = mix(centre)
                own = viscosity + slope * rim[side, 0, t, at, :]
                for c in range(3):
                    v = centre[c]
                    plane = halo.at[side, c, near]
                    inner, outer = rim[side, c, t, at, :], halo[side, c, side, t, at, :]
                    east, west = (outer, inner) if side else (inner, outer)
                    north, south = shifted(v, plane[(t + 1) % count, at, :], plane[(t - 1) % count, at, :], 1)
                    up, down = shifted(v, plane[t, after : after + 8, :], plane[t, before : before + 8, :], 0)
                    mid[side, c, t, at, :] = scale * update(
                        centre, weights, c, east, west, north, south, up, down
                    )
                    term = own * v
                    strided = pl.ds(g * rows + row, 8, stride=rows)
                    u1[c, t, strided, :] += term * mask if t == tiles else term

    def store(c, t, here, new):
        fluid[c, here, t * LANES : (t + 1) * LANES] = new

    depth = 8

    def write(step):
        at = pl.ds(pl.multiple_of(step * depth * rows, depth * rows), depth * rows)
        return pltpu.make_async_copy(fluid.at[:, at], fluid_hbm.at[:, at], sems.at[step])

    @pl.loop(0, layers // depth)
    def _(step):
        @pl.loop(0, depth // 2)
        def _(i):
            sweep_pair(
                u1,
                layers,
                step * depth + 2 * i,
                lambda c, t, z: mid[0, c, t, pl.ds(z, 1), :],
                lambda c, t, z: mid[1, c, t, pl.ds(z, 1), :],
                store,
                tiles,
            )

        write(step).start()

    for c in range(3):
        replies[:, c * patch : (c + 1) * patch] = dot(pick[...], fluid[c].astype(BF16)).astype(BF16)
    for step in range(layers // depth):
        write(step).wait()


def gather_kernel(pts, dest, returned, dw_hbm, out, dw, picked, moved, sems):
    entries, slots = dest.shape[0], returned.shape[0]
    blocks, patch, points = dw.shape[0], dw.shape[2], pts.shape[2]
    inter = entries // blocks
    for b in range(blocks):
        pltpu.make_async_copy(dw_hbm.at[b], dw.at[b], sems.at[b]).start()
    to = dest[:, 0:1].astype(jnp.int32)
    pick = (iota((entries, slots), 1) == to).astype(F32).astype(BF16)
    for c in range(3):
        picked[c] = dot(pick, returned[:, c * patch : (c + 1) * patch])
    k_of_lane = lax.rem(iota((points, LANES), 1), inter)

    @pl.loop(0, blocks)
    def _(b):
        at = pl.ds(pl.multiple_of(b * inter, inter), inter)
        parts = [picked[c, at, :] for c in range(3)]
        parts.append(jnp.zeros((LANES - 3 * inter, patch), F32))
        cells = jnp.concatenate(parts, axis=0).astype(BF16)
        pltpu.make_async_copy(dw_hbm.at[b], dw.at[b], sems.at[b]).wait()
        every = lax.dot_general(dw[b], cells, (((1,), (1,)), ((), ())), preferred_element_type=F32)
        folded = jnp.zeros((points, LANES), F32)
        for k in range(inter):
            folded += jnp.where(k_of_lane == k, every[k * points : (k + 1) * points], 0.0)
        turned = jnp.transpose(folded)
        for c in range(3):
            moved[c, pl.ds(b, 1), :] = jnp.sum(turned[c * inter : (c + 1) * inter], axis=0, keepdims=True)

    for c in range(3):
        out[c] = pts[c] + fiber_step * moved[c]


def in_hbm(x):
    return pltpu.with_memory_space_constraint(x, pltpu.HBM)


def params(limit):
    return pltpu.CompilerParams(vmem_limit_bytes=limit << 20)


def cost(flops, size):
    return pl.CostEstimate(flops=flops, bytes_accessed=size << 20, transcendentals=0)


VMEM = pl.BlockSpec(memory_space=pltpu.VMEM)
HBM = pl.BlockSpec(memory_space=pltpu.HBM)


def run_spread(gy_size, slots, pts, stiffness, links, owners, patch_slots, dw):
    blocks, points = links.shape
    inter, patch = owners.shape[1], dw.shape[2]
    entries = blocks * inter
    return pl.pallas_call(
        functools.partial(spread_kernel, gy_size, slots),
        in_specs=[HBM] * 6,
        out_specs=[VMEM, VMEM],
        out_shape=[
            jax.ShapeDtypeStruct((slots, 3 * patch + LANES), BF16),
            jax.ShapeDtypeStruct((entries, LANES), F32),
        ],
        scratch_shapes=[
            pltpu.VMEM(dw.shape, BF16),
            pltpu.VMEM((3, blocks, points), F32),
            pltpu.VMEM((3, entries, patch), F32),
            pltpu.VMEM((3, slots, entries), BF16),
            pltpu.VMEM((3, blocks, points), F32),
            pltpu.SMEM((blocks,), F32),
            pltpu.VMEM((blocks, points), jnp.int32),
            pltpu.VMEM((blocks, inter), jnp.int32),
            pltpu.VMEM((blocks, inter), jnp.int32),
            pltpu.SemaphoreType.DMA((blocks + 5,)),
        ],
        compiler_params=params(24),
        cost_estimate=cost(10**9, 9),
        name="spread",
    )(*[in_hbm(x) for x in (pts, stiffness, links, owners, patch_slots, dw)])


def run_rim(layer_rows, layers, rim_velocity, rim_edge, received):
    patch = rim_velocity.shape[2]
    wide = patch + LANES
    side = (3, 2, layers, wide)
    return pl.pallas_call(
        functools.partial(rim_kernel, layer_rows),
        in_specs=[VMEM] * 3,
        out_specs=[VMEM] * 3,
        out_shape=[
            jax.ShapeDtypeStruct(side, BF16),
            jax.ShapeDtypeStruct(side, BF16),
            jax.ShapeDtypeStruct((2, 3, wide // LANES, layers, LANES), F32),
        ],
        compiler_params=params(24),
        cost_estimate=cost(10**8, 3),
        name="rim",
    )(rim_velocity, rim_edge, received)


def run_first(layers, velocity, edge, received):
    cells, patch = velocity.shape[1:]
    block = (3, patch // LANES + 1, cells, LANES)
    return pl.pallas_call(
        functools.partial(first_kernel, layers),
        in_specs=[HBM, VMEM, VMEM],
        out_specs=VMEM,
        out_shape=jax.ShapeDtypeStruct(block, F32),
        scratch_shapes=[pltpu.VMEM(block, F32), pltpu.SemaphoreType.DMA((layers // 8 * (patch // LANES),))],
        compiler_params=params(24),
        cost_estimate=cost(2 * 10**9, 24),
        name="sweep_first",
    )(in_hbm(velocity), edge, received)


def run_last(layers, u1, rim, below_x, above_x, received):
    count, cells = u1.shape[1:3]
    patch, slots = (count - 1) * LANES, received.shape[0]
    return pl.pallas_call(
        functools.partial(last_kernel, layers),
        in_specs=[VMEM] * 5,
        out_specs=[HBM, VMEM, VMEM],
        out_shape=[
            jax.ShapeDtypeStruct((3, cells, patch), F32),
            jax.ShapeDtypeStruct((slots, 3 * patch), BF16),
            jax.ShapeDtypeStruct(u1.shape, F32),
        ],
        scratch_shapes=[
            pltpu.VMEM((2, 3, count, layers, LANES), F32),
            pltpu.VMEM((2, 3, 2, count, layers, LANES), F32),
            pltpu.VMEM((3, cells, patch), F32),
            pltpu.VMEM((slots, cells), BF16),
            pltpu.SemaphoreType.DMA((layers // 8,)),
        ],
        input_output_aliases={0: 2},
        compiler_params=params(24),
        cost_estimate=cost(2 * 10**9, 16),
        name="sweep_last",
    )(u1, rim, below_x, above_x, received)[:2]


def run_gather(pts, dest, returned, dw):
    blocks, patch = dw.shape[0], dw.shape[2]
    return pl.pallas_call(
        gather_kernel,
        in_specs=[VMEM] * 3 + [HBM],
        out_specs=VMEM,
        out_shape=jax.ShapeDtypeStruct(pts.shape, F32),
        scratch_shapes=[
            pltpu.VMEM(dw.shape, BF16),
            pltpu.VMEM((3, dest.shape[0], patch), F32),
            pltpu.VMEM(pts.shape, F32),
            pltpu.SemaphoreType.DMA((blocks,)),
        ],
        compiler_params=params(24),
        cost_estimate=cost(10**9, 9),
        name="interp",
    )(pts, dest, returned, in_hbm(dw))


def shards(velocity, fiber_points, stiffness, links, delta_weights, owners, patch_slots):
    blocks, inter, points, patch = delta_weights.shape
    layers, rows, columns = velocity.shape[1:]
    gx_size, gy_size = lax.axis_size("gx"), lax.axis_size("gy")
    devices = gx_size * gy_size
    slots, cells = devices * 2, layers * rows
    pts = fiber_points.transpose(1, 0, 2)
    dw = delta_weights.reshape(blocks, inter * points, patch)
    outgoing, dest = run_spread(
        gy_size, slots, pts, stiffness, links, owners.reshape(blocks, inter), patch_slots, dw
    )

    def exchange(rows_out):
        size = rows_out.shape[1]
        return lax.all_to_all(
            rows_out.reshape(devices, 2, size), ("gx", "gy"), split_axis=0, concat_axis=0, tiled=True
        ).reshape(slots, size)

    received = exchange(outgoing)

    ahead = [(i + 1, i) for i in range(gy_size - 1)]
    behind = [(i, i + 1) for i in range(gy_size - 1)]
    flat = velocity.reshape(3, cells, columns)
    first = lax.ppermute(flat[:, :, :2].transpose(0, 2, 1), "gy", ahead)
    last = lax.ppermute(flat[:, :, columns - 2 :].transpose(0, 2, 1), "gy", behind)
    edge = jnp.concatenate(
        [first.transpose(0, 2, 1), jnp.zeros((3, cells, LANES - 4), F32), last.transpose(0, 2, 1)], axis=2
    )
    planes = edge.reshape(3, layers, rows, LANES)
    lines = (0, 1, rows - 2, rows - 1)
    rim_velocity = jnp.stack([velocity[:, :, x, :] for x in lines], axis=1).reshape(3, 4 * layers, patch)
    rim_edge = jnp.stack([planes[:, :, x, :] for x in lines], axis=1).reshape(3, 4 * layers, LANES)
    low_rows, high_rows, rim = run_rim(rows, layers, rim_velocity, rim_edge, received)

    up = [(i, i + 1) for i in range(gx_size - 1)]
    below_x = lax.ppermute(high_rows, "gx", up)
    above_x = lax.ppermute(low_rows, "gx", [(b, a) for a, b in up])
    u1 = run_first(layers, flat, edge, received)
    fluid, replies = run_last(layers, u1, rim, below_x, above_x, received)
    moved = run_gather(pts, dest, exchange(replies), dw)
    return fluid.reshape(3, layers, rows, columns), moved.transpose(1, 0, 2)


def solution(mesh):
    placed = (
        P(None, None, "gx", "gy"),
        P(("gx", "gy"), None, None),
        P(("gx", "gy")),
        P(("gx", "gy"), None),
        P(("gx", "gy"), None, None, None),
        P(("gx", "gy"), None, None),
        P(("gx", "gy"), None),
    )
    return jax.shard_map(
        shards,
        mesh=mesh,
        in_specs=placed,
        out_specs=(P(None, None, "gx", "gy"), P(("gx", "gy"), None, None)),
        check_vma=False,
    )
```

```python
import functools

import jax
import jax.numpy as jnp
from jax import lax
from jax.experimental import pallas as pl
from jax.experimental.pallas import tpu as pltpu
from jax.sharding import PartitionSpec as P

viscosity = 0.1
transport_rate = 0.1
force_step = 0.5
fiber_step = 0.25

F32 = jnp.float32
BF16 = jnp.bfloat16
LANES = 128
BELOW, ABOVE = 2, 10


def dot(a, b):
    return jnp.dot(a, b, preferred_element_type=F32)


def iota(shape, axis):
    return lax.broadcasted_iota(jnp.int32, shape, axis)


def spread_kernel(
    gy_size, slots, pts_hbm, stiff_hbm, links_hbm, owners_hbm, patch_slots_hbm, dw_hbm, out, dest_out,
    dw, force, rows, choose, pts, stiff, links, owners, patch_slots, sems,
):
    blocks, points = links.shape
    inter = owners.shape[1]
    entries = blocks * inter
    patch = rows.shape[2]
    small = [
        (pts_hbm, pts), (stiff_hbm, stiff), (links_hbm, links), (owners_hbm, owners), (patch_slots_hbm, patch_slots)
    ]
    small = [pltpu.make_async_copy(a, b, sems.at[blocks + i]) for i, (a, b) in enumerate(small)]
    for copy in small + [pltpu.make_async_copy(dw_hbm.at[b], dw.at[b], sems.at[b]) for b in range(blocks)]:
        copy.start()
    for copy in small:
        copy.wait()
    partner = lax.rem(iota((blocks, points), 1) + links[...], points)
    for c in range(3):
        own = pts[c]
        force[c] = jnp.take_along_axis(own, partner, axis=1) - own

    pick_block = (iota((entries, blocks), 0) // inter == iota((entries, blocks), 1)).astype(F32).astype(BF16)
    pick_k = lax.rem(iota((entries, inter), 0), inter) == iota((entries, inter), 1)

    def as_column(table):
        spread_rows = dot(pick_block, table.astype(F32).astype(BF16))
        return jnp.sum(jnp.where(pick_k, spread_rows, 0.0), axis=1, keepdims=True)

    owner = as_column(owners[...])
    code = patch_slots[...] + 1
    high, low = as_column(code // 32), as_column(lax.rem(code, 32))
    owner_wide = jnp.broadcast_to(owner, (entries, LANES))
    owner_row = jnp.transpose(
        jnp.concatenate([owner_wide, jnp.zeros((LANES - entries, LANES), F32)], axis=0)
    )[:entries, :entries]
    same = (owner_wide[:, :entries] == owner_row) & (iota((entries, entries), 1) < iota((entries, entries), 0))
    rank = jnp.sum(jnp.where(same, 1.0, 0.0), axis=1, keepdims=True)
    dest_wide = jnp.broadcast_to(owner * 2.0 + rank, (entries, LANES))
    dest_out[...] = dest_wide
    padded = jnp.concatenate([dest_wide, jnp.full((LANES - entries, LANES), -8.0, F32)], axis=0)
    dest_row = jnp.transpose(padded)[0:1, :entries].astype(jnp.int32)
    position = lax.rem(dest_row // 2, gy_size)
    slot = iota((slots, entries), 0)
    choose[0] = (slot == dest_row).astype(F32).astype(BF16)
    choose[1] = ((slot == dest_row + 2) & (position < gy_size - 1)).astype(F32).astype(BF16)
    choose[2] = ((slot == dest_row - 2) & (position > 0)).astype(F32).astype(BF16)
    lane = iota((entries, LANES), 1)

    def digits(at):
        return jnp.where(lane == at, high, 0.0) + jnp.where(lane == at + 1, low, 0.0)

    own_head, above_head, below_head = digits(0), digits(BELOW), digits(ABOVE)
    group = iota((inter, inter * points), 0)
    column = iota((inter, inter * points), 1) // points

    @pl.loop(0, blocks)
    def _(b):
        stiffness = stiff[b]
        parts = []
        for c in range(3):
            row = (stiffness * force[c, pl.ds(b, 1), :]).astype(BF16).astype(F32)
            wide = jnp.concatenate([jnp.broadcast_to(row, (inter, points))] * inter, axis=1)
            parts.append(jnp.where(group == column, wide, 0.0))
        parts.append(jnp.zeros_like(parts[0]))
        pltpu.make_async_copy(dw_hbm.at[b], dw.at[b], sems.at[b]).wait()
        spread = dot(jnp.concatenate(parts, axis=0).astype(BF16), dw[b])
        for c in range(3):
            rows[c, pl.ds(pl.multiple_of(b * inter, inter), inter), :] = spread[c * inter : (c + 1) * inter]

    for c in range(3):
        tail = pltpu.roll(rows[c, :, patch - LANES :], BELOW + 4 + 2 * c, axis=1)
        at = BELOW + 2 + 2 * c
        above_head += jnp.where((lane == at) | (lane == at + 1), tail, 0.0)
        at = ABOVE + 2 + 2 * c
        start = pltpu.roll(rows[c, :, :LANES], at, axis=1)
        below_head += jnp.where((lane == at) | (lane == at + 1), start, 0.0)
        out[:, c * patch : (c + 1) * patch] = dot(choose[0], rows[c].astype(BF16)).astype(BF16)
    head = dot(choose[0], own_head.astype(BF16))
    head += dot(choose[1], above_head.astype(BF16))
    head += dot(choose[2], below_head.astype(BF16))
    out[:, 3 * patch :] = head.astype(BF16)


def edge_kernel(velocity, first, last, start, end, sems):
    patch = velocity.shape[2]
    loads = []
    for c in range(3):
        for i, (to, lane) in enumerate(((start, 0), (end, patch - LANES))):
            loads.append(pltpu.make_async_copy(velocity.at[c, :, pl.ds(lane, LANES)], to.at[c], sems.at[2 * c + i]))
    for load in loads:
        load.start()
    row, lane = iota((16, LANES), 0), iota((16, LANES), 1)
    across = (((1,), (1,)), ((), ()))
    sums = [0.0, 0.0]
    for c in range(3):
        for i, (tile, at) in enumerate(((start, 0), (end, LANES - 2))):
            loads[2 * c + i].wait()
            pick = ((row - 2 * c == lane - at) & (lane >= at) & (lane < at + 2)).astype(F32).astype(BF16)
            sums[i] += lax.dot_general(pick, tile[c].astype(BF16), across, preferred_element_type=F32)
    first[...] = sums[0][:8]
    last[...] = sums[1][:8]


def line_kernel(velocity, out, lines, sems):
    layers, rows, patch = velocity.shape[1:]
    loads = []
    for i, x in enumerate((0, rows - 8)):
        for t in range(patch // LANES):
            part = velocity.at[:, :, pl.ds(x, 8), pl.ds(t * LANES, LANES)]
            loads.append(pltpu.make_async_copy(part, lines.at[i, t], sems.at[len(loads)]))
    for load in loads:
        load.start()
    for i in range(2):
        for t in range(patch // LANES):
            loads[i * (patch // LANES) + t].wait()
            for c in range(3):
                for j in range(2):
                    at = (2 * i + j) * layers
                    out[c, at : at + layers, t * LANES : (t + 1) * LANES] = lines[i, t, c, :, 6 * i + j, :]


class Arrived:
    def __init__(self, received, patch):
        self.received, self.patch = received, patch
        slots = received.shape[0]
        head = received[:, 3 * patch :].astype(F32)
        head_t = jnp.transpose(head)
        lane = iota((slots, LANES), 1)
        self.tails, self.starts = [], []
        for c in range(3):
            tail = pltpu.roll(head, LANES - 4 - BELOW - 2 * c, axis=1)
            self.tails.append(jnp.where(lane >= LANES - 2, tail, 0.0).astype(BF16))
            start = pltpu.roll(head, LANES - (ABOVE + 2 + 2 * c), axis=1)
            self.starts.append(jnp.where(lane < 2, start, 0.0).astype(BF16))
        self.slots = [
            (head_t[at : at + 1] * 32.0 + head_t[at + 1 : at + 2] - 1.0).astype(jnp.int32) for at in (0, BELOW, ABOVE)
        ]

    def choose(self, row):
        return [(row == slot).astype(F32).astype(BF16) for slot in self.slots]

    def force(self, chosen, c):
        here, below, above = chosen
        main = dot(here, self.received[:, c * self.patch : (c + 1) * self.patch])
        return force_step * main, force_step * (dot(below, self.tails[c]) + dot(above, self.starts[c]))


def rim_kernel(layer_rows, velocity, ahead, behind, received, low_rows, high_rows, rim, edges):
    layers, patch = low_rows.shape[2], velocity.shape[2]
    slots, cells = received.shape[0], ahead.shape[1]

    turned = jnp.transpose(jnp.concatenate([ahead[...], behind[...], jnp.zeros((LANES - 16, cells), F32)], axis=0))
    turned = turned.astype(BF16)
    row, lane = iota((LANES, LANES), 0), iota((LANES, LANES), 1)
    for c in range(3):
        put = ((lane < 2) & (row == lane + 2 * c)) | ((lane >= LANES - 2) & (row == lane - (LANES - 2) + 8 + 2 * c))
        edges[c] = dot(turned, put.astype(F32).astype(BF16))

    arrived = Arrived(received, patch)
    row = iota((4 * layers, slots), 0)
    line, z = row // layers, lax.rem(row, layers)
    chosen = arrived.choose(z * layer_rows + jnp.where(line < 2, line, layer_rows - 4 + line))
    for c in range(3):
        main, edge = arrived.force(chosen, c)
        main = velocity[c] + main
        for j in range(4):
            at = slice(j * layers, (j + 1) * layers)
            x = j if j < 2 else layer_rows - 4 + j
            side = edges[c, pl.ds(x, layers, stride=layer_rows), :] + edge[at]
            to = low_rows if j < 2 else high_rows
            to[c, j % 2, :, :patch] = main[at].astype(BF16)
            to[c, j % 2, :, patch:] = side.astype(BF16)
            if j in (0, 3):
                for t in range(patch // LANES):
                    rim[j // 3, c, t] = main[at, t * LANES : (t + 1) * LANES]
                rim[j // 3, c, patch // LANES] = side


def update(centre, weights, c, east, west, north, south, up, down):
    (px, mx), (py, my), (pz, mz) = weights
    keep = 1.0 - 6.0 * viscosity
    return keep * centre[c] + px * east + mx * west + py * north + my * south + pz * up + mz * down


def mix(centre):
    return [(viscosity - transport_rate * v, viscosity + transport_rate * v) for v in centre]


def beside():
    flags = []
    for axis in ("gx", "gy"):
        at, size = lax.axis_index(axis), lax.axis_size(axis)
        flags += [jnp.where(at > 0, 1.0, 0.0).astype(F32), jnp.where(at < size - 1, 1.0, 0.0).astype(F32)]
    return flags


def edge_mask(sides):
    lane = iota((8, LANES), 1)
    return jnp.where(lane == 0, sides[3], 0.0) + jnp.where(lane == LANES - 1, sides[2], 0.0)


def rows_at(z, x, rows):
    return pl.ds(pl.multiple_of(z * rows + x, 8), 8)


def shifted(v, ahead, behind, axis):
    size = v.shape[axis]
    at = iota(v.shape, axis)
    return (
        pltpu.roll(jnp.where(at == 0, ahead, v), size - 1, axis=axis),
        pltpu.roll(jnp.where(at == size - 1, behind, v), 1, axis=axis),
    )


def sweep_pair(source, layers, z, low_row, high_row, store, tiles):
    count, rows = source.shape[1], source.shape[2] // layers
    z1 = lax.rem(z + 1, layers)
    for z, up, down in ((z, z1, lax.rem(z + layers - 1, layers)), (z1, lax.rem(z + 2, layers), z)):
        for x in range(0, rows, 8):
            for t in range(tiles):
                here = rows_at(z, x, rows)
                centre = [source[c, t, here, :] for c in range(3)]
                weights = mix(centre)
                for c in range(3):
                    v = centre[c]
                    ahead = source[c, t, rows_at(z, x + 8, rows), :] if x + 8 < rows else high_row(c, t, z)
                    behind = source[c, t, rows_at(z, x - 8, rows), :] if x > 0 else low_row(c, t, z)
                    east, west = shifted(v, ahead, behind, 0)
                    north, south = shifted(v, source[c, (t + 1) % count, here, :], source[c, (t - 1) % count, here, :], 1)
                    above, below = source[c, t, rows_at(up, x, rows), :], source[c, t, rows_at(down, x, rows), :]
                    store(c, t, here, update(centre, weights, c, east, west, north, south, above, below))


def first_kernel(layers, velocity, edges, received, u1, u0, sems):
    count, cells = u0.shape[1:3]
    rows, tiles = cells // layers, count - 1
    depth, slots = 8, received.shape[0]
    part, steps = depth * rows, layers // depth

    def load(step, t):
        at = pl.ds(pl.multiple_of(step * part, part), part)
        return pltpu.make_async_copy(
            velocity.at[:, at, pl.ds(t * LANES, LANES)], u0.at[:, t, at], sems.at[step * tiles + t]
        )

    for step in range(steps):
        for t in range(tiles):
            load(step, t).start()
    arrived = Arrived(received, tiles * LANES)
    mask = edge_mask(beside())

    def store(c, t, here, new):
        u1[c, t, here, :] = new * mask if t == tiles else new

    def nothing(c, t, z):
        return 0.0

    @pl.loop(0, steps)
    def _(step):
        at = pl.ds(pl.multiple_of(step * part, part), part)
        chosen = arrived.choose(iota((part, slots), 0) + step * part)
        for t in range(tiles):
            load(step, t).wait()
        for c in range(3):
            main, edge = arrived.force(chosen, c)
            for t in range(tiles):
                u0[c, t, at, :] += main[:, t * LANES : (t + 1) * LANES]
            u0[c, tiles, at, :] = edges[c, at, :] + edge

        @pl.loop(jnp.where(step == 0, 1, 0), jnp.where(step == steps - 1, depth // 2 + 1, depth // 2))
        def _(i):
            sweep_pair(u0, layers, step * depth - 1 + 2 * i, nothing, nothing, store, count)


def last_kernel(layers, u1_in, rim, below_x, above_x, received, fluid_hbm, replies, u1, mid, halo, fluid, pick, sems):
    count, cells = u1.shape[1:3]
    rows, tiles = cells // layers, count - 1
    patch, slots = tiles * LANES, received.shape[0]
    sides = beside()
    mask = edge_mask(sides)

    heads = received[:, 3 * patch :].astype(F32)
    slot = (heads[:, 0:1] * 32.0 + heads[:, 1:2] - 1.0).astype(jnp.int32)
    for first in range(0, cells, 256):
        pick[:, first : first + 256] = (iota((slots, 256), 1) + first == slot).astype(F32).astype(BF16)

    for side, source in enumerate((below_x, above_x)):
        for c in range(3):
            for j in range(2):
                for t in range(count):
                    halo[side, c, j, t] = source[c, j, :, t * LANES : (t + 1) * LANES].astype(F32)
    for side in range(2):
        near, row = 1 - side, (rows - 1) * side
        slope = -transport_rate if side else transport_rate
        for t in range(count):
            scale = sides[side] * mask if t == tiles else sides[side]
            for g in range(0, layers, 8):
                at = slice(g, g + 8)
                after, before = (g + 8) % layers, (g - 8) % layers
                centre = [halo[side, c, near, t, at, :] for c in range(3)]
                weights = mix(centre)
                own = viscosity + slope * rim[side, 0, t, at, :]
                for c in range(3):
                    v = centre[c]
                    plane = halo.at[side, c, near]
                    inner, outer = rim[side, c, t, at, :], halo[side, c, side, t, at, :]
                    east, west = (outer, inner) if side else (inner, outer)
                    north, south = shifted(v, plane[(t + 1) % count, at, :], plane[(t - 1) % count, at, :], 1)
                    up, down = shifted(v, plane[t, after : after + 8, :], plane[t, before : before + 8, :], 0)
                    mid[side, c, t, at, :] = scale * update(
                        centre, weights, c, east, west, north, south, up, down
                    )
                    term = own * v
                    strided = pl.ds(g * rows + row, 8, stride=rows)
                    u1[c, t, strided, :] += term * mask if t == tiles else term

    def store(c, t, here, new):
        fluid[c, here, t * LANES : (t + 1) * LANES] = new

    depth = 8

    def write(step):
        at = pl.ds(pl.multiple_of(step * depth * rows, depth * rows), depth * rows)
        return pltpu.make_async_copy(fluid.at[:, at], fluid_hbm.at[:, at], sems.at[step])

    @pl.loop(0, layers // depth)
    def _(step):
        @pl.loop(0, depth // 2)
        def _(i):
            sweep_pair(
                u1,
                layers,
                step * depth + 2 * i,
                lambda c, t, z: mid[0, c, t, pl.ds(z, 1), :],
                lambda c, t, z: mid[1, c, t, pl.ds(z, 1), :],
                store,
                tiles,
            )

        write(step).start()

    for c in range(3):
        replies[:, c * patch : (c + 1) * patch] = dot(pick[...], fluid[c].astype(BF16)).astype(BF16)
    for step in range(layers // depth):
        write(step).wait()


def gather_kernel(pts, dest, returned, dw_hbm, out, dw, picked, moved, sems):
    entries, slots = dest.shape[0], returned.shape[0]
    blocks, patch, points = dw.shape[0], dw.shape[2], pts.shape[2]
    inter = entries // blocks
    for b in range(blocks):
        pltpu.make_async_copy(dw_hbm.at[b], dw.at[b], sems.at[b]).start()
    to = dest[:, 0:1].astype(jnp.int32)
    pick = (iota((entries, slots), 1) == to).astype(F32).astype(BF16)
    for c in range(3):
        picked[c] = dot(pick, returned[:, c * patch : (c + 1) * patch])
    k_of_lane = lax.rem(iota((points, LANES), 1), inter)

    @pl.loop(0, blocks)
    def _(b):
        at = pl.ds(pl.multiple_of(b * inter, inter), inter)
        parts = [picked[c, at, :] for c in range(3)]
        parts.append(jnp.zeros((LANES - 3 * inter, patch), F32))
        cells = jnp.concatenate(parts, axis=0).astype(BF16)
        pltpu.make_async_copy(dw_hbm.at[b], dw.at[b], sems.at[b]).wait()
        every = lax.dot_general(dw[b], cells, (((1,), (1,)), ((), ())), preferred_element_type=F32)
        folded = jnp.zeros((points, LANES), F32)
        for k in range(inter):
            folded += jnp.where(k_of_lane == k, every[k * points : (k + 1) * points], 0.0)
        turned = jnp.transpose(folded)
        for c in range(3):
            moved[c, pl.ds(b, 1), :] = jnp.sum(turned[c * inter : (c + 1) * inter], axis=0, keepdims=True)

    for c in range(3):
        out[c] = pts[c] + fiber_step * moved[c]


def in_hbm(x):
    return pltpu.with_memory_space_constraint(x, pltpu.HBM)


def params(limit):
    return pltpu.CompilerParams(vmem_limit_bytes=limit << 20)


def cost(flops, size):
    return pl.CostEstimate(flops=flops, bytes_accessed=size << 20, transcendentals=0)


VMEM = pl.BlockSpec(memory_space=pltpu.VMEM)
HBM = pl.BlockSpec(memory_space=pltpu.HBM)


def run_spread(gy_size, slots, pts, stiffness, links, owners, patch_slots, dw):
    blocks, points = links.shape
    inter, patch = owners.shape[1], dw.shape[2]
    entries = blocks * inter
    return pl.pallas_call(
        functools.partial(spread_kernel, gy_size, slots),
        in_specs=[HBM] * 6,
        out_specs=[VMEM, VMEM],
        out_shape=[
            jax.ShapeDtypeStruct((slots, 3 * patch + LANES), BF16),
            jax.ShapeDtypeStruct((entries, LANES), F32),
        ],
        scratch_shapes=[
            pltpu.VMEM(dw.shape, BF16),
            pltpu.VMEM((3, blocks, points), F32),
            pltpu.VMEM((3, entries, patch), F32),
            pltpu.VMEM((3, slots, entries), BF16),
            pltpu.VMEM((3, blocks, points), F32),
            pltpu.SMEM((blocks,), F32),
            pltpu.VMEM((blocks, points), jnp.int32),
            pltpu.VMEM((blocks, inter), jnp.int32),
            pltpu.VMEM((blocks, inter), jnp.int32),
            pltpu.SemaphoreType.DMA((blocks + 5,)),
        ],
        compiler_params=params(24),
        cost_estimate=cost(10**9, 9),
        name="spread",
    )(*[in_hbm(x) for x in (pts, stiffness, links, owners, patch_slots, dw)])


def run_edges(velocity):
    cells = velocity.shape[1]
    return pl.pallas_call(
        edge_kernel,
        in_specs=[HBM],
        out_specs=[VMEM, VMEM],
        out_shape=[jax.ShapeDtypeStruct((8, cells), F32)] * 2,
        scratch_shapes=[pltpu.VMEM((3, cells, LANES), F32)] * 2 + [pltpu.SemaphoreType.DMA((6,))],
        compiler_params=params(24),
        cost_estimate=cost(10**8, 3),
        name="edges",
    )(in_hbm(velocity))


def run_lines(velocity):
    layers, patch = velocity.shape[1], velocity.shape[3]
    tiles = patch // LANES
    return pl.pallas_call(
        line_kernel,
        in_specs=[HBM],
        out_specs=VMEM,
        out_shape=jax.ShapeDtypeStruct((3, 4 * layers, patch), F32),
        scratch_shapes=[pltpu.VMEM((2, tiles, 3, layers, 8, LANES), F32), pltpu.SemaphoreType.DMA((2 * tiles,))],
        compiler_params=params(24),
        cost_estimate=cost(10**8, 3),
        name="lines",
    )(in_hbm(velocity))


def run_rim(layer_rows, layers, rim_velocity, ahead, behind, received):
    patch, cells = rim_velocity.shape[2], ahead.shape[1]
    wide = patch + LANES
    side = (3, 2, layers, wide)
    return pl.pallas_call(
        functools.partial(rim_kernel, layer_rows),
        in_specs=[VMEM] * 4,
        out_specs=[VMEM] * 4,
        out_shape=[
            jax.ShapeDtypeStruct(side, BF16),
            jax.ShapeDtypeStruct(side, BF16),
            jax.ShapeDtypeStruct((2, 3, wide // LANES, layers, LANES), F32),
            jax.ShapeDtypeStruct((3, cells, LANES), F32),
        ],
        compiler_params=params(24),
        cost_estimate=cost(10**8, 3),
        name="rim",
    )(rim_velocity, ahead, behind, received)


def run_first(layers, velocity, edge, received):
    cells, patch = velocity.shape[1:]
    block = (3, patch // LANES + 1, cells, LANES)
    return pl.pallas_call(
        functools.partial(first_kernel, layers),
        in_specs=[HBM, VMEM, VMEM],
        out_specs=VMEM,
        out_shape=jax.ShapeDtypeStruct(block, F32),
        scratch_shapes=[pltpu.VMEM(block, F32), pltpu.SemaphoreType.DMA((layers // 8 * (patch // LANES),))],
        compiler_params=params(24),
        cost_estimate=cost(2 * 10**9, 24),
        name="sweep_first",
    )(in_hbm(velocity), edge, received)


def run_last(layers, u1, rim, below_x, above_x, received):
    count, cells = u1.shape[1:3]
    patch, slots = (count - 1) * LANES, received.shape[0]
    return pl.pallas_call(
        functools.partial(last_kernel, layers),
        in_specs=[VMEM] * 5,
        out_specs=[HBM, VMEM, VMEM],
        out_shape=[
            jax.ShapeDtypeStruct((3, cells, patch), F32),
            jax.ShapeDtypeStruct((slots, 3 * patch), BF16),
            jax.ShapeDtypeStruct(u1.shape, F32),
        ],
        scratch_shapes=[
            pltpu.VMEM((2, 3, count, layers, LANES), F32),
            pltpu.VMEM((2, 3, 2, count, layers, LANES), F32),
            pltpu.VMEM((3, cells, patch), F32),
            pltpu.VMEM((slots, cells), BF16),
            pltpu.SemaphoreType.DMA((layers // 8,)),
        ],
        input_output_aliases={0: 2},
        compiler_params=params(24),
        cost_estimate=cost(2 * 10**9, 16),
        name="sweep_last",
    )(u1, rim, below_x, above_x, received)[:2]


def run_gather(pts, dest, returned, dw):
    blocks, patch = dw.shape[0], dw.shape[2]
    return pl.pallas_call(
        gather_kernel,
        in_specs=[VMEM] * 3 + [HBM],
        out_specs=VMEM,
        out_shape=jax.ShapeDtypeStruct(pts.shape, F32),
        scratch_shapes=[
            pltpu.VMEM(dw.shape, BF16),
            pltpu.VMEM((3, dest.shape[0], patch), F32),
            pltpu.VMEM(pts.shape, F32),
            pltpu.SemaphoreType.DMA((blocks,)),
        ],
        compiler_params=params(24),
        cost_estimate=cost(10**9, 9),
        name="interp",
    )(pts, dest, returned, in_hbm(dw))


def shards(velocity, fiber_points, stiffness, links, delta_weights, owners, patch_slots):
    blocks, inter, points, patch = delta_weights.shape
    layers, rows, columns = velocity.shape[1:]
    gx_size, gy_size = lax.axis_size("gx"), lax.axis_size("gy")
    devices = gx_size * gy_size
    slots, cells = devices * 2, layers * rows
    pts = fiber_points.transpose(1, 0, 2)
    dw = delta_weights.reshape(blocks, inter * points, patch)
    outgoing, dest = run_spread(
        gy_size, slots, pts, stiffness, links, owners.reshape(blocks, inter), patch_slots, dw
    )

    def exchange(rows_out):
        size = rows_out.shape[1]
        return lax.all_to_all(
            rows_out.reshape(devices, 2, size), ("gx", "gy"), split_axis=0, concat_axis=0, tiled=True
        ).reshape(slots, size)

    received = exchange(outgoing)

    flat = velocity.reshape(3, cells, columns)
    first, last = run_edges(flat)
    ahead = lax.ppermute(first, "gy", [(i + 1, i) for i in range(gy_size - 1)])
    behind = lax.ppermute(last, "gy", [(i, i + 1) for i in range(gy_size - 1)])
    low_rows, high_rows, rim, edge = run_rim(rows, layers, run_lines(velocity), ahead, behind, received)

    up = [(i, i + 1) for i in range(gx_size - 1)]
    below_x = lax.ppermute(high_rows, "gx", up)
    above_x = lax.ppermute(low_rows, "gx", [(b, a) for a, b in up])
    u1 = run_first(layers, flat, edge, received)
    fluid, replies = run_last(layers, u1, rim, below_x, above_x, received)
    moved = run_gather(pts, dest, exchange(replies), dw)
    return fluid.reshape(3, layers, rows, columns), moved.transpose(1, 0, 2)


def solution(mesh):
    placed = (
        P(None, None, "gx", "gy"),
        P(("gx", "gy"), None, None),
        P(("gx", "gy")),
        P(("gx", "gy"), None),
        P(("gx", "gy"), None, None, None),
        P(("gx", "gy"), None, None),
        P(("gx", "gy"), None),
    )
    return jax.shard_map(
        shards,
        mesh=mesh,
        in_specs=placed,
        out_specs=(P(None, None, "gx", "gy"), P(("gx", "gy"), None, None)),
        check_vma=False,
    )
```

```python
import functools

import jax
import jax.numpy as jnp
from jax import lax
from jax.experimental import pallas as pl
from jax.experimental.pallas import tpu as pltpu
from jax.sharding import PartitionSpec as P

viscosity = 0.1
transport_rate = 0.1
force_step = 0.5
fiber_step = 0.25

F32 = jnp.float32
BF16 = jnp.bfloat16
LANES = 128
BELOW, ABOVE = 2, 10
NEAR = 1


def dot(a, b):
    return jnp.dot(a, b, preferred_element_type=F32)


def iota(shape, axis):
    return lax.broadcasted_iota(jnp.int32, shape, axis)


def spread_kernel(
    gy_size, slots, pts_hbm, stiff_hbm, links_hbm, owners_hbm, patch_slots_hbm, dw_hbm, out, dest_out,
    dw, force, rows, choose, pts, stiff, links, owners, patch_slots, sems,
):
    blocks, points = links.shape
    inter = owners.shape[1]
    entries = blocks * inter
    patch = rows.shape[2]
    small = [
        (pts_hbm, pts), (stiff_hbm, stiff), (links_hbm, links), (owners_hbm, owners), (patch_slots_hbm, patch_slots)
    ]
    small = [pltpu.make_async_copy(a, b, sems.at[blocks + i]) for i, (a, b) in enumerate(small)]
    for copy in small + [pltpu.make_async_copy(dw_hbm.at[b], dw.at[b], sems.at[b]) for b in range(blocks)]:
        copy.start()
    for copy in small:
        copy.wait()
    partner = lax.rem(iota((blocks, points), 1) + links[...], points)
    for c in range(3):
        own = pts[c]
        force[c] = jnp.take_along_axis(own, partner, axis=1) - own

    pick_block = (iota((entries, blocks), 0) // inter == iota((entries, blocks), 1)).astype(F32).astype(BF16)
    pick_k = lax.rem(iota((entries, inter), 0), inter) == iota((entries, inter), 1)

    def as_column(table):
        spread_rows = dot(pick_block, table.astype(F32).astype(BF16))
        return jnp.sum(jnp.where(pick_k, spread_rows, 0.0), axis=1, keepdims=True)

    owner = as_column(owners[...])
    code = patch_slots[...] + 1
    high, low = as_column(code // 32), as_column(lax.rem(code, 32))
    owner_wide = jnp.broadcast_to(owner, (entries, LANES))
    owner_row = jnp.transpose(
        jnp.concatenate([owner_wide, jnp.zeros((LANES - entries, LANES), F32)], axis=0)
    )[:entries, :entries]
    same = (owner_wide[:, :entries] == owner_row) & (iota((entries, entries), 1) < iota((entries, entries), 0))
    rank = jnp.sum(jnp.where(same, 1.0, 0.0), axis=1, keepdims=True)
    dest_wide = jnp.broadcast_to(owner * 2.0 + rank, (entries, LANES))
    dest_out[...] = dest_wide
    padded = jnp.concatenate([dest_wide, jnp.full((LANES - entries, LANES), -8.0, F32)], axis=0)
    dest_row = jnp.transpose(padded)[0:1, :entries].astype(jnp.int32)
    position = lax.rem(dest_row // 2, gy_size)
    slot = iota((slots, entries), 0)
    choose[0] = (slot == dest_row).astype(F32).astype(BF16)
    choose[1] = ((slot == dest_row + 2) & (position < gy_size - 1)).astype(F32).astype(BF16)
    choose[2] = ((slot == dest_row - 2) & (position > 0)).astype(F32).astype(BF16)
    lane = iota((entries, LANES), 1)

    def digits(at):
        return jnp.where(lane == at, high, 0.0) + jnp.where(lane == at + 1, low, 0.0)

    own_head, above_head, below_head = digits(0), digits(BELOW), digits(ABOVE)
    group = iota((inter, inter * points), 0)
    column = iota((inter, inter * points), 1) // points

    @pl.loop(0, blocks)
    def _(b):
        stiffness = stiff[b]
        parts = []
        for c in range(3):
            row = (stiffness * force[c, pl.ds(b, 1), :]).astype(BF16).astype(F32)
            wide = jnp.concatenate([jnp.broadcast_to(row, (inter, points))] * inter, axis=1)
            parts.append(jnp.where(group == column, wide, 0.0))
        parts.append(jnp.zeros_like(parts[0]))
        pltpu.make_async_copy(dw_hbm.at[b], dw.at[b], sems.at[b]).wait()
        spread = dot(jnp.concatenate(parts, axis=0).astype(BF16), dw[b])
        for c in range(3):
            rows[c, pl.ds(pl.multiple_of(b * inter, inter), inter), :] = spread[c * inter : (c + 1) * inter]

    for c in range(3):
        tail = pltpu.roll(rows[c, :, patch - LANES :], BELOW + 4 + 2 * c, axis=1)
        at = BELOW + 2 + 2 * c
        above_head += jnp.where((lane == at) | (lane == at + 1), tail, 0.0)
        at = ABOVE + 2 + 2 * c
        start = pltpu.roll(rows[c, :, :LANES], at, axis=1)
        below_head += jnp.where((lane == at) | (lane == at + 1), start, 0.0)
        out[:, c * patch : (c + 1) * patch] = dot(choose[0], rows[c].astype(BF16)).astype(BF16)
    head = dot(choose[0], own_head.astype(BF16))
    head += dot(choose[1], above_head.astype(BF16))
    head += dot(choose[2], below_head.astype(BF16))
    out[:, 3 * patch :] = head.astype(BF16)


def edge_kernel(velocity, first, last, start, end, sems):
    patch = velocity.shape[2]
    loads = []
    for c in range(3):
        for i, (to, lane) in enumerate(((start, 0), (end, patch - LANES))):
            loads.append(pltpu.make_async_copy(velocity.at[c, :, pl.ds(lane, LANES)], to.at[c], sems.at[2 * c + i]))
    for load in loads:
        load.start()
    row, lane = iota((16, LANES), 0), iota((16, LANES), 1)
    across = (((1,), (1,)), ((), ()))
    sums = [0.0, 0.0]
    for c in range(3):
        for i, (tile, at) in enumerate(((start, 0), (end, LANES - 2))):
            loads[2 * c + i].wait()
            pick = ((row - 2 * c == lane - at) & (lane >= at) & (lane < at + 2)).astype(F32).astype(BF16)
            sums[i] += lax.dot_general(pick, tile[c].astype(BF16), across, preferred_element_type=F32)
    first[...] = sums[0][:8]
    last[...] = sums[1][:8]


def line_kernel(velocity, out, lines, sems):
    layers, rows, patch = velocity.shape[1:]
    loads = []
    for i, x in enumerate((0, rows - 8)):
        for t in range(patch // LANES):
            part = velocity.at[:, :, pl.ds(x, 8), pl.ds(t * LANES, LANES)]
            loads.append(pltpu.make_async_copy(part, lines.at[i, t], sems.at[len(loads)]))
    for load in loads:
        load.start()
    for i in range(2):
        for t in range(patch // LANES):
            loads[i * (patch // LANES) + t].wait()
            for c in range(3):
                for j in range(2):
                    at = (2 * i + j) * layers
                    out[c, at : at + layers, t * LANES : (t + 1) * LANES] = lines[i, t, c, :, 6 * i + j, :]


class Arrived:
    def __init__(self, received, patch):
        self.received, self.patch = received, patch
        slots = received.shape[0]
        head = received[:, 3 * patch :].astype(F32)
        head_t = jnp.transpose(head)
        lane = iota((slots, LANES), 1)
        self.tails, self.starts = [], []
        for c in range(3):
            tail = pltpu.roll(head, LANES - 4 - BELOW - 2 * c, axis=1)
            self.tails.append(jnp.where(lane >= LANES - 2, tail, 0.0).astype(BF16))
            start = pltpu.roll(head, LANES - (ABOVE + 2 + 2 * c), axis=1)
            self.starts.append(jnp.where(lane < 2, start, 0.0).astype(BF16))
        self.slots = [
            (head_t[at : at + 1] * 32.0 + head_t[at + 1 : at + 2] - 1.0).astype(jnp.int32) for at in (0, BELOW, ABOVE)
        ]

    def choose(self, row):
        return [(row == slot).astype(F32).astype(BF16) for slot in self.slots]

    def force(self, chosen, c):
        here, below, above = chosen
        main = dot(here, self.received[:, c * self.patch : (c + 1) * self.patch])
        return force_step * main, force_step * (dot(below, self.tails[c]) + dot(above, self.starts[c]))


def rim_kernel(layer_rows, velocity, ahead, behind, received, low_rows, high_rows, rim, edges):
    layers, patch = low_rows.shape[2], velocity.shape[2]
    slots, cells = received.shape[0], ahead.shape[1]

    sides = beside()
    from_ahead = jnp.where(sides[3] > 0.0, ahead[...], 0.0)
    from_behind = jnp.where(sides[2] > 0.0, behind[...], 0.0)
    turned = jnp.transpose(jnp.concatenate([from_ahead, from_behind, jnp.zeros((LANES - 16, cells), F32)], axis=0))
    turned = turned.astype(BF16)
    row, lane = iota((LANES, LANES), 0), iota((LANES, LANES), 1)
    for c in range(3):
        put = ((lane < 2) & (row == lane + 2 * c)) | ((lane >= LANES - 2) & (row == lane - (LANES - 2) + 8 + 2 * c))
        edges[c] = dot(turned, put.astype(F32).astype(BF16))

    arrived = Arrived(received, patch)
    row = iota((4 * layers, slots), 0)
    line, z = row // layers, lax.rem(row, layers)
    chosen = arrived.choose(z * layer_rows + jnp.where(line < 2, line, layer_rows - 4 + line))
    for c in range(3):
        main, edge = arrived.force(chosen, c)
        main = velocity[c] + main
        for j in range(4):
            at = slice(j * layers, (j + 1) * layers)
            x = j if j < 2 else layer_rows - 4 + j
            side = edges[c, pl.ds(x, layers, stride=layer_rows), :] + edge[at]
            to = low_rows if j < 2 else high_rows
            to[c, j % 2, :, :patch] = main[at].astype(BF16)
            to[c, j % 2, :, patch:] = side.astype(BF16)
            if j in (0, 3):
                for t in range(patch // LANES):
                    rim[j // 3, c, t] = main[at, t * LANES : (t + 1) * LANES]
                rim[j // 3, c, patch // LANES] = side


def update(centre, weights, c, east, west, north, south, up, down):
    (px, mx), (py, my), (pz, mz) = weights
    keep = 1.0 - 6.0 * viscosity
    return keep * centre[c] + px * east + mx * west + py * north + my * south + pz * up + mz * down


def mix(centre):
    return [(viscosity - transport_rate * v, viscosity + transport_rate * v) for v in centre]


def beside():
    flags = []
    for axis in ("gx", "gy"):
        at, size = lax.axis_index(axis), lax.axis_size(axis)
        flags += [jnp.where(at > 0, 1.0, 0.0).astype(F32), jnp.where(at < size - 1, 1.0, 0.0).astype(F32)]
    return flags


def edge_mask(sides):
    lane = iota((8, LANES), 1)
    return jnp.where(lane == 0, sides[3], 0.0) + jnp.where(lane == LANES - 1, sides[2], 0.0)


def rows_at(z, x, rows):
    return pl.ds(pl.multiple_of(z * rows + x, 8), 8)


def shifted(v, ahead, behind, axis):
    size = v.shape[axis]
    at = iota(v.shape, axis)
    return (
        pltpu.roll(jnp.where(at == 0, ahead, v), size - 1, axis=axis),
        pltpu.roll(jnp.where(at == size - 1, behind, v), 1, axis=axis),
    )


def sweep_pair(source, layers, z, low_row, high_row, store, tiles):
    count, rows = source.shape[1], source.shape[2] // layers
    z1 = lax.rem(z + 1, layers)
    for z, up, down in ((z, z1, lax.rem(z + layers - 1, layers)), (z1, lax.rem(z + 2, layers), z)):
        for x in range(0, rows, 8):
            for t in range(tiles):
                here = rows_at(z, x, rows)
                centre = [source[c, t, here, :] for c in range(3)]
                weights = mix(centre)
                for c in range(3):
                    v = centre[c]
                    ahead = source[c, t, rows_at(z, x + 8, rows), :] if x + 8 < rows else high_row(c, t, z)
                    behind = source[c, t, rows_at(z, x - 8, rows), :] if x > 0 else low_row(c, t, z)
                    east, west = shifted(v, ahead, behind, 0)
                    north, south = shifted(v, source[c, (t + 1) % count, here, :], source[c, (t - 1) % count, here, :], 1)
                    above, below = source[c, t, rows_at(up, x, rows), :], source[c, t, rows_at(down, x, rows), :]
                    store(c, t, here, update(centre, weights, c, east, west, north, south, above, below))


def first_kernel(layers, velocity, edges, received, u1, u0, sems):
    count, cells = u0.shape[1:3]
    rows, tiles = cells // layers, count - 1
    depth, slots = 8, received.shape[0]
    part, steps = depth * rows, layers // depth

    def load(step, t):
        at = pl.ds(pl.multiple_of(step * part, part), part)
        return pltpu.make_async_copy(
            velocity.at[:, at, pl.ds(t * LANES, LANES)], u0.at[:, t, at], sems.at[step * tiles + t]
        )

    for step in range(steps):
        for t in range(tiles):
            load(step, t).start()
    arrived = Arrived(received, tiles * LANES)
    mask = edge_mask(beside())

    def store(c, t, here, new):
        u1[c, t, here, :] = new * mask if t == tiles else new

    def nothing(c, t, z):
        return 0.0

    @pl.loop(0, steps)
    def _(step):
        at = pl.ds(pl.multiple_of(step * part, part), part)
        chosen = arrived.choose(iota((part, slots), 0) + step * part)
        for t in range(tiles):
            load(step, t).wait()
        for c in range(3):
            main, edge = arrived.force(chosen, c)
            for t in range(tiles):
                u0[c, t, at, :] += main[:, t * LANES : (t + 1) * LANES]
            u0[c, tiles, at, :] = edges[c, at, :] + edge

        @pl.loop(jnp.where(step == 0, 1, 0), jnp.where(step == steps - 1, depth // 2 + 1, depth // 2))
        def _(i):
            sweep_pair(u0, layers, step * depth - 1 + 2 * i, nothing, nothing, store, count)


def last_kernel(
    layers, u1_in, rim, below_x, above_x, received, dw_hbm, fluid_hbm, replies, u1, near_dw, mid, halo, fluid, pick, sems
):
    count, cells = u1.shape[1:3]
    rows, tiles = cells // layers, count - 1
    patch, slots = tiles * LANES, received.shape[0]
    sides = beside()
    mask = edge_mask(sides)
    ahead = pltpu.make_async_copy(dw_hbm.at[pl.ds(0, near_dw.shape[0])], near_dw, sems.at[layers // 8])
    ahead.start()

    heads = received[:, 3 * patch :].astype(F32)
    slot = (heads[:, 0:1] * 32.0 + heads[:, 1:2] - 1.0).astype(jnp.int32)
    for first in range(0, cells, 256):
        pick[:, first : first + 256] = (iota((slots, 256), 1) + first == slot).astype(F32).astype(BF16)

    for side, source in enumerate((below_x, above_x)):
        for c in range(3):
            for j in range(2):
                for t in range(count):
                    arrived = source[c, j, :, t * LANES : (t + 1) * LANES].astype(F32)
                    halo[side, c, j, t] = jnp.where(sides[side] > 0.0, arrived, 0.0)
    for side in range(2):
        near, row = 1 - side, (rows - 1) * side
        slope = -transport_rate if side else transport_rate
        for t in range(count):
            scale = sides[side] * mask if t == tiles else sides[side]
            for g in range(0, layers, 8):
                at = slice(g, g + 8)
                after, before = (g + 8) % layers, (g - 8) % layers
                centre = [halo[side, c, near, t, at, :] for c in range(3)]
                weights = mix(centre)
                own = viscosity + slope * rim[side, 0, t, at, :]
                for c in range(3):
                    v = centre[c]
                    plane = halo.at[side, c, near]
                    inner, outer = rim[side, c, t, at, :], halo[side, c, side, t, at, :]
                    east, west = (outer, inner) if side else (inner, outer)
                    north, south = shifted(v, plane[(t + 1) % count, at, :], plane[(t - 1) % count, at, :], 1)
                    up, down = shifted(v, plane[t, after : after + 8, :], plane[t, before : before + 8, :], 0)
                    mid[side, c, t, at, :] = scale * update(
                        centre, weights, c, east, west, north, south, up, down
                    )
                    term = own * v
                    strided = pl.ds(g * rows + row, 8, stride=rows)
                    u1[c, t, strided, :] += term * mask if t == tiles else term

    def store(c, t, here, new):
        fluid[c, here, t * LANES : (t + 1) * LANES] = new

    depth = 8

    def write(step):
        at = pl.ds(pl.multiple_of(step * depth * rows, depth * rows), depth * rows)
        return pltpu.make_async_copy(fluid.at[:, at], fluid_hbm.at[:, at], sems.at[step])

    @pl.loop(0, layers // depth)
    def _(step):
        @pl.loop(0, depth // 2)
        def _(i):
            sweep_pair(
                u1,
                layers,
                step * depth + 2 * i,
                lambda c, t, z: mid[0, c, t, pl.ds(z, 1), :],
                lambda c, t, z: mid[1, c, t, pl.ds(z, 1), :],
                store,
                tiles,
            )

        write(step).start()

    for c in range(3):
        replies[:, c * patch : (c + 1) * patch] = dot(pick[...], fluid[c].astype(BF16)).astype(BF16)
    for step in range(layers // depth):
        write(step).wait()
    ahead.wait()


def gather_kernel(pts, dest, returned, near_dw, dw_hbm, out, dw, picked, moved, sems):
    entries, slots = dest.shape[0], returned.shape[0]
    near, blocks, patch, points = near_dw.shape[0], dw.shape[0], dw.shape[2], pts.shape[2]
    inter = entries // blocks
    for b in range(near, blocks):
        pltpu.make_async_copy(dw_hbm.at[b], dw.at[b], sems.at[b]).start()
    to = dest[:, 0:1].astype(jnp.int32)
    pick = (iota((entries, slots), 1) == to).astype(F32).astype(BF16)
    for c in range(3):
        picked[c] = dot(pick, returned[:, c * patch : (c + 1) * patch])
    k_of_lane = lax.rem(iota((points, LANES), 1), inter)

    def block(b, weights):
        at = pl.ds(pl.multiple_of(b * inter, inter), inter)
        parts = [picked[c, at, :] for c in range(3)]
        parts.append(jnp.zeros((LANES - 3 * inter, patch), F32))
        cells = jnp.concatenate(parts, axis=0).astype(BF16)
        every = lax.dot_general(weights, cells, (((1,), (1,)), ((), ())), preferred_element_type=F32)
        folded = jnp.zeros((points, LANES), F32)
        for k in range(inter):
            folded += jnp.where(k_of_lane == k, every[k * points : (k + 1) * points], 0.0)
        turned = jnp.transpose(folded)
        for c in range(3):
            moved[c, pl.ds(b, 1), :] = jnp.sum(turned[c * inter : (c + 1) * inter], axis=0, keepdims=True)

    @pl.loop(0, near)
    def _(b):
        block(b, near_dw[b])

    @pl.loop(near, blocks)
    def _(b):
        pltpu.make_async_copy(dw_hbm.at[b], dw.at[b], sems.at[b]).wait()
        block(b, dw[b])

    for c in range(3):
        out[c] = pts[c] + fiber_step * moved[c]


def in_hbm(x):
    return pltpu.with_memory_space_constraint(x, pltpu.HBM)


def params(limit):
    return pltpu.CompilerParams(vmem_limit_bytes=limit << 20)


def cost(flops, size):
    return pl.CostEstimate(flops=flops, bytes_accessed=size << 20, transcendentals=0)


VMEM = pl.BlockSpec(memory_space=pltpu.VMEM)
HBM = pl.BlockSpec(memory_space=pltpu.HBM)


def run_spread(gy_size, slots, pts, stiffness, links, owners, patch_slots, dw):
    blocks, points = links.shape
    inter, patch = owners.shape[1], dw.shape[2]
    entries = blocks * inter
    return pl.pallas_call(
        functools.partial(spread_kernel, gy_size, slots),
        in_specs=[HBM] * 6,
        out_specs=[VMEM, VMEM],
        out_shape=[
            jax.ShapeDtypeStruct((slots, 3 * patch + LANES), BF16),
            jax.ShapeDtypeStruct((entries, LANES), F32),
        ],
        scratch_shapes=[
            pltpu.VMEM(dw.shape, BF16),
            pltpu.VMEM((3, blocks, points), F32),
            pltpu.VMEM((3, entries, patch), F32),
            pltpu.VMEM((3, slots, entries), BF16),
            pltpu.VMEM((3, blocks, points), F32),
            pltpu.SMEM((blocks,), F32),
            pltpu.VMEM((blocks, points), jnp.int32),
            pltpu.VMEM((blocks, inter), jnp.int32),
            pltpu.VMEM((blocks, inter), jnp.int32),
            pltpu.SemaphoreType.DMA((blocks + 5,)),
        ],
        compiler_params=params(24),
        cost_estimate=cost(10**9, 9),
        name="spread",
    )(*[in_hbm(x) for x in (pts, stiffness, links, owners, patch_slots, dw)])


def run_edges(velocity):
    cells = velocity.shape[1]
    return pl.pallas_call(
        edge_kernel,
        in_specs=[HBM],
        out_specs=[VMEM, VMEM],
        out_shape=[jax.ShapeDtypeStruct((8, cells), F32)] * 2,
        scratch_shapes=[pltpu.VMEM((3, cells, LANES), F32)] * 2 + [pltpu.SemaphoreType.DMA((6,))],
        compiler_params=params(24),
        cost_estimate=cost(10**8, 3),
        name="edges",
    )(in_hbm(velocity))


def run_lines(velocity):
    layers, patch = velocity.shape[1], velocity.shape[3]
    tiles = patch // LANES
    return pl.pallas_call(
        line_kernel,
        in_specs=[HBM],
        out_specs=VMEM,
        out_shape=jax.ShapeDtypeStruct((3, 4 * layers, patch), F32),
        scratch_shapes=[pltpu.VMEM((2, tiles, 3, layers, 8, LANES), F32), pltpu.SemaphoreType.DMA((2 * tiles,))],
        compiler_params=params(24),
        cost_estimate=cost(10**8, 3),
        name="lines",
    )(in_hbm(velocity))


def run_rim(layer_rows, layers, rim_velocity, ahead, behind, received):
    patch, cells = rim_velocity.shape[2], ahead.shape[1]
    wide = patch + LANES
    side = (3, 2, layers, wide)
    return pl.pallas_call(
        functools.partial(rim_kernel, layer_rows),
        in_specs=[VMEM] * 4,
        out_specs=[VMEM] * 4,
        out_shape=[
            jax.ShapeDtypeStruct(side, BF16),
            jax.ShapeDtypeStruct(side, BF16),
            jax.ShapeDtypeStruct((2, 3, wide // LANES, layers, LANES), F32),
            jax.ShapeDtypeStruct((3, cells, LANES), F32),
        ],
        compiler_params=params(24),
        cost_estimate=cost(10**8, 3),
        name="rim",
    )(rim_velocity, ahead, behind, received)


def run_first(layers, velocity, edge, received):
    cells, patch = velocity.shape[1:]
    block = (3, patch // LANES + 1, cells, LANES)
    return pl.pallas_call(
        functools.partial(first_kernel, layers),
        in_specs=[HBM, VMEM, VMEM],
        out_specs=VMEM,
        out_shape=jax.ShapeDtypeStruct(block, F32),
        scratch_shapes=[pltpu.VMEM(block, F32), pltpu.SemaphoreType.DMA((layers // 8 * (patch // LANES),))],
        compiler_params=params(24),
        cost_estimate=cost(2 * 10**9, 24),
        name="sweep_first",
    )(in_hbm(velocity), edge, received)


def run_last(layers, near, u1, rim, below_x, above_x, received, dw):
    count, cells = u1.shape[1:3]
    patch, slots = (count - 1) * LANES, received.shape[0]
    return pl.pallas_call(
        functools.partial(last_kernel, layers),
        in_specs=[VMEM] * 5 + [HBM],
        out_specs=[HBM, VMEM, VMEM, VMEM],
        out_shape=[
            jax.ShapeDtypeStruct((3, cells, patch), F32),
            jax.ShapeDtypeStruct((slots, 3 * patch), BF16),
            jax.ShapeDtypeStruct(u1.shape, F32),
            jax.ShapeDtypeStruct((near, *dw.shape[1:]), BF16),
        ],
        scratch_shapes=[
            pltpu.VMEM((2, 3, count, layers, LANES), F32),
            pltpu.VMEM((2, 3, 2, count, layers, LANES), F32),
            pltpu.VMEM((3, cells, patch), F32),
            pltpu.VMEM((slots, cells), BF16),
            pltpu.SemaphoreType.DMA((layers // 8 + 1,)),
        ],
        input_output_aliases={0: 2},
        compiler_params=params(34),
        cost_estimate=cost(2 * 10**9, 16),
        name="sweep_last",
    )(u1, rim, below_x, above_x, received, in_hbm(dw))


def run_gather(pts, dest, returned, near_dw, dw):
    blocks, patch = dw.shape[0], dw.shape[2]
    return pl.pallas_call(
        gather_kernel,
        in_specs=[VMEM] * 4 + [HBM],
        out_specs=VMEM,
        out_shape=jax.ShapeDtypeStruct(pts.shape, F32),
        scratch_shapes=[
            pltpu.VMEM(dw.shape, BF16),
            pltpu.VMEM((3, dest.shape[0], patch), F32),
            pltpu.VMEM(pts.shape, F32),
            pltpu.SemaphoreType.DMA((blocks,)),
        ],
        compiler_params=params(24),
        cost_estimate=cost(10**9, 9),
        name="interp",
    )(pts, dest, returned, near_dw, in_hbm(dw))


def shards(velocity, fiber_points, stiffness, links, delta_weights, owners, patch_slots):
    blocks, inter, points, patch = delta_weights.shape
    layers, rows, columns = velocity.shape[1:]
    gx_size, gy_size = lax.axis_size("gx"), lax.axis_size("gy")
    devices = gx_size * gy_size
    slots, cells = devices * 2, layers * rows
    pts = fiber_points.transpose(1, 0, 2)
    dw = delta_weights.reshape(blocks, inter * points, patch)
    outgoing, dest = run_spread(
        gy_size, slots, pts, stiffness, links, owners.reshape(blocks, inter), patch_slots, dw
    )

    def exchange(rows_out):
        size = rows_out.shape[1]
        return lax.all_to_all(
            rows_out.reshape(devices, 2, size), ("gx", "gy"), split_axis=0, concat_axis=0, tiled=True
        ).reshape(slots, size)

    received = exchange(outgoing)

    flat = velocity.reshape(3, cells, columns)
    first, last = run_edges(flat)
    ahead = lax.ppermute(first, "gy", [((i + 1) % gy_size, i) for i in range(gy_size)])
    behind = lax.ppermute(last, "gy", [(i, (i + 1) % gy_size) for i in range(gy_size)])
    low_rows, high_rows, rim, edge = run_rim(rows, layers, run_lines(velocity), ahead, behind, received)

    up = [(i, (i + 1) % gx_size) for i in range(gx_size)]
    below_x = lax.ppermute(high_rows, "gx", up)
    above_x = lax.ppermute(low_rows, "gx", [(b, a) for a, b in up])
    u1 = run_first(layers, flat, edge, received)
    fluid, replies, _, near_dw = run_last(layers, NEAR, u1, rim, below_x, above_x, received, dw)
    moved = run_gather(pts, dest, exchange(replies), near_dw, dw)
    return fluid.reshape(3, layers, rows, columns), moved.transpose(1, 0, 2)


def solution(mesh):
    placed = (
        P(None, None, "gx", "gy"),
        P(("gx", "gy"), None, None),
        P(("gx", "gy")),
        P(("gx", "gy"), None),
        P(("gx", "gy"), None, None, None),
        P(("gx", "gy"), None, None),
        P(("gx", "gy"), None),
    )
    return jax.shard_map(
        shards,
        mesh=mesh,
        in_specs=placed,
        out_specs=(P(None, None, "gx", "gy"), P(("gx", "gy"), None, None)),
        check_vma=False,
    )
```

```python
import functools

import jax
import jax.numpy as jnp
from jax import lax
from jax.experimental import pallas as pl
from jax.experimental.pallas import tpu as pltpu
from jax.sharding import PartitionSpec as P

viscosity = 0.1
transport_rate = 0.1
force_step = 0.5
fiber_step = 0.25

F32 = jnp.float32
BF16 = jnp.bfloat16
LANES = 128
BELOW, ABOVE = 2, 10
NEAR = 1


def dot(a, b):
    return jnp.dot(a, b, preferred_element_type=F32)


def iota(shape, axis):
    return lax.broadcasted_iota(jnp.int32, shape, axis)


def spread_kernel(
    gy_size, slots, pts_hbm, stiff_hbm, links_hbm, owners_hbm, patch_slots_hbm, dw_hbm, out, dest_out,
    dw, force, rows, choose, pts, stiff, links, owners, patch_slots, sems,
):
    blocks, points = links.shape
    inter = owners.shape[1]
    entries = blocks * inter
    patch = rows.shape[2]
    small = [
        (pts_hbm, pts), (stiff_hbm, stiff), (links_hbm, links), (owners_hbm, owners), (patch_slots_hbm, patch_slots)
    ]
    small = [pltpu.make_async_copy(a, b, sems.at[blocks + i]) for i, (a, b) in enumerate(small)]
    for copy in small + [pltpu.make_async_copy(dw_hbm.at[b], dw.at[b], sems.at[b]) for b in range(blocks)]:
        copy.start()
    for copy in small:
        copy.wait()
    partner = lax.rem(iota((blocks, points), 1) + links[...], points)
    for c in range(3):
        own = pts[c]
        force[c] = jnp.take_along_axis(own, partner, axis=1) - own

    pick_block = (iota((entries, blocks), 0) // inter == iota((entries, blocks), 1)).astype(F32).astype(BF16)
    pick_k = lax.rem(iota((entries, inter), 0), inter) == iota((entries, inter), 1)

    def as_column(table):
        spread_rows = dot(pick_block, table.astype(F32).astype(BF16))
        return jnp.sum(jnp.where(pick_k, spread_rows, 0.0), axis=1, keepdims=True)

    owner = as_column(owners[...])
    code = patch_slots[...] + 1
    high, low = as_column(code // 32), as_column(lax.rem(code, 32))
    owner_wide = jnp.broadcast_to(owner, (entries, LANES))
    owner_row = jnp.transpose(
        jnp.concatenate([owner_wide, jnp.zeros((LANES - entries, LANES), F32)], axis=0)
    )[:entries, :entries]
    same = (owner_wide[:, :entries] == owner_row) & (iota((entries, entries), 1) < iota((entries, entries), 0))
    rank = jnp.sum(jnp.where(same, 1.0, 0.0), axis=1, keepdims=True)
    dest_wide = jnp.broadcast_to(owner * 2.0 + rank, (entries, LANES))
    dest_out[...] = dest_wide
    padded = jnp.concatenate([dest_wide, jnp.full((LANES - entries, LANES), -8.0, F32)], axis=0)
    dest_row = jnp.transpose(padded)[0:1, :entries].astype(jnp.int32)
    position = lax.rem(dest_row // 2, gy_size)
    slot = iota((slots, entries), 0)
    choose[0] = (slot == dest_row).astype(F32).astype(BF16)
    choose[1] = ((slot == dest_row + 2) & (position < gy_size - 1)).astype(F32).astype(BF16)
    choose[2] = ((slot == dest_row - 2) & (position > 0)).astype(F32).astype(BF16)
    lane = iota((entries, LANES), 1)

    def digits(at):
        return jnp.where(lane == at, high, 0.0) + jnp.where(lane == at + 1, low, 0.0)

    own_head, above_head, below_head = digits(0), digits(BELOW), digits(ABOVE)
    group = iota((inter, inter * points), 0)
    column = iota((inter, inter * points), 1) // points

    @pl.loop(0, blocks)
    def _(b):
        stiffness = stiff[b]
        parts = []
        for c in range(3):
            row = (stiffness * force[c, pl.ds(b, 1), :]).astype(BF16).astype(F32)
            wide = jnp.concatenate([jnp.broadcast_to(row, (inter, points))] * inter, axis=1)
            parts.append(jnp.where(group == column, wide, 0.0))
        parts.append(jnp.zeros_like(parts[0]))
        pltpu.make_async_copy(dw_hbm.at[b], dw.at[b], sems.at[b]).wait()
        spread = dot(jnp.concatenate(parts, axis=0).astype(BF16), dw[b])
        for c in range(3):
            rows[c, pl.ds(pl.multiple_of(b * inter, inter), inter), :] = spread[c * inter : (c + 1) * inter]

    for c in range(3):
        tail = pltpu.roll(rows[c, :, patch - LANES :], BELOW + 4 + 2 * c, axis=1)
        at = BELOW + 2 + 2 * c
        above_head += jnp.where((lane == at) | (lane == at + 1), tail, 0.0)
        at = ABOVE + 2 + 2 * c
        start = pltpu.roll(rows[c, :, :LANES], at, axis=1)
        below_head += jnp.where((lane == at) | (lane == at + 1), start, 0.0)
        out[:, c * patch : (c + 1) * patch] = dot(choose[0], rows[c].astype(BF16)).astype(BF16)
    head = dot(choose[0], own_head.astype(BF16))
    head += dot(choose[1], above_head.astype(BF16))
    head += dot(choose[2], below_head.astype(BF16))
    out[:, 3 * patch :] = head.astype(BF16)


def edge_kernel(velocity, first, last, start, end, sems):
    patch = velocity.shape[2]
    loads = []
    for c in range(3):
        for i, (to, lane) in enumerate(((start, 0), (end, patch - LANES))):
            loads.append(pltpu.make_async_copy(velocity.at[c, :, pl.ds(lane, LANES)], to.at[c], sems.at[2 * c + i]))
    for load in loads:
        load.start()
    row, lane = iota((16, LANES), 0), iota((16, LANES), 1)
    across = (((1,), (1,)), ((), ()))
    sums = [0.0, 0.0]
    for c in range(3):
        for i, (tile, at) in enumerate(((start, 0), (end, LANES - 2))):
            loads[2 * c + i].wait()
            pick = ((row - 2 * c == lane - at) & (lane >= at) & (lane < at + 2)).astype(F32).astype(BF16)
            sums[i] += lax.dot_general(pick, tile[c].astype(BF16), across, preferred_element_type=F32)
    first[...] = sums[0][:8]
    last[...] = sums[1][:8]


def line_kernel(velocity, out, lines, sems):
    layers, rows, patch = velocity.shape[1:]
    loads = []
    for i, x in enumerate((0, rows - 8)):
        for t in range(patch // LANES):
            part = velocity.at[:, :, pl.ds(x, 8), pl.ds(t * LANES, LANES)]
            loads.append(pltpu.make_async_copy(part, lines.at[i, t], sems.at[len(loads)]))
    for load in loads:
        load.start()
    for i in range(2):
        for t in range(patch // LANES):
            loads[i * (patch // LANES) + t].wait()
            for c in range(3):
                for j in range(2):
                    at = (2 * i + j) * layers
                    out[c, at : at + layers, t * LANES : (t + 1) * LANES] = lines[i, t, c, :, 6 * i + j, :]


class Arrived:
    def __init__(self, received, patch):
        self.received, self.patch = received, patch
        slots = received.shape[0]
        head = received[:, 3 * patch :].astype(F32)
        head_t = jnp.transpose(head)
        lane = iota((slots, LANES), 1)
        self.tails, self.starts = [], []
        for c in range(3):
            tail = pltpu.roll(head, LANES - 4 - BELOW - 2 * c, axis=1)
            self.tails.append(jnp.where(lane >= LANES - 2, tail, 0.0).astype(BF16))
            start = pltpu.roll(head, LANES - (ABOVE + 2 + 2 * c), axis=1)
            self.starts.append(jnp.where(lane < 2, start, 0.0).astype(BF16))
        self.slots = [
            (head_t[at : at + 1] * 32.0 + head_t[at + 1 : at + 2] - 1.0).astype(jnp.int32) for at in (0, BELOW, ABOVE)
        ]

    def choose(self, row):
        return [(row == slot).astype(F32).astype(BF16) for slot in self.slots]

    def force(self, chosen, c):
        return force_step * dot(chosen[0], self.received[:, c * self.patch : (c + 1) * self.patch])

    def edges(self, chosen):
        tails, starts = jnp.concatenate(self.tails, axis=1), jnp.concatenate(self.starts, axis=1)
        return force_step * (dot(chosen[1], tails) + dot(chosen[2], starts))


def rim_kernel(layer_rows, velocity, ahead, behind, received, low_rows, high_rows, rim, edges):
    layers, patch = low_rows.shape[2], velocity.shape[2]
    slots, cells = received.shape[0], ahead.shape[1]

    sides = beside()
    from_ahead = jnp.where(sides[3] > 0.0, ahead[...], 0.0)
    from_behind = jnp.where(sides[2] > 0.0, behind[...], 0.0)
    turned = jnp.transpose(jnp.concatenate([from_ahead, from_behind, jnp.zeros((LANES - 16, cells), F32)], axis=0))
    turned = turned.astype(BF16)
    row, lane = iota((LANES, LANES), 0), iota((LANES, LANES), 1)
    for c in range(3):
        put = ((lane < 2) & (row == lane + 2 * c)) | ((lane >= LANES - 2) & (row == lane - (LANES - 2) + 8 + 2 * c))
        edges[c] = dot(turned, put.astype(F32).astype(BF16))

    arrived = Arrived(received, patch)
    row = iota((4 * layers, slots), 0)
    line, z = row // layers, lax.rem(row, layers)
    chosen = arrived.choose(z * layer_rows + jnp.where(line < 2, line, layer_rows - 4 + line))
    from_edges = arrived.edges(chosen)
    for c in range(3):
        main = velocity[c] + arrived.force(chosen, c)
        edge = from_edges[:, c * LANES : (c + 1) * LANES]
        for j in range(4):
            at = slice(j * layers, (j + 1) * layers)
            x = j if j < 2 else layer_rows - 4 + j
            side = edges[c, pl.ds(x, layers, stride=layer_rows), :] + edge[at]
            to = low_rows if j < 2 else high_rows
            to[c, j % 2, :, :patch] = main[at].astype(BF16)
            to[c, j % 2, :, patch:] = side.astype(BF16)
            if j in (0, 3):
                for t in range(patch // LANES):
                    rim[j // 3, c, t] = main[at, t * LANES : (t + 1) * LANES]
                rim[j // 3, c, patch // LANES] = side


def update(centre, weights, c, east, west, north, south, up, down):
    (px, mx), (py, my), (pz, mz) = weights
    keep = 1.0 - 6.0 * viscosity
    return keep * centre[c] + px * east + mx * west + py * north + my * south + pz * up + mz * down


def mix(centre):
    return [(viscosity - transport_rate * v, viscosity + transport_rate * v) for v in centre]


def beside():
    flags = []
    for axis in ("gx", "gy"):
        at, size = lax.axis_index(axis), lax.axis_size(axis)
        flags += [jnp.where(at > 0, 1.0, 0.0).astype(F32), jnp.where(at < size - 1, 1.0, 0.0).astype(F32)]
    return flags


def edge_mask(sides):
    lane = iota((8, LANES), 1)
    return jnp.where(lane == 0, sides[3], 0.0) + jnp.where(lane == LANES - 1, sides[2], 0.0)


def rows_at(z, x, rows):
    return pl.ds(pl.multiple_of(z * rows + x, 8), 8)


def shifted(v, ahead, behind, axis):
    size = v.shape[axis]
    at = iota(v.shape, axis)
    return (
        pltpu.roll(jnp.where(at == 0, ahead, v), size - 1, axis=axis),
        pltpu.roll(jnp.where(at == size - 1, behind, v), 1, axis=axis),
    )


def sweep_pair(source, layers, z, low_row, high_row, store, tiles):
    count, rows = source.shape[1], source.shape[2] // layers
    z1 = lax.rem(z + 1, layers)
    for z, up, down in ((z, z1, lax.rem(z + layers - 1, layers)), (z1, lax.rem(z + 2, layers), z)):
        for x in range(0, rows, 8):
            for t in range(tiles):
                here = rows_at(z, x, rows)
                centre = [source[c, t, here, :] for c in range(3)]
                weights = mix(centre)
                for c in range(3):
                    v = centre[c]
                    ahead = source[c, t, rows_at(z, x + 8, rows), :] if x + 8 < rows else high_row(c, t, z)
                    behind = source[c, t, rows_at(z, x - 8, rows), :] if x > 0 else low_row(c, t, z)
                    east, west = shifted(v, ahead, behind, 0)
                    north, south = shifted(v, source[c, (t + 1) % count, here, :], source[c, (t - 1) % count, here, :], 1)
                    above, below = source[c, t, rows_at(up, x, rows), :], source[c, t, rows_at(down, x, rows), :]
                    store(c, t, here, update(centre, weights, c, east, west, north, south, above, below))


def first_kernel(layers, velocity, edges, received, u1, u0, sems):
    count, cells = u0.shape[1:3]
    rows, tiles = cells // layers, count - 1
    depth, slots = 8, received.shape[0]
    part, steps = depth * rows, layers // depth

    def load(step, t):
        at = pl.ds(pl.multiple_of(step * part, part), part)
        return pltpu.make_async_copy(
            velocity.at[:, at, pl.ds(t * LANES, LANES)], u0.at[:, t, at], sems.at[step * tiles + t]
        )

    for step in range(steps):
        for t in range(tiles):
            load(step, t).start()
    arrived = Arrived(received, tiles * LANES)
    mask = edge_mask(beside())

    def store(c, t, here, new):
        u1[c, t, here, :] = new * mask if t == tiles else new

    def nothing(c, t, z):
        return 0.0

    @pl.loop(0, steps)
    def _(step):
        at = pl.ds(pl.multiple_of(step * part, part), part)
        chosen = arrived.choose(iota((part, slots), 0) + step * part)
        for t in range(tiles):
            load(step, t).wait()
        from_edges = arrived.edges(chosen)
        for c in range(3):
            main = arrived.force(chosen, c)
            for t in range(tiles):
                u0[c, t, at, :] += main[:, t * LANES : (t + 1) * LANES]
            u0[c, tiles, at, :] = edges[c, at, :] + from_edges[:, c * LANES : (c + 1) * LANES]

        @pl.loop(jnp.where(step == 0, 1, 0), jnp.where(step == steps - 1, depth // 2 + 1, depth // 2))
        def _(i):
            sweep_pair(u0, layers, step * depth - 1 + 2 * i, nothing, nothing, store, count)


def last_kernel(
    layers, u1_in, rim, below_x, above_x, received, dw_hbm, fluid_hbm, replies, u1, near_dw, mid, halo, fluid, pick, sems
):
    count, cells = u1.shape[1:3]
    rows, tiles = cells // layers, count - 1
    patch, slots = tiles * LANES, received.shape[0]
    sides = beside()
    mask = edge_mask(sides)
    ahead = pltpu.make_async_copy(dw_hbm.at[pl.ds(0, near_dw.shape[0])], near_dw, sems.at[layers // 4])
    ahead.start()

    heads = received[:, 3 * patch :].astype(F32)
    slot = (heads[:, 0:1] * 32.0 + heads[:, 1:2] - 1.0).astype(jnp.int32)
    for first in range(0, cells, 256):
        pick[:, first : first + 256] = (iota((slots, 256), 1) + first == slot).astype(F32).astype(BF16)

    for side, source in enumerate((below_x, above_x)):
        for c in range(3):
            for j in range(2):
                for t in range(count):
                    arrived = source[c, j, :, t * LANES : (t + 1) * LANES].astype(F32)
                    halo[side, c, j, t] = jnp.where(sides[side] > 0.0, arrived, 0.0)
    for side in range(2):
        near, row = 1 - side, (rows - 1) * side
        slope = -transport_rate if side else transport_rate
        for t in range(count):
            scale = sides[side] * mask if t == tiles else sides[side]
            for g in range(0, layers, 8):
                at = slice(g, g + 8)
                after, before = (g + 8) % layers, (g - 8) % layers
                centre = [halo[side, c, near, t, at, :] for c in range(3)]
                weights = mix(centre)
                own = viscosity + slope * rim[side, 0, t, at, :]
                for c in range(3):
                    v = centre[c]
                    plane = halo.at[side, c, near]
                    inner, outer = rim[side, c, t, at, :], halo[side, c, side, t, at, :]
                    east, west = (outer, inner) if side else (inner, outer)
                    north, south = shifted(v, plane[(t + 1) % count, at, :], plane[(t - 1) % count, at, :], 1)
                    up, down = shifted(v, plane[t, after : after + 8, :], plane[t, before : before + 8, :], 0)
                    mid[side, c, t, at, :] = scale * update(
                        centre, weights, c, east, west, north, south, up, down
                    )
                    term = own * v
                    strided = pl.ds(g * rows + row, 8, stride=rows)
                    u1[c, t, strided, :] += term * mask if t == tiles else term

    def store(c, t, here, new):
        fluid[c, here, t * LANES : (t + 1) * LANES] = new

    depth = 4

    def write(step):
        at = pl.ds(pl.multiple_of(step * depth * rows, depth * rows), depth * rows)
        return pltpu.make_async_copy(fluid.at[:, at], fluid_hbm.at[:, at], sems.at[step])

    @pl.loop(0, layers // depth)
    def _(step):
        @pl.loop(0, depth // 2)
        def _(i):
            sweep_pair(
                u1,
                layers,
                step * depth + 2 * i,
                lambda c, t, z: mid[0, c, t, pl.ds(z, 1), :],
                lambda c, t, z: mid[1, c, t, pl.ds(z, 1), :],
                store,
                tiles,
            )

        write(step).start()

    for c in range(3):
        replies[:, c * patch : (c + 1) * patch] = dot(pick[...], fluid[c].astype(BF16)).astype(BF16)
    for step in range(layers // depth):
        write(step).wait()
    ahead.wait()


def gather_kernel(pts, dest, returned, near_dw, dw_hbm, out, dw, picked, moved, sems):
    entries, slots = dest.shape[0], returned.shape[0]
    near, blocks, patch, points = near_dw.shape[0], dw.shape[0], dw.shape[2], pts.shape[2]
    inter = entries // blocks
    for b in range(near, blocks):
        pltpu.make_async_copy(dw_hbm.at[b], dw.at[b], sems.at[b]).start()
    to = dest[:, 0:1].astype(jnp.int32)
    pick = (iota((entries, slots), 1) == to).astype(F32).astype(BF16)
    for c in range(3):
        picked[c] = dot(pick, returned[:, c * patch : (c + 1) * patch])
    group = iota((inter, inter * points), 0)
    column = iota((inter, inter * points), 1) // points

    def block(b, weights):
        at = pl.ds(pl.multiple_of(b * inter, inter), inter)
        parts = [picked[c, at, :] for c in range(3)]
        parts.append(jnp.zeros((inter, patch), F32))
        cells = jnp.concatenate(parts, axis=0).astype(BF16)
        every = lax.dot_general(cells, weights, (((1,), (1,)), ((), ())), preferred_element_type=F32)
        for c in range(3):
            own = jnp.where(group == column, every[c * inter : (c + 1) * inter], 0.0)
            folded = own[:, :points]
            for k in range(1, inter):
                folded = folded + own[:, k * points : (k + 1) * points]
            moved[c, pl.ds(b, 1), :] = jnp.sum(folded, axis=0, keepdims=True)

    @pl.loop(0, near)
    def _(b):
        block(b, near_dw[b])

    @pl.loop(near, blocks)
    def _(b):
        pltpu.make_async_copy(dw_hbm.at[b], dw.at[b], sems.at[b]).wait()
        block(b, dw[b])

    for c in range(3):
        out[c] = pts[c] + fiber_step * moved[c]


def in_hbm(x):
    return pltpu.with_memory_space_constraint(x, pltpu.HBM)


def params(limit):
    return pltpu.CompilerParams(vmem_limit_bytes=limit << 20)


def cost(flops, size):
    return pl.CostEstimate(flops=flops, bytes_accessed=size << 20, transcendentals=0)


VMEM = pl.BlockSpec(memory_space=pltpu.VMEM)
HBM = pl.BlockSpec(memory_space=pltpu.HBM)


def run_spread(gy_size, slots, pts, stiffness, links, owners, patch_slots, dw):
    blocks, points = links.shape
    inter, patch = owners.shape[1], dw.shape[2]
    entries = blocks * inter
    return pl.pallas_call(
        functools.partial(spread_kernel, gy_size, slots),
        in_specs=[HBM] * 6,
        out_specs=[VMEM, VMEM],
        out_shape=[
            jax.ShapeDtypeStruct((slots, 3 * patch + LANES), BF16),
            jax.ShapeDtypeStruct((entries, LANES), F32),
        ],
        scratch_shapes=[
            pltpu.VMEM(dw.shape, BF16),
            pltpu.VMEM((3, blocks, points), F32),
            pltpu.VMEM((3, entries, patch), F32),
            pltpu.VMEM((3, slots, entries), BF16),
            pltpu.VMEM((3, blocks, points), F32),
            pltpu.SMEM((blocks,), F32),
            pltpu.VMEM((blocks, points), jnp.int32),
            pltpu.VMEM((blocks, inter), jnp.int32),
            pltpu.VMEM((blocks, inter), jnp.int32),
            pltpu.SemaphoreType.DMA((blocks + 5,)),
        ],
        compiler_params=params(24),
        cost_estimate=cost(10**9, 9),
        name="spread",
    )(*[in_hbm(x) for x in (pts, stiffness, links, owners, patch_slots, dw)])


def run_edges(velocity):
    cells = velocity.shape[1]
    return pl.pallas_call(
        edge_kernel,
        in_specs=[HBM],
        out_specs=[VMEM, VMEM],
        out_shape=[jax.ShapeDtypeStruct((8, cells), F32)] * 2,
        scratch_shapes=[pltpu.VMEM((3, cells, LANES), F32)] * 2 + [pltpu.SemaphoreType.DMA((6,))],
        compiler_params=params(24),
        cost_estimate=cost(10**8, 3),
        name="edges",
    )(in_hbm(velocity))


def run_lines(velocity):
    layers, patch = velocity.shape[1], velocity.shape[3]
    tiles = patch // LANES
    return pl.pallas_call(
        line_kernel,
        in_specs=[HBM],
        out_specs=VMEM,
        out_shape=jax.ShapeDtypeStruct((3, 4 * layers, patch), F32),
        scratch_shapes=[pltpu.VMEM((2, tiles, 3, layers, 8, LANES), F32), pltpu.SemaphoreType.DMA((2 * tiles,))],
        compiler_params=params(24),
        cost_estimate=cost(10**8, 3),
        name="lines",
    )(in_hbm(velocity))


def run_rim(layer_rows, layers, rim_velocity, ahead, behind, received):
    patch, cells = rim_velocity.shape[2], ahead.shape[1]
    wide = patch + LANES
    side = (3, 2, layers, wide)
    return pl.pallas_call(
        functools.partial(rim_kernel, layer_rows),
        in_specs=[VMEM] * 4,
        out_specs=[VMEM] * 4,
        out_shape=[
            jax.ShapeDtypeStruct(side, BF16),
            jax.ShapeDtypeStruct(side, BF16),
            jax.ShapeDtypeStruct((2, 3, wide // LANES, layers, LANES), F32),
            jax.ShapeDtypeStruct((3, cells, LANES), F32),
        ],
        compiler_params=params(24),
        cost_estimate=cost(10**8, 3),
        name="rim",
    )(rim_velocity, ahead, behind, received)


def run_first(layers, velocity, edge, received):
    cells, patch = velocity.shape[1:]
    block = (3, patch // LANES + 1, cells, LANES)
    return pl.pallas_call(
        functools.partial(first_kernel, layers),
        in_specs=[HBM, VMEM, VMEM],
        out_specs=VMEM,
        out_shape=jax.ShapeDtypeStruct(block, F32),
        scratch_shapes=[pltpu.VMEM(block, F32), pltpu.SemaphoreType.DMA((layers // 8 * (patch // LANES),))],
        compiler_params=params(24),
        cost_estimate=cost(2 * 10**9, 24),
        name="sweep_first",
    )(in_hbm(velocity), edge, received)


def run_last(layers, near, u1, rim, below_x, above_x, received, dw):
    count, cells = u1.shape[1:3]
    patch, slots = (count - 1) * LANES, received.shape[0]
    return pl.pallas_call(
        functools.partial(last_kernel, layers),
        in_specs=[VMEM] * 5 + [HBM],
        out_specs=[HBM, VMEM, VMEM, VMEM],
        out_shape=[
            jax.ShapeDtypeStruct((3, cells, patch), F32),
            jax.ShapeDtypeStruct((slots, 3 * patch), BF16),
            jax.ShapeDtypeStruct(u1.shape, F32),
            jax.ShapeDtypeStruct((near, *dw.shape[1:]), BF16),
        ],
        scratch_shapes=[
            pltpu.VMEM((2, 3, count, layers, LANES), F32),
            pltpu.VMEM((2, 3, 2, count, layers, LANES), F32),
            pltpu.VMEM((3, cells, patch), F32),
            pltpu.VMEM((slots, cells), BF16),
            pltpu.SemaphoreType.DMA((layers // 4 + 1,)),
        ],
        input_output_aliases={0: 2},
        compiler_params=params(34),
        cost_estimate=cost(2 * 10**9, 16),
        name="sweep_last",
    )(u1, rim, below_x, above_x, received, in_hbm(dw))


def run_gather(pts, dest, returned, near_dw, dw):
    blocks, patch = dw.shape[0], dw.shape[2]
    return pl.pallas_call(
        gather_kernel,
        in_specs=[VMEM] * 4 + [HBM],
        out_specs=VMEM,
        out_shape=jax.ShapeDtypeStruct(pts.shape, F32),
        scratch_shapes=[
            pltpu.VMEM(dw.shape, BF16),
            pltpu.VMEM((3, dest.shape[0], patch), F32),
            pltpu.VMEM(pts.shape, F32),
            pltpu.SemaphoreType.DMA((blocks,)),
        ],
        compiler_params=params(24),
        cost_estimate=cost(10**9, 9),
        name="interp",
    )(pts, dest, returned, near_dw, in_hbm(dw))


def shards(velocity, fiber_points, stiffness, links, delta_weights, owners, patch_slots):
    blocks, inter, points, patch = delta_weights.shape
    layers, rows, columns = velocity.shape[1:]
    gx_size, gy_size = lax.axis_size("gx"), lax.axis_size("gy")
    devices = gx_size * gy_size
    slots, cells = devices * 2, layers * rows
    pts = fiber_points.transpose(1, 0, 2)
    dw = delta_weights.reshape(blocks, inter * points, patch)
    outgoing, dest = run_spread(
        gy_size, slots, pts, stiffness, links, owners.reshape(blocks, inter), patch_slots, dw
    )

    def exchange(rows_out):
        size = rows_out.shape[1]
        return lax.all_to_all(
            rows_out.reshape(devices, 2, size), ("gx", "gy"), split_axis=0, concat_axis=0, tiled=True
        ).reshape(slots, size)

    received = exchange(outgoing)

    flat = velocity.reshape(3, cells, columns)
    first, last = run_edges(flat)
    ahead = lax.ppermute(first, "gy", [((i + 1) % gy_size, i) for i in range(gy_size)])
    behind = lax.ppermute(last, "gy", [(i, (i + 1) % gy_size) for i in range(gy_size)])
    low_rows, high_rows, rim, edge = run_rim(rows, layers, run_lines(velocity), ahead, behind, received)

    up = [(i, (i + 1) % gx_size) for i in range(gx_size)]
    below_x = lax.ppermute(high_rows, "gx", up)
    above_x = lax.ppermute(low_rows, "gx", [(b, a) for a, b in up])
    u1 = run_first(layers, flat, edge, received)
    fluid, replies, _, near_dw = run_last(layers, NEAR, u1, rim, below_x, above_x, received, dw)
    moved = run_gather(pts, dest, exchange(replies), near_dw, dw)
    return fluid.reshape(3, layers, rows, columns), moved.transpose(1, 0, 2)


def solution(mesh):
    placed = (
        P(None, None, "gx", "gy"),
        P(("gx", "gy"), None, None),
        P(("gx", "gy")),
        P(("gx", "gy"), None),
        P(("gx", "gy"), None, None, None),
        P(("gx", "gy"), None, None),
        P(("gx", "gy"), None),
    )
    return jax.shard_map(
        shards,
        mesh=mesh,
        in_specs=placed,
        out_specs=(P(None, None, "gx", "gy"), P(("gx", "gy"), None, None)),
        check_vma=False,
    )
```

```python
import functools

import jax
import jax.numpy as jnp
from jax import lax
from jax.experimental import pallas as pl
from jax.experimental.pallas import tpu as pltpu
from jax.sharding import PartitionSpec as P

viscosity = 0.1
transport_rate = 0.1
force_step = 0.5
fiber_step = 0.25

F32 = jnp.float32
BF16 = jnp.bfloat16
LANES = 128
BELOW, ABOVE = 2, 10
NEAR = 1


def dot(a, b):
    return jnp.dot(a, b, preferred_element_type=F32)


def iota(shape, axis):
    return lax.broadcasted_iota(jnp.int32, shape, axis)


def spread_kernel(
    gy_size, slots, pts_hbm, stiff_hbm, links_hbm, owners_hbm, patch_slots_hbm, dw_hbm, out, dest_out,
    dw, force, rows, choose, pts, stiff, links, owners, patch_slots, sems,
):
    blocks, points = links.shape
    inter = owners.shape[1]
    entries = blocks * inter
    patch = rows.shape[2]
    small = [
        (pts_hbm, pts), (stiff_hbm, stiff), (links_hbm, links), (owners_hbm, owners), (patch_slots_hbm, patch_slots)
    ]
    small = [pltpu.make_async_copy(a, b, sems.at[blocks + i]) for i, (a, b) in enumerate(small)]
    for copy in small + [pltpu.make_async_copy(dw_hbm.at[b], dw.at[b], sems.at[b]) for b in range(blocks)]:
        copy.start()
    for copy in small:
        copy.wait()
    partner = lax.rem(iota((blocks, points), 1) + links[...], points)
    for c in range(3):
        own = pts[c]
        force[c] = jnp.take_along_axis(own, partner, axis=1) - own

    pick_block = (iota((entries, blocks), 0) // inter == iota((entries, blocks), 1)).astype(F32).astype(BF16)
    pick_k = lax.rem(iota((entries, inter), 0), inter) == iota((entries, inter), 1)

    def as_column(table):
        spread_rows = dot(pick_block, table.astype(F32).astype(BF16))
        return jnp.sum(jnp.where(pick_k, spread_rows, 0.0), axis=1, keepdims=True)

    owner = as_column(owners[...])
    code = patch_slots[...] + 1
    high, low = as_column(code // 32), as_column(lax.rem(code, 32))
    owner_wide = jnp.broadcast_to(owner, (entries, LANES))
    owner_row = jnp.transpose(
        jnp.concatenate([owner_wide, jnp.zeros((LANES - entries, LANES), F32)], axis=0)
    )[:entries, :entries]
    same = (owner_wide[:, :entries] == owner_row) & (iota((entries, entries), 1) < iota((entries, entries), 0))
    rank = jnp.sum(jnp.where(same, 1.0, 0.0), axis=1, keepdims=True)
    dest_wide = jnp.broadcast_to(owner * 2.0 + rank, (entries, LANES))
    dest_out[...] = dest_wide
    padded = jnp.concatenate([dest_wide, jnp.full((LANES - entries, LANES), -8.0, F32)], axis=0)
    dest_row = jnp.transpose(padded)[0:1, :entries].astype(jnp.int32)
    position = lax.rem(dest_row // 2, gy_size)
    slot = iota((slots, entries), 0)
    choose[0] = (slot == dest_row).astype(F32).astype(BF16)
    choose[1] = ((slot == dest_row + 2) & (position < gy_size - 1)).astype(F32).astype(BF16)
    choose[2] = ((slot == dest_row - 2) & (position > 0)).astype(F32).astype(BF16)
    lane = iota((entries, LANES), 1)

    def digits(at):
        return jnp.where(lane == at, high, 0.0) + jnp.where(lane == at + 1, low, 0.0)

    own_head, above_head, below_head = digits(0), digits(BELOW), digits(ABOVE)
    group = iota((inter, inter * points), 0)
    column = iota((inter, inter * points), 1) // points

    @pl.loop(0, blocks)
    def _(b):
        stiffness = stiff[b]
        parts = []
        for c in range(3):
            row = (stiffness * force[c, pl.ds(b, 1), :]).astype(BF16).astype(F32)
            wide = jnp.concatenate([jnp.broadcast_to(row, (inter, points))] * inter, axis=1)
            parts.append(jnp.where(group == column, wide, 0.0))
        parts.append(jnp.zeros_like(parts[0]))
        pltpu.make_async_copy(dw_hbm.at[b], dw.at[b], sems.at[b]).wait()
        spread = dot(jnp.concatenate(parts, axis=0).astype(BF16), dw[b])
        for c in range(3):
            rows[c, pl.ds(pl.multiple_of(b * inter, inter), inter), :] = spread[c * inter : (c + 1) * inter]

    for c in range(3):
        tail = pltpu.roll(rows[c, :, patch - LANES :], BELOW + 4 + 2 * c, axis=1)
        at = BELOW + 2 + 2 * c
        above_head += jnp.where((lane == at) | (lane == at + 1), tail, 0.0)
        at = ABOVE + 2 + 2 * c
        start = pltpu.roll(rows[c, :, :LANES], at, axis=1)
        below_head += jnp.where((lane == at) | (lane == at + 1), start, 0.0)
        out[:, c * patch : (c + 1) * patch] = dot(choose[0], rows[c].astype(BF16)).astype(BF16)
    head = dot(choose[0], own_head.astype(BF16))
    head += dot(choose[1], above_head.astype(BF16))
    head += dot(choose[2], below_head.astype(BF16))
    out[:, 3 * patch :] = head.astype(BF16)


def edge_kernel(velocity, first, last, start, end, sems):
    patch = velocity.shape[2]
    loads = []
    for c in range(3):
        for i, (to, lane) in enumerate(((start, 0), (end, patch - LANES))):
            loads.append(pltpu.make_async_copy(velocity.at[c, :, pl.ds(lane, LANES)], to.at[c], sems.at[2 * c + i]))
    for load in loads:
        load.start()
    row, lane = iota((16, LANES), 0), iota((16, LANES), 1)
    across = (((1,), (1,)), ((), ()))
    sums = [0.0, 0.0]
    for c in range(3):
        for i, (tile, at) in enumerate(((start, 0), (end, LANES - 2))):
            loads[2 * c + i].wait()
            pick = ((row - 2 * c == lane - at) & (lane >= at) & (lane < at + 2)).astype(F32).astype(BF16)
            sums[i] += lax.dot_general(pick, tile[c].astype(BF16), across, preferred_element_type=F32)
    first[...] = sums[0][:8]
    last[...] = sums[1][:8]


def line_kernel(velocity, out, lines, sems):
    layers, rows, patch = velocity.shape[1:]
    loads = []
    for i, x in enumerate((0, rows - 8)):
        for t in range(patch // LANES):
            part = velocity.at[:, :, pl.ds(x, 8), pl.ds(t * LANES, LANES)]
            loads.append(pltpu.make_async_copy(part, lines.at[i, t], sems.at[len(loads)]))
    for load in loads:
        load.start()
    for i in range(2):
        for t in range(patch // LANES):
            loads[i * (patch // LANES) + t].wait()
            for c in range(3):
                for j in range(2):
                    at = (2 * i + j) * layers
                    out[c, at : at + layers, t * LANES : (t + 1) * LANES] = lines[i, t, c, :, 6 * i + j, :]


class Arrived:
    def __init__(self, received, patch):
        self.received, self.patch = received, patch
        slots = received.shape[0]
        head = received[:, 3 * patch :].astype(F32)
        head_t = jnp.transpose(head)
        lane = iota((slots, LANES), 1)
        self.tails, self.starts = [], []
        for c in range(3):
            tail = pltpu.roll(head, LANES - 4 - BELOW - 2 * c, axis=1)
            self.tails.append(jnp.where(lane >= LANES - 2, tail, 0.0).astype(BF16))
            start = pltpu.roll(head, LANES - (ABOVE + 2 + 2 * c), axis=1)
            self.starts.append(jnp.where(lane < 2, start, 0.0).astype(BF16))
        self.slots = [
            (head_t[at : at + 1] * 32.0 + head_t[at + 1 : at + 2] - 1.0).astype(jnp.int32) for at in (0, BELOW, ABOVE)
        ]

    def choose(self, row):
        return [(row == slot).astype(F32).astype(BF16) for slot in self.slots]

    def force(self, chosen, c):
        return force_step * dot(chosen[0], self.received[:, c * self.patch : (c + 1) * self.patch])

    def edges(self, chosen):
        tails, starts = jnp.concatenate(self.tails, axis=1), jnp.concatenate(self.starts, axis=1)
        both = jnp.concatenate([tails, starts], axis=0)
        return force_step * dot(jnp.concatenate([chosen[1], chosen[2]], axis=1), both)


def rim_kernel(layer_rows, velocity, ahead, behind, received, low_rows, high_rows, rim, edges):
    layers, patch = low_rows.shape[1], velocity.shape[2]
    slots, cells, tiles = received.shape[0], ahead.shape[1], patch // LANES
    corners = [0.0, 0.0]
    z_lane = iota((layers, LANES), 1)

    sides = beside()
    from_ahead = jnp.where(sides[3] > 0.0, ahead[...], 0.0)
    from_behind = jnp.where(sides[2] > 0.0, behind[...], 0.0)
    turned = jnp.transpose(jnp.concatenate([from_ahead, from_behind, jnp.zeros((LANES - 16, cells), F32)], axis=0))
    turned = turned.astype(BF16)
    row, lane = iota((LANES, LANES), 0), iota((LANES, LANES), 1)
    for c in range(3):
        put = ((lane < 2) & (row == lane + 2 * c)) | ((lane >= LANES - 2) & (row == lane - (LANES - 2) + 8 + 2 * c))
        edges[c] = dot(turned, put.astype(F32).astype(BF16))

    arrived = Arrived(received, patch)
    row = iota((4 * layers, slots), 0)
    line, z = row // layers, lax.rem(row, layers)
    chosen = arrived.choose(z * layer_rows + jnp.where(line < 2, line, layer_rows - 4 + line))
    from_edges = arrived.edges(chosen)
    for c in range(3):
        main = velocity[c] + arrived.force(chosen, c)
        edge = from_edges[:, c * LANES : (c + 1) * LANES]
        for j in range(4):
            at = slice(j * layers, (j + 1) * layers)
            x = j if j < 2 else layer_rows - 4 + j
            side = edges[c, pl.ds(x, layers, stride=layer_rows), :] + edge[at]
            to = low_rows if j < 2 else high_rows
            for t in range(tiles):
                to[(c * 2 + j % 2) * tiles + t] = main[at, t * LANES : (t + 1) * LANES].astype(BF16)
            if j in (0, 3):
                for t in range(tiles):
                    rim[j // 3, c, t] = main[at, t * LANES : (t + 1) * LANES]
                rim[j // 3, c, tiles] = side
                corners[j // 3] += jnp.where(z_lane == 2 * c, pltpu.roll(side, 2 * c, axis=1), 0.0)
                corners[j // 3] += jnp.where(z_lane == 2 * c + 1, pltpu.roll(side, 2 * c + 2, axis=1), 0.0)
    low_rows[6 * tiles] = corners[0].astype(BF16)
    high_rows[6 * tiles] = corners[1].astype(BF16)


def update(centre, weights, c, east, west, north, south, up, down):
    (px, mx), (py, my), (pz, mz) = weights
    keep = 1.0 - 6.0 * viscosity
    return keep * centre[c] + px * east + mx * west + py * north + my * south + pz * up + mz * down


def mix(centre):
    return [(viscosity - transport_rate * v, viscosity + transport_rate * v) for v in centre]


def beside():
    flags = []
    for axis in ("gx", "gy"):
        at, size = lax.axis_index(axis), lax.axis_size(axis)
        flags += [jnp.where(at > 0, 1.0, 0.0).astype(F32), jnp.where(at < size - 1, 1.0, 0.0).astype(F32)]
    return flags


def edge_mask(sides):
    lane = iota((8, LANES), 1)
    return jnp.where(lane == 0, sides[3], 0.0) + jnp.where(lane == LANES - 1, sides[2], 0.0)


def rows_at(z, x, rows):
    return pl.ds(pl.multiple_of(z * rows + x, 8), 8)


def shifted(v, ahead, behind, axis):
    size = v.shape[axis]
    at = iota(v.shape, axis)
    return (
        pltpu.roll(jnp.where(at == 0, ahead, v), size - 1, axis=axis),
        pltpu.roll(jnp.where(at == size - 1, behind, v), 1, axis=axis),
    )


def sweep_pair(source, layers, z, low_row, high_row, store, tiles):
    count, rows = source.shape[1], source.shape[2] // layers
    z1 = lax.rem(z + 1, layers)
    for z, up, down in ((z, z1, lax.rem(z + layers - 1, layers)), (z1, lax.rem(z + 2, layers), z)):
        for x in range(0, rows, 8):
            for t in range(tiles):
                here = rows_at(z, x, rows)
                centre = [source[c, t, here, :] for c in range(3)]
                weights = mix(centre)
                for c in range(3):
                    v = centre[c]
                    ahead = source[c, t, rows_at(z, x + 8, rows), :] if x + 8 < rows else high_row(c, t, z)
                    behind = source[c, t, rows_at(z, x - 8, rows), :] if x > 0 else low_row(c, t, z)
                    east, west = shifted(v, ahead, behind, 0)
                    north, south = shifted(v, source[c, (t + 1) % count, here, :], source[c, (t - 1) % count, here, :], 1)
                    above, below = source[c, t, rows_at(up, x, rows), :], source[c, t, rows_at(down, x, rows), :]
                    store(c, t, here, update(centre, weights, c, east, west, north, south, above, below))


def first_kernel(layers, velocity, edges, received, u1, u0, sems):
    count, cells = u0.shape[1:3]
    rows, tiles = cells // layers, count - 1
    depth, slots = 8, received.shape[0]
    part, steps = depth * rows, layers // depth

    def load(step, t):
        at = pl.ds(pl.multiple_of(step * part, part), part)
        return pltpu.make_async_copy(
            velocity.at[:, at, pl.ds(t * LANES, LANES)], u0.at[:, t, at], sems.at[step * tiles + t]
        )

    for step in range(steps):
        for t in range(tiles):
            load(step, t).start()
    arrived = Arrived(received, tiles * LANES)
    mask = edge_mask(beside())

    def store(c, t, here, new):
        u1[c, t, here, :] = new * mask if t == tiles else new

    def nothing(c, t, z):
        return 0.0

    @pl.loop(0, steps)
    def _(step):
        at = pl.ds(pl.multiple_of(step * part, part), part)
        chosen = arrived.choose(iota((part, slots), 0) + step * part)
        for t in range(tiles):
            load(step, t).wait()
        from_edges = arrived.edges(chosen)
        for c in range(3):
            main = arrived.force(chosen, c)
            for t in range(tiles):
                u0[c, t, at, :] += main[:, t * LANES : (t + 1) * LANES]
            u0[c, tiles, at, :] = edges[c, at, :] + from_edges[:, c * LANES : (c + 1) * LANES]

        @pl.loop(jnp.where(step == 0, 1, 0), jnp.where(step == steps - 1, depth // 2 + 1, depth // 2))
        def _(i):
            sweep_pair(u0, layers, step * depth - 1 + 2 * i, nothing, nothing, store, count)


def last_kernel(
    layers, u1_in, rim, below_x, above_x, received, dw_hbm, fluid_hbm, replies, u1, near_dw, mid, halo, fluid, pick, sems
):
    count, cells = u1.shape[1:3]
    rows, tiles = cells // layers, count - 1
    patch, slots = tiles * LANES, received.shape[0]
    sides = beside()
    mask = edge_mask(sides)
    ahead = pltpu.make_async_copy(dw_hbm.at[pl.ds(0, near_dw.shape[0])], near_dw, sems.at[layers // 4])
    ahead.start()

    heads = received[:, 3 * patch :].astype(F32)
    slot = (heads[:, 0:1] * 32.0 + heads[:, 1:2] - 1.0).astype(jnp.int32)
    for first in range(0, cells, 256):
        pick[:, first : first + 256] = (iota((slots, 256), 1) + first == slot).astype(F32).astype(BF16)

    for side, source in enumerate((below_x, above_x)):
        for c in range(3):
            for j in range(2):
                for t in range(count):
                    if t < tiles:
                        arrived = source[(c * 2 + j) * tiles + t].astype(F32)
                    elif j == 1 - side:
                        corner = source[6 * tiles].astype(F32)
                        lane = iota(corner.shape, 1)
                        arrived = jnp.where(lane == 0, pltpu.roll(corner, (LANES - 2 * c) % LANES, axis=1), 0.0)
                        arrived += jnp.where(lane == LANES - 1, pltpu.roll(corner, LANES - 2 - 2 * c, axis=1), 0.0)
                    else:
                        continue
                    halo[side, c, j, t] = jnp.where(sides[side] > 0.0, arrived, 0.0)
    for side in range(2):
        near, row = 1 - side, (rows - 1) * side
        slope = -transport_rate if side else transport_rate
        for t in range(count):
            for g in range(0, layers, 8):
                at = slice(g, g + 8)
                after, before = (g + 8) % layers, (g - 8) % layers
                centre = [halo[side, c, near, t, at, :] for c in range(3)]
                weights = mix(centre)
                own = viscosity + slope * rim[side, 0, t, at, :]
                for c in range(3):
                    v = centre[c]
                    if t < tiles:
                        plane = halo.at[side, c, near]
                        inner, outer = rim[side, c, t, at, :], halo[side, c, side, t, at, :]
                        east, west = (outer, inner) if side else (inner, outer)
                        north, south = shifted(v, plane[(t + 1) % count, at, :], plane[(t - 1) % count, at, :], 1)
                        up, down = shifted(v, plane[t, after : after + 8, :], plane[t, before : before + 8, :], 0)
                        mid[side, c, t, at, :] = sides[side] * update(
                            centre, weights, c, east, west, north, south, up, down
                        )
                    term = own * v
                    strided = pl.ds(g * rows + row, 8, stride=rows)
                    u1[c, t, strided, :] += term * mask if t == tiles else term

    def store(c, t, here, new):
        fluid[c, here, t * LANES : (t + 1) * LANES] = new

    depth = 4

    def write(step):
        at = pl.ds(pl.multiple_of(step * depth * rows, depth * rows), depth * rows)
        return pltpu.make_async_copy(fluid.at[:, at], fluid_hbm.at[:, at], sems.at[step])

    @pl.loop(0, layers // depth)
    def _(step):
        @pl.loop(0, depth // 2)
        def _(i):
            sweep_pair(
                u1,
                layers,
                step * depth + 2 * i,
                lambda c, t, z: mid[0, c, t, pl.ds(z, 1), :],
                lambda c, t, z: mid[1, c, t, pl.ds(z, 1), :],
                store,
                tiles,
            )

        write(step).start()

    for c in range(3):
        replies[:, c * patch : (c + 1) * patch] = dot(pick[...], fluid[c].astype(BF16)).astype(BF16)
    for step in range(layers // depth):
        write(step).wait()
    ahead.wait()


def gather_kernel(pts, dest, returned, near_dw, dw_hbm, out, dw, picked, moved, sems):
    entries, slots = dest.shape[0], returned.shape[0]
    near, blocks, patch, points = near_dw.shape[0], dw.shape[0], dw.shape[2], pts.shape[2]
    inter = entries // blocks
    for b in range(near, blocks):
        pltpu.make_async_copy(dw_hbm.at[b], dw.at[b], sems.at[b]).start()
    to = dest[:, 0:1].astype(jnp.int32)
    pick = (iota((entries, slots), 1) == to).astype(F32).astype(BF16)
    for c in range(3):
        picked[c] = dot(pick, returned[:, c * patch : (c + 1) * patch])
    group = iota((inter, inter * points), 0)
    column = iota((inter, inter * points), 1) // points

    def block(b, weights):
        at = pl.ds(pl.multiple_of(b * inter, inter), inter)
        parts = [picked[c, at, :] for c in range(3)]
        parts.append(jnp.zeros((inter, patch), F32))
        cells = jnp.concatenate(parts, axis=0).astype(BF16)
        every = lax.dot_general(cells, weights, (((1,), (1,)), ((), ())), preferred_element_type=F32)
        for c in range(3):
            own = jnp.where(group == column, every[c * inter : (c + 1) * inter], 0.0)
            folded = own[:, :points]
            for k in range(1, inter):
                folded = folded + own[:, k * points : (k + 1) * points]
            moved[c, pl.ds(b, 1), :] = jnp.sum(folded, axis=0, keepdims=True)

    @pl.loop(0, near)
    def _(b):
        block(b, near_dw[b])

    @pl.loop(near, blocks)
    def _(b):
        pltpu.make_async_copy(dw_hbm.at[b], dw.at[b], sems.at[b]).wait()
        block(b, dw[b])

    for c in range(3):
        out[c] = pts[c] + fiber_step * moved[c]


def in_hbm(x):
    return pltpu.with_memory_space_constraint(x, pltpu.HBM)


def params(limit):
    return pltpu.CompilerParams(vmem_limit_bytes=limit << 20)


def cost(flops, size):
    return pl.CostEstimate(flops=flops, bytes_accessed=size << 20, transcendentals=0)


VMEM = pl.BlockSpec(memory_space=pltpu.VMEM)
HBM = pl.BlockSpec(memory_space=pltpu.HBM)


def run_spread(gy_size, slots, pts, stiffness, links, owners, patch_slots, dw):
    blocks, points = links.shape
    inter, patch = owners.shape[1], dw.shape[2]
    entries = blocks * inter
    return pl.pallas_call(
        functools.partial(spread_kernel, gy_size, slots),
        in_specs=[HBM] * 6,
        out_specs=[VMEM, VMEM],
        out_shape=[
            jax.ShapeDtypeStruct((slots, 3 * patch + LANES), BF16),
            jax.ShapeDtypeStruct((entries, LANES), F32),
        ],
        scratch_shapes=[
            pltpu.VMEM(dw.shape, BF16),
            pltpu.VMEM((3, blocks, points), F32),
            pltpu.VMEM((3, entries, patch), F32),
            pltpu.VMEM((3, slots, entries), BF16),
            pltpu.VMEM((3, blocks, points), F32),
            pltpu.SMEM((blocks,), F32),
            pltpu.VMEM((blocks, points), jnp.int32),
            pltpu.VMEM((blocks, inter), jnp.int32),
            pltpu.VMEM((blocks, inter), jnp.int32),
            pltpu.SemaphoreType.DMA((blocks + 5,)),
        ],
        compiler_params=params(24),
        cost_estimate=cost(10**9, 9),
        name="spread",
    )(*[in_hbm(x) for x in (pts, stiffness, links, owners, patch_slots, dw)])


def run_edges(velocity):
    cells = velocity.shape[1]
    return pl.pallas_call(
        edge_kernel,
        in_specs=[HBM],
        out_specs=[VMEM, VMEM],
        out_shape=[jax.ShapeDtypeStruct((8, cells), F32)] * 2,
        scratch_shapes=[pltpu.VMEM((3, cells, LANES), F32)] * 2 + [pltpu.SemaphoreType.DMA((6,))],
        compiler_params=params(24),
        cost_estimate=cost(10**8, 3),
        name="edges",
    )(in_hbm(velocity))


def run_lines(velocity):
    layers, patch = velocity.shape[1], velocity.shape[3]
    tiles = patch // LANES
    return pl.pallas_call(
        line_kernel,
        in_specs=[HBM],
        out_specs=VMEM,
        out_shape=jax.ShapeDtypeStruct((3, 4 * layers, patch), F32),
        scratch_shapes=[pltpu.VMEM((2, tiles, 3, layers, 8, LANES), F32), pltpu.SemaphoreType.DMA((2 * tiles,))],
        compiler_params=params(24),
        cost_estimate=cost(10**8, 3),
        name="lines",
    )(in_hbm(velocity))


def run_rim(layer_rows, layers, rim_velocity, ahead, behind, received):
    patch, cells = rim_velocity.shape[2], ahead.shape[1]
    side = (6 * (patch // LANES) + 1, layers, LANES)
    return pl.pallas_call(
        functools.partial(rim_kernel, layer_rows),
        in_specs=[VMEM] * 4,
        out_specs=[VMEM] * 4,
        out_shape=[
            jax.ShapeDtypeStruct(side, BF16),
            jax.ShapeDtypeStruct(side, BF16),
            jax.ShapeDtypeStruct((2, 3, patch // LANES + 1, layers, LANES), F32),
            jax.ShapeDtypeStruct((3, cells, LANES), F32),
        ],
        compiler_params=params(24),
        cost_estimate=cost(10**8, 3),
        name="rim",
    )(rim_velocity, ahead, behind, received)


def run_first(layers, velocity, edge, received):
    cells, patch = velocity.shape[1:]
    block = (3, patch // LANES + 1, cells, LANES)
    return pl.pallas_call(
        functools.partial(first_kernel, layers),
        in_specs=[HBM, VMEM, VMEM],
        out_specs=VMEM,
        out_shape=jax.ShapeDtypeStruct(block, F32),
        scratch_shapes=[pltpu.VMEM(block, F32), pltpu.SemaphoreType.DMA((layers // 8 * (patch // LANES),))],
        compiler_params=params(24),
        cost_estimate=cost(2 * 10**9, 24),
        name="sweep_first",
    )(in_hbm(velocity), edge, received)


def run_last(layers, near, u1, rim, below_x, above_x, received, dw):
    count, cells = u1.shape[1:3]
    patch, slots = (count - 1) * LANES, received.shape[0]
    return pl.pallas_call(
        functools.partial(last_kernel, layers),
        in_specs=[VMEM] * 5 + [HBM],
        out_specs=[HBM, VMEM, VMEM, VMEM],
        out_shape=[
            jax.ShapeDtypeStruct((3, cells, patch), F32),
            jax.ShapeDtypeStruct((slots, 3 * patch), BF16),
            jax.ShapeDtypeStruct(u1.shape, F32),
            jax.ShapeDtypeStruct((near, *dw.shape[1:]), BF16),
        ],
        scratch_shapes=[
            pltpu.VMEM((2, 3, count - 1, layers, LANES), F32),
            pltpu.VMEM((2, 3, 2, count, layers, LANES), F32),
            pltpu.VMEM((3, cells, patch), F32),
            pltpu.VMEM((slots, cells), BF16),
            pltpu.SemaphoreType.DMA((layers // 4 + 1,)),
        ],
        input_output_aliases={0: 2},
        compiler_params=params(34),
        cost_estimate=cost(2 * 10**9, 16),
        name="sweep_last",
    )(u1, rim, below_x, above_x, received, in_hbm(dw))


def run_gather(pts, dest, returned, near_dw, dw):
    blocks, patch = dw.shape[0], dw.shape[2]
    return pl.pallas_call(
        gather_kernel,
        in_specs=[VMEM] * 4 + [HBM],
        out_specs=VMEM,
        out_shape=jax.ShapeDtypeStruct(pts.shape, F32),
        scratch_shapes=[
            pltpu.VMEM(dw.shape, BF16),
            pltpu.VMEM((3, dest.shape[0], patch), F32),
            pltpu.VMEM(pts.shape, F32),
            pltpu.SemaphoreType.DMA((blocks,)),
        ],
        compiler_params=params(24),
        cost_estimate=cost(10**9, 9),
        name="interp",
    )(pts, dest, returned, near_dw, in_hbm(dw))


def shards(velocity, fiber_points, stiffness, links, delta_weights, owners, patch_slots):
    blocks, inter, points, patch = delta_weights.shape
    layers, rows, columns = velocity.shape[1:]
    gx_size, gy_size = lax.axis_size("gx"), lax.axis_size("gy")
    devices = gx_size * gy_size
    slots, cells = devices * 2, layers * rows
    pts = fiber_points.transpose(1, 0, 2)
    dw = delta_weights.reshape(blocks, inter * points, patch)
    outgoing, dest = run_spread(
        gy_size, slots, pts, stiffness, links, owners.reshape(blocks, inter), patch_slots, dw
    )

    def exchange(rows_out):
        size = rows_out.shape[1]
        return lax.all_to_all(
            rows_out.reshape(devices, 2, size), ("gx", "gy"), split_axis=0, concat_axis=0, tiled=True
        ).reshape(slots, size)

    received = exchange(outgoing)

    flat = velocity.reshape(3, cells, columns)
    first, last = run_edges(flat)
    ahead = lax.ppermute(first, "gy", [((i + 1) % gy_size, i) for i in range(gy_size)])
    behind = lax.ppermute(last, "gy", [(i, (i + 1) % gy_size) for i in range(gy_size)])
    low_rows, high_rows, rim, edge = run_rim(rows, layers, run_lines(velocity), ahead, behind, received)

    up = [(i, (i + 1) % gx_size) for i in range(gx_size)]
    below_x = lax.ppermute(high_rows, "gx", up)
    above_x = lax.ppermute(low_rows, "gx", [(b, a) for a, b in up])
    u1 = run_first(layers, flat, edge, received)
    fluid, replies, _, near_dw = run_last(layers, NEAR, u1, rim, below_x, above_x, received, dw)
    moved = run_gather(pts, dest, exchange(replies), near_dw, dw)
    return fluid.reshape(3, layers, rows, columns), moved.transpose(1, 0, 2)


def solution(mesh):
    placed = (
        P(None, None, "gx", "gy"),
        P(("gx", "gy"), None, None),
        P(("gx", "gy")),
        P(("gx", "gy"), None),
        P(("gx", "gy"), None, None, None),
        P(("gx", "gy"), None, None),
        P(("gx", "gy"), None),
    )
    return jax.shard_map(
        shards,
        mesh=mesh,
        in_specs=placed,
        out_specs=(P(None, None, "gx", "gy"), P(("gx", "gy"), None, None)),
        check_vma=False,
    )
```

```python
import functools

import jax
import jax.numpy as jnp
from jax import lax
from jax.experimental import pallas as pl
from jax.experimental.pallas import tpu as pltpu
from jax.sharding import PartitionSpec as P

viscosity = 0.1
transport_rate = 0.1
force_step = 0.5
fiber_step = 0.25

F32 = jnp.float32
BF16 = jnp.bfloat16
LANES = 128
BELOW, ABOVE = 2, 10
NEAR = 1


def dot(a, b):
    return jnp.dot(a, b, preferred_element_type=F32)


def iota(shape, axis):
    return lax.broadcasted_iota(jnp.int32, shape, axis)


def spread_kernel(
    gy_size, slots, pts_hbm, stiff_hbm, links_hbm, owners_hbm, patch_slots_hbm, dw_hbm, out, dest_out,
    dw, force, rows, choose, pts, stiff, links, owners, patch_slots, sems,
):
    blocks, points = links.shape
    inter = owners.shape[1]
    entries = blocks * inter
    patch = rows.shape[2]
    small = [
        (pts_hbm, pts), (stiff_hbm, stiff), (links_hbm, links), (owners_hbm, owners), (patch_slots_hbm, patch_slots)
    ]
    small = [pltpu.make_async_copy(a, b, sems.at[blocks + i]) for i, (a, b) in enumerate(small)]
    for copy in small + [pltpu.make_async_copy(dw_hbm.at[b], dw.at[b], sems.at[b]) for b in range(blocks)]:
        copy.start()
    for copy in small:
        copy.wait()
    partner = lax.rem(iota((blocks, points), 1) + links[...], points)
    for c in range(3):
        own = pts[c]
        force[c] = jnp.take_along_axis(own, partner, axis=1) - own

    pick_block = (iota((entries, blocks), 0) // inter == iota((entries, blocks), 1)).astype(F32).astype(BF16)
    pick_k = lax.rem(iota((entries, inter), 0), inter) == iota((entries, inter), 1)

    def as_column(table):
        spread_rows = dot(pick_block, table.astype(F32).astype(BF16))
        return jnp.sum(jnp.where(pick_k, spread_rows, 0.0), axis=1, keepdims=True)

    owner = as_column(owners[...])
    code = patch_slots[...] + 1
    high, low = as_column(code // 32), as_column(lax.rem(code, 32))
    owner_wide = jnp.broadcast_to(owner, (entries, LANES))
    owner_row = jnp.transpose(
        jnp.concatenate([owner_wide, jnp.zeros((LANES - entries, LANES), F32)], axis=0)
    )[:entries, :entries]
    same = (owner_wide[:, :entries] == owner_row) & (iota((entries, entries), 1) < iota((entries, entries), 0))
    rank = jnp.sum(jnp.where(same, 1.0, 0.0), axis=1, keepdims=True)
    dest_wide = jnp.broadcast_to(owner * 2.0 + rank, (entries, LANES))
    dest_out[...] = dest_wide
    padded = jnp.concatenate([dest_wide, jnp.full((LANES - entries, LANES), -8.0, F32)], axis=0)
    dest_row = jnp.transpose(padded)[0:1, :entries].astype(jnp.int32)
    position = lax.rem(dest_row // 2, gy_size)
    slot = iota((slots, entries), 0)
    choose[0] = (slot == dest_row).astype(F32).astype(BF16)
    choose[1] = ((slot == dest_row + 2) & (position < gy_size - 1)).astype(F32).astype(BF16)
    choose[2] = ((slot == dest_row - 2) & (position > 0)).astype(F32).astype(BF16)
    lane = iota((entries, LANES), 1)

    def digits(at):
        return jnp.where(lane == at, high, 0.0) + jnp.where(lane == at + 1, low, 0.0)

    own_head, above_head, below_head = digits(0), digits(BELOW), digits(ABOVE)
    group = iota((inter, inter * points), 0)
    column = iota((inter, inter * points), 1) // points

    @pl.loop(0, blocks)
    def _(b):
        stiffness = stiff[b]
        parts = []
        for c in range(3):
            row = (stiffness * force[c, pl.ds(b, 1), :]).astype(BF16).astype(F32)
            wide = jnp.concatenate([jnp.broadcast_to(row, (inter, points))] * inter, axis=1)
            parts.append(jnp.where(group == column, wide, 0.0))
        parts.append(jnp.zeros_like(parts[0]))
        pltpu.make_async_copy(dw_hbm.at[b], dw.at[b], sems.at[b]).wait()
        spread = dot(jnp.concatenate(parts, axis=0).astype(BF16), dw[b])
        for c in range(3):
            rows[c, pl.ds(pl.multiple_of(b * inter, inter), inter), :] = spread[c * inter : (c + 1) * inter]

    for c in range(3):
        tail = pltpu.roll(rows[c, :, patch - LANES :], BELOW + 4 + 2 * c, axis=1)
        at = BELOW + 2 + 2 * c
        above_head += jnp.where((lane == at) | (lane == at + 1), tail, 0.0)
        at = ABOVE + 2 + 2 * c
        start = pltpu.roll(rows[c, :, :LANES], at, axis=1)
        below_head += jnp.where((lane == at) | (lane == at + 1), start, 0.0)
        out[:, c * patch : (c + 1) * patch] = dot(choose[0], rows[c].astype(BF16)).astype(BF16)
    head = dot(choose[0], own_head.astype(BF16))
    head += dot(choose[1], above_head.astype(BF16))
    head += dot(choose[2], below_head.astype(BF16))
    out[:, 3 * patch :] = head.astype(BF16)


def edge_kernel(velocity, first, last, start, end, sems):
    patch = velocity.shape[2]
    loads = []
    for c in range(3):
        for i, (to, lane) in enumerate(((start, 0), (end, patch - LANES))):
            loads.append(pltpu.make_async_copy(velocity.at[c, :, pl.ds(lane, LANES)], to.at[c], sems.at[2 * c + i]))
    for load in loads:
        load.start()
    row, lane = iota((16, LANES), 0), iota((16, LANES), 1)
    across = (((1,), (1,)), ((), ()))
    sums = [0.0, 0.0]
    for c in range(3):
        for i, (tile, at) in enumerate(((start, 0), (end, LANES - 2))):
            loads[2 * c + i].wait()
            pick = ((row - 2 * c == lane - at) & (lane >= at) & (lane < at + 2)).astype(F32).astype(BF16)
            sums[i] += lax.dot_general(pick, tile[c].astype(BF16), across, preferred_element_type=F32)
    first[...] = sums[0][:8]
    last[...] = sums[1][:8]


def line_kernel(velocity, out, lines, sems):
    layers, rows, patch = velocity.shape[1:]
    loads = []
    for i, x in enumerate((0, rows - 8)):
        for t in range(patch // LANES):
            part = velocity.at[:, :, pl.ds(x, 8), pl.ds(t * LANES, LANES)]
            loads.append(pltpu.make_async_copy(part, lines.at[i, t], sems.at[len(loads)]))
    for load in loads:
        load.start()
    for i in range(2):
        for t in range(patch // LANES):
            loads[i * (patch // LANES) + t].wait()
            for c in range(3):
                for j in range(2):
                    at = (2 * i + j) * layers
                    out[c, at : at + layers, t * LANES : (t + 1) * LANES] = lines[i, t, c, :, 6 * i + j, :]


class Arrived:
    def __init__(self, received, patch):
        self.received, self.patch = received, patch
        slots = received.shape[0]
        head = received[:, 3 * patch :].astype(F32)
        head_t = jnp.transpose(head)
        lane = iota((slots, LANES), 1)
        self.tails, self.starts = [], []
        for c in range(3):
            tail = pltpu.roll(head, LANES - 4 - BELOW - 2 * c, axis=1)
            self.tails.append(jnp.where(lane >= LANES - 2, tail, 0.0).astype(BF16))
            start = pltpu.roll(head, LANES - (ABOVE + 2 + 2 * c), axis=1)
            self.starts.append(jnp.where(lane < 2, start, 0.0).astype(BF16))
        self.slots = [
            (head_t[at : at + 1] * 32.0 + head_t[at + 1 : at + 2] - 1.0).astype(jnp.int32) for at in (0, BELOW, ABOVE)
        ]

    def choose(self, row):
        return [(row == slot).astype(F32).astype(BF16) for slot in self.slots]

    def force(self, chosen, c):
        return force_step * dot(chosen[0], self.received[:, c * self.patch : (c + 1) * self.patch])

    def edges(self, chosen):
        tails, starts = jnp.concatenate(self.tails, axis=1), jnp.concatenate(self.starts, axis=1)
        both = jnp.concatenate([tails, starts], axis=0)
        return force_step * dot(jnp.concatenate([chosen[1], chosen[2]], axis=1), both)


def rim_kernel(layer_rows, velocity, ahead, behind, received, low_rows, high_rows, rim, edges):
    layers, patch = low_rows.shape[1], velocity.shape[2]
    slots, cells, tiles = received.shape[0], ahead.shape[1], patch // LANES
    corners = [0.0, 0.0]
    z_lane = iota((layers, LANES), 1)

    sides = beside()
    from_ahead = jnp.where(sides[3] > 0.0, ahead[...], 0.0)
    from_behind = jnp.where(sides[2] > 0.0, behind[...], 0.0)
    turned = jnp.transpose(jnp.concatenate([from_ahead, from_behind, jnp.zeros((LANES - 16, cells), F32)], axis=0))
    turned = turned.astype(BF16)
    row, lane = iota((LANES, LANES), 0), iota((LANES, LANES), 1)
    for c in range(3):
        put = ((lane < 2) & (row == lane + 2 * c)) | ((lane >= LANES - 2) & (row == lane - (LANES - 2) + 8 + 2 * c))
        edges[c] = dot(turned, put.astype(F32).astype(BF16))

    arrived = Arrived(received, patch)
    row = iota((4 * layers, slots), 0)
    line, z = row // layers, lax.rem(row, layers)
    chosen = arrived.choose(z * layer_rows + jnp.where(line < 2, line, layer_rows - 4 + line))
    from_edges = arrived.edges(chosen)
    for c in range(3):
        main = velocity[c] + arrived.force(chosen, c)
        edge = from_edges[:, c * LANES : (c + 1) * LANES]
        for j in range(4):
            at = slice(j * layers, (j + 1) * layers)
            x = j if j < 2 else layer_rows - 4 + j
            side = edges[c, pl.ds(x, layers, stride=layer_rows), :] + edge[at]
            to = low_rows if j < 2 else high_rows
            for t in range(tiles):
                to[(c * 2 + j % 2) * tiles + t] = main[at, t * LANES : (t + 1) * LANES].astype(BF16)
            if j in (0, 3):
                for t in range(tiles):
                    rim[j // 3, c, t] = main[at, t * LANES : (t + 1) * LANES]
                rim[j // 3, c, tiles] = side
                corners[j // 3] += jnp.where(z_lane == 2 * c, pltpu.roll(side, 2 * c, axis=1), 0.0)
                corners[j // 3] += jnp.where(z_lane == 2 * c + 1, pltpu.roll(side, 2 * c + 2, axis=1), 0.0)
    low_rows[6 * tiles] = corners[0].astype(BF16)
    high_rows[6 * tiles] = corners[1].astype(BF16)


def update(centre, weights, c, east, west, north, south, up, down):
    (px, mx), (py, my), (pz, mz) = weights
    keep = 1.0 - 6.0 * viscosity
    return keep * centre[c] + px * east + mx * west + py * north + my * south + pz * up + mz * down


def mix(centre):
    return [(viscosity - transport_rate * v, viscosity + transport_rate * v) for v in centre]


def beside():
    flags = []
    for axis in ("gx", "gy"):
        at, size = lax.axis_index(axis), lax.axis_size(axis)
        flags += [jnp.where(at > 0, 1.0, 0.0).astype(F32), jnp.where(at < size - 1, 1.0, 0.0).astype(F32)]
    return flags


def edge_mask(sides):
    lane = iota((8, LANES), 1)
    return jnp.where(lane == 0, sides[3], 0.0) + jnp.where(lane == LANES - 1, sides[2], 0.0)


def rows_at(z, x, rows):
    return pl.ds(pl.multiple_of(z * rows + x, 8), 8)


def shifted(v, ahead, behind, axis):
    size = v.shape[axis]
    at = iota(v.shape, axis)
    return (
        pltpu.roll(jnp.where(at == 0, ahead, v), size - 1, axis=axis),
        pltpu.roll(jnp.where(at == size - 1, behind, v), 1, axis=axis),
    )


def sweep_pair(source, layers, z, low_row, high_row, store, tiles):
    count, rows = source.shape[1], source.shape[2] // layers
    z1 = lax.rem(z + 1, layers)
    for z, up, down in ((z, z1, lax.rem(z + layers - 1, layers)), (z1, lax.rem(z + 2, layers), z)):
        for x in range(0, rows, 8):
            for t in range(tiles):
                here = rows_at(z, x, rows)
                centre = [source[c, t, here, :] for c in range(3)]
                weights = mix(centre)
                for c in range(3):
                    v = centre[c]
                    ahead = source[c, t, rows_at(z, x + 8, rows), :] if x + 8 < rows else high_row(c, t, z)
                    behind = source[c, t, rows_at(z, x - 8, rows), :] if x > 0 else low_row(c, t, z)
                    east, west = shifted(v, ahead, behind, 0)
                    north, south = shifted(v, source[c, (t + 1) % count, here, :], source[c, (t - 1) % count, here, :], 1)
                    above, below = source[c, t, rows_at(up, x, rows), :], source[c, t, rows_at(down, x, rows), :]
                    store(c, t, here, update(centre, weights, c, east, west, north, south, above, below))


def place_kernel(layers, velocity, edges, received, low_in, u0, low_rows, sems):
    count, cells = u0.shape[1:3]
    rows, tiles = cells // layers, count - 1
    depth, slots = 8, received.shape[0]
    part, steps = depth * rows, layers // depth

    def load(step, t):
        at = pl.ds(pl.multiple_of(step * part, part), part)
        return pltpu.make_async_copy(
            velocity.at[:, at, pl.ds(t * LANES, LANES)], u0.at[:, t, at], sems.at[step * tiles + t]
        )

    for step in range(steps):
        for t in range(tiles):
            load(step, t).start()
    arrived = Arrived(received, tiles * LANES)
    low_rows[...] = low_in[...]

    @pl.loop(0, steps)
    def _(step):
        at = pl.ds(pl.multiple_of(step * part, part), part)
        chosen = arrived.choose(iota((part, slots), 0) + step * part)
        for t in range(tiles):
            load(step, t).wait()
        from_edges = arrived.edges(chosen)
        for c in range(3):
            main = arrived.force(chosen, c)
            for t in range(tiles):
                u0[c, t, at, :] += main[:, t * LANES : (t + 1) * LANES]
            u0[c, tiles, at, :] = edges[c, at, :] + from_edges[:, c * LANES : (c + 1) * LANES]


def first_kernel(layers, u0, u1):
    count = u0.shape[1]
    mask = edge_mask(beside())

    def store(c, t, here, new):
        u1[c, t, here, :] = new * mask if t == count - 1 else new

    def nothing(c, t, z):
        return 0.0

    @pl.loop(0, layers // 2)
    def _(i):
        sweep_pair(u0, layers, 2 * i, nothing, nothing, store, count)


def last_kernel(
    layers, u1_in, rim, below_x, above_x, received, dw_hbm, fluid_hbm, replies, u1, near_dw, mid, halo, fluid, pick, sems
):
    count, cells = u1.shape[1:3]
    rows, tiles = cells // layers, count - 1
    patch, slots = tiles * LANES, received.shape[0]
    sides = beside()
    mask = edge_mask(sides)
    ahead = pltpu.make_async_copy(dw_hbm.at[pl.ds(0, near_dw.shape[0])], near_dw, sems.at[layers // 4])
    ahead.start()

    heads = received[:, 3 * patch :].astype(F32)
    slot = (heads[:, 0:1] * 32.0 + heads[:, 1:2] - 1.0).astype(jnp.int32)
    for first in range(0, cells, 256):
        pick[:, first : first + 256] = (iota((slots, 256), 1) + first == slot).astype(F32).astype(BF16)

    for side, source in enumerate((below_x, above_x)):
        for c in range(3):
            for j in range(2):
                for t in range(count):
                    if t < tiles:
                        arrived = source[(c * 2 + j) * tiles + t].astype(F32)
                    elif j == 1 - side:
                        corner = source[6 * tiles].astype(F32)
                        lane = iota(corner.shape, 1)
                        arrived = jnp.where(lane == 0, pltpu.roll(corner, (LANES - 2 * c) % LANES, axis=1), 0.0)
                        arrived += jnp.where(lane == LANES - 1, pltpu.roll(corner, LANES - 2 - 2 * c, axis=1), 0.0)
                    else:
                        continue
                    halo[side, c, j, t] = jnp.where(sides[side] > 0.0, arrived, 0.0)
    for side in range(2):
        near, row = 1 - side, (rows - 1) * side
        slope = -transport_rate if side else transport_rate
        for t in range(count):
            for g in range(0, layers, 8):
                at = slice(g, g + 8)
                after, before = (g + 8) % layers, (g - 8) % layers
                centre = [halo[side, c, near, t, at, :] for c in range(3)]
                weights = mix(centre)
                own = viscosity + slope * rim[side, 0, t, at, :]
                for c in range(3):
                    v = centre[c]
                    if t < tiles:
                        plane = halo.at[side, c, near]
                        inner, outer = rim[side, c, t, at, :], halo[side, c, side, t, at, :]
                        east, west = (outer, inner) if side else (inner, outer)
                        north, south = shifted(v, plane[(t + 1) % count, at, :], plane[(t - 1) % count, at, :], 1)
                        up, down = shifted(v, plane[t, after : after + 8, :], plane[t, before : before + 8, :], 0)
                        mid[side, c, t, at, :] = sides[side] * update(
                            centre, weights, c, east, west, north, south, up, down
                        )
                    term = own * v
                    strided = pl.ds(g * rows + row, 8, stride=rows)
                    u1[c, t, strided, :] += term * mask if t == tiles else term

    def store(c, t, here, new):
        fluid[c, here, t * LANES : (t + 1) * LANES] = new

    depth = 4

    def write(step):
        at = pl.ds(pl.multiple_of(step * depth * rows, depth * rows), depth * rows)
        return pltpu.make_async_copy(fluid.at[:, at], fluid_hbm.at[:, at], sems.at[step])

    @pl.loop(0, layers // depth)
    def _(step):
        @pl.loop(0, depth // 2)
        def _(i):
            sweep_pair(
                u1,
                layers,
                step * depth + 2 * i,
                lambda c, t, z: mid[0, c, t, pl.ds(z, 1), :],
                lambda c, t, z: mid[1, c, t, pl.ds(z, 1), :],
                store,
                tiles,
            )

        write(step).start()

    for c in range(3):
        replies[:, c * patch : (c + 1) * patch] = dot(pick[...], fluid[c].astype(BF16)).astype(BF16)
    for step in range(layers // depth):
        write(step).wait()
    ahead.wait()


def gather_kernel(pts, dest, returned, near_dw, dw_hbm, out, dw, picked, moved, sems):
    entries, slots = dest.shape[0], returned.shape[0]
    near, blocks, patch, points = near_dw.shape[0], dw.shape[0], dw.shape[2], pts.shape[2]
    inter = entries // blocks
    for b in range(near, blocks):
        pltpu.make_async_copy(dw_hbm.at[b], dw.at[b], sems.at[b]).start()
    to = dest[:, 0:1].astype(jnp.int32)
    pick = (iota((entries, slots), 1) == to).astype(F32).astype(BF16)
    for c in range(3):
        picked[c] = dot(pick, returned[:, c * patch : (c + 1) * patch])
    group = iota((inter, inter * points), 0)
    column = iota((inter, inter * points), 1) // points

    def block(b, weights):
        at = pl.ds(pl.multiple_of(b * inter, inter), inter)
        parts = [picked[c, at, :] for c in range(3)]
        parts.append(jnp.zeros((inter, patch), F32))
        cells = jnp.concatenate(parts, axis=0).astype(BF16)
        every = lax.dot_general(cells, weights, (((1,), (1,)), ((), ())), preferred_element_type=F32)
        for c in range(3):
            own = jnp.where(group == column, every[c * inter : (c + 1) * inter], 0.0)
            folded = own[:, :points]
            for k in range(1, inter):
                folded = folded + own[:, k * points : (k + 1) * points]
            moved[c, pl.ds(b, 1), :] = jnp.sum(folded, axis=0, keepdims=True)

    @pl.loop(0, near)
    def _(b):
        block(b, near_dw[b])

    @pl.loop(near, blocks)
    def _(b):
        pltpu.make_async_copy(dw_hbm.at[b], dw.at[b], sems.at[b]).wait()
        block(b, dw[b])

    for c in range(3):
        out[c] = pts[c] + fiber_step * moved[c]


def in_hbm(x):
    return pltpu.with_memory_space_constraint(x, pltpu.HBM)


def params(limit):
    return pltpu.CompilerParams(vmem_limit_bytes=limit << 20)


def cost(flops, size):
    return pl.CostEstimate(flops=flops, bytes_accessed=size << 20, transcendentals=0)


VMEM = pl.BlockSpec(memory_space=pltpu.VMEM)
HBM = pl.BlockSpec(memory_space=pltpu.HBM)


def run_spread(gy_size, slots, pts, stiffness, links, owners, patch_slots, dw):
    blocks, points = links.shape
    inter, patch = owners.shape[1], dw.shape[2]
    entries = blocks * inter
    return pl.pallas_call(
        functools.partial(spread_kernel, gy_size, slots),
        in_specs=[HBM] * 6,
        out_specs=[VMEM, VMEM],
        out_shape=[
            jax.ShapeDtypeStruct((slots, 3 * patch + LANES), BF16),
            jax.ShapeDtypeStruct((entries, LANES), F32),
        ],
        scratch_shapes=[
            pltpu.VMEM(dw.shape, BF16),
            pltpu.VMEM((3, blocks, points), F32),
            pltpu.VMEM((3, entries, patch), F32),
            pltpu.VMEM((3, slots, entries), BF16),
            pltpu.VMEM((3, blocks, points), F32),
            pltpu.SMEM((blocks,), F32),
            pltpu.VMEM((blocks, points), jnp.int32),
            pltpu.VMEM((blocks, inter), jnp.int32),
            pltpu.VMEM((blocks, inter), jnp.int32),
            pltpu.SemaphoreType.DMA((blocks + 5,)),
        ],
        compiler_params=params(24),
        cost_estimate=cost(10**9, 9),
        name="spread",
    )(*[in_hbm(x) for x in (pts, stiffness, links, owners, patch_slots, dw)])


def run_edges(velocity):
    cells = velocity.shape[1]
    return pl.pallas_call(
        edge_kernel,
        in_specs=[HBM],
        out_specs=[VMEM, VMEM],
        out_shape=[jax.ShapeDtypeStruct((8, cells), F32)] * 2,
        scratch_shapes=[pltpu.VMEM((3, cells, LANES), F32)] * 2 + [pltpu.SemaphoreType.DMA((6,))],
        compiler_params=params(24),
        cost_estimate=cost(10**8, 3),
        name="edges",
    )(in_hbm(velocity))


def run_lines(velocity):
    layers, patch = velocity.shape[1], velocity.shape[3]
    tiles = patch // LANES
    return pl.pallas_call(
        line_kernel,
        in_specs=[HBM],
        out_specs=VMEM,
        out_shape=jax.ShapeDtypeStruct((3, 4 * layers, patch), F32),
        scratch_shapes=[pltpu.VMEM((2, tiles, 3, layers, 8, LANES), F32), pltpu.SemaphoreType.DMA((2 * tiles,))],
        compiler_params=params(24),
        cost_estimate=cost(10**8, 3),
        name="lines",
    )(in_hbm(velocity))


def run_rim(layer_rows, layers, rim_velocity, ahead, behind, received):
    patch, cells = rim_velocity.shape[2], ahead.shape[1]
    side = (6 * (patch // LANES) + 1, layers, LANES)
    return pl.pallas_call(
        functools.partial(rim_kernel, layer_rows),
        in_specs=[VMEM] * 4,
        out_specs=[VMEM] * 4,
        out_shape=[
            jax.ShapeDtypeStruct(side, BF16),
            jax.ShapeDtypeStruct(side, BF16),
            jax.ShapeDtypeStruct((2, 3, patch // LANES + 1, layers, LANES), F32),
            jax.ShapeDtypeStruct((3, cells, LANES), F32),
        ],
        compiler_params=params(24),
        cost_estimate=cost(10**8, 3),
        name="rim",
    )(rim_velocity, ahead, behind, received)


def run_place(layers, velocity, edge, received, low_rows):
    cells, patch = velocity.shape[1:]
    return pl.pallas_call(
        functools.partial(place_kernel, layers),
        in_specs=[HBM, VMEM, VMEM, VMEM],
        out_specs=[VMEM, VMEM],
        out_shape=[
            jax.ShapeDtypeStruct((3, patch // LANES + 1, cells, LANES), F32),
            jax.ShapeDtypeStruct(low_rows.shape, BF16),
        ],
        scratch_shapes=[pltpu.SemaphoreType.DMA((layers // 8 * (patch // LANES),))],
        compiler_params=params(24),
        cost_estimate=cost(10**9, 8),
        name="place",
    )(in_hbm(velocity), edge, received, low_rows)


def run_first(layers, u0):
    return pl.pallas_call(
        functools.partial(first_kernel, layers),
        in_specs=[VMEM],
        out_specs=VMEM,
        out_shape=jax.ShapeDtypeStruct(u0.shape, F32),
        compiler_params=params(24),
        cost_estimate=cost(2 * 10**9, 24),
        name="sweep_first",
    )(u0)


def run_last(layers, near, u1, rim, below_x, above_x, received, dw):
    count, cells = u1.shape[1:3]
    patch, slots = (count - 1) * LANES, received.shape[0]
    return pl.pallas_call(
        functools.partial(last_kernel, layers),
        in_specs=[VMEM] * 5 + [HBM],
        out_specs=[HBM, VMEM, VMEM, VMEM],
        out_shape=[
            jax.ShapeDtypeStruct((3, cells, patch), F32),
            jax.ShapeDtypeStruct((slots, 3 * patch), BF16),
            jax.ShapeDtypeStruct(u1.shape, F32),
            jax.ShapeDtypeStruct((near, *dw.shape[1:]), BF16),
        ],
        scratch_shapes=[
            pltpu.VMEM((2, 3, count - 1, layers, LANES), F32),
            pltpu.VMEM((2, 3, 2, count, layers, LANES), F32),
            pltpu.VMEM((3, cells, patch), F32),
            pltpu.VMEM((slots, cells), BF16),
            pltpu.SemaphoreType.DMA((layers // 4 + 1,)),
        ],
        input_output_aliases={0: 2},
        compiler_params=params(34),
        cost_estimate=cost(2 * 10**9, 16),
        name="sweep_last",
    )(u1, rim, below_x, above_x, received, in_hbm(dw))


def run_gather(pts, dest, returned, near_dw, dw):
    blocks, patch = dw.shape[0], dw.shape[2]
    return pl.pallas_call(
        gather_kernel,
        in_specs=[VMEM] * 4 + [HBM],
        out_specs=VMEM,
        out_shape=jax.ShapeDtypeStruct(pts.shape, F32),
        scratch_shapes=[
            pltpu.VMEM(dw.shape, BF16),
            pltpu.VMEM((3, dest.shape[0], patch), F32),
            pltpu.VMEM(pts.shape, F32),
            pltpu.SemaphoreType.DMA((blocks,)),
        ],
        compiler_params=params(24),
        cost_estimate=cost(10**9, 9),
        name="interp",
    )(pts, dest, returned, near_dw, in_hbm(dw))


def shards(velocity, fiber_points, stiffness, links, delta_weights, owners, patch_slots):
    blocks, inter, points, patch = delta_weights.shape
    layers, rows, columns = velocity.shape[1:]
    gx_size, gy_size = lax.axis_size("gx"), lax.axis_size("gy")
    devices = gx_size * gy_size
    slots, cells = devices * 2, layers * rows
    pts = fiber_points.transpose(1, 0, 2)
    dw = delta_weights.reshape(blocks, inter * points, patch)
    outgoing, dest = run_spread(
        gy_size, slots, pts, stiffness, links, owners.reshape(blocks, inter), patch_slots, dw
    )

    def exchange(rows_out):
        size = rows_out.shape[1]
        return lax.all_to_all(
            rows_out.reshape(devices, 2, size), ("gx", "gy"), split_axis=0, concat_axis=0, tiled=True
        ).reshape(slots, size)

    received = exchange(outgoing)

    flat = velocity.reshape(3, cells, columns)
    first, last = run_edges(flat)
    ahead = lax.ppermute(first, "gy", [((i + 1) % gy_size, i) for i in range(gy_size)])
    behind = lax.ppermute(last, "gy", [(i, (i + 1) % gy_size) for i in range(gy_size)])
    low_rows, high_rows, rim, edge = run_rim(rows, layers, run_lines(velocity), ahead, behind, received)

    up = [(i, (i + 1) % gx_size) for i in range(gx_size)]
    below_x = lax.ppermute(high_rows, "gx", up)
    u0, low_rows = run_place(layers, flat, edge, received, low_rows)
    above_x = lax.ppermute(low_rows, "gx", [(b, a) for a, b in up])
    u1 = run_first(layers, u0)
    fluid, replies, _, near_dw = run_last(layers, NEAR, u1, rim, below_x, above_x, received, dw)
    moved = run_gather(pts, dest, exchange(replies), near_dw, dw)
    return fluid.reshape(3, layers, rows, columns), moved.transpose(1, 0, 2)


def solution(mesh):
    placed = (
        P(None, None, "gx", "gy"),
        P(("gx", "gy"), None, None),
        P(("gx", "gy")),
        P(("gx", "gy"), None),
        P(("gx", "gy"), None, None, None),
        P(("gx", "gy"), None, None),
        P(("gx", "gy"), None),
    )
    return jax.shard_map(
        shards,
        mesh=mesh,
        in_specs=placed,
        out_specs=(P(None, None, "gx", "gy"), P(("gx", "gy"), None, None)),
        check_vma=False,
    )
```

```python
import functools

import jax
import jax.numpy as jnp
from jax import lax
from jax.experimental import pallas as pl
from jax.experimental.pallas import tpu as pltpu
from jax.sharding import PartitionSpec as P

viscosity = 0.1
transport_rate = 0.1
force_step = 0.5
fiber_step = 0.25

F32 = jnp.float32
BF16 = jnp.bfloat16
LANES = 128
BELOW, ABOVE = 2, 10
NEAR = 1


def dot(a, b):
    return jnp.dot(a, b, preferred_element_type=F32)


def iota(shape, axis):
    return lax.broadcasted_iota(jnp.int32, shape, axis)


def spread_kernel(
    gy_size, slots, pts_hbm, stiff_hbm, links_hbm, owners_hbm, patch_slots_hbm, dw_hbm, out, dest_out,
    dw, force, rows, choose, pts, stiff, links, owners, patch_slots, sems,
):
    blocks, points = links.shape
    inter = owners.shape[1]
    entries = blocks * inter
    patch = rows.shape[2]
    small = [
        (pts_hbm, pts), (stiff_hbm, stiff), (links_hbm, links), (owners_hbm, owners), (patch_slots_hbm, patch_slots)
    ]
    small = [pltpu.make_async_copy(a, b, sems.at[blocks + i]) for i, (a, b) in enumerate(small)]
    for copy in small + [pltpu.make_async_copy(dw_hbm.at[b], dw.at[b], sems.at[b]) for b in range(blocks)]:
        copy.start()
    for copy in small:
        copy.wait()
    partner = lax.rem(iota((blocks, points), 1) + links[...], points)
    for c in range(3):
        own = pts[c]
        force[c] = jnp.take_along_axis(own, partner, axis=1) - own

    pick_block = (iota((entries, blocks), 0) // inter == iota((entries, blocks), 1)).astype(F32).astype(BF16)
    pick_k = lax.rem(iota((entries, inter), 0), inter) == iota((entries, inter), 1)

    def as_column(table):
        spread_rows = dot(pick_block, table.astype(F32).astype(BF16))
        return jnp.sum(jnp.where(pick_k, spread_rows, 0.0), axis=1, keepdims=True)

    owner = as_column(owners[...])
    code = patch_slots[...] + 1
    high, low = as_column(code // 32), as_column(lax.rem(code, 32))
    owner_wide = jnp.broadcast_to(owner, (entries, LANES))
    owner_row = jnp.transpose(
        jnp.concatenate([owner_wide, jnp.zeros((LANES - entries, LANES), F32)], axis=0)
    )[:entries, :entries]
    same = (owner_wide[:, :entries] == owner_row) & (iota((entries, entries), 1) < iota((entries, entries), 0))
    rank = jnp.sum(jnp.where(same, 1.0, 0.0), axis=1, keepdims=True)
    dest_wide = jnp.broadcast_to(owner * 2.0 + rank, (entries, LANES))
    dest_out[...] = dest_wide
    padded = jnp.concatenate([dest_wide, jnp.full((LANES - entries, LANES), -8.0, F32)], axis=0)
    dest_row = jnp.transpose(padded)[0:1, :entries].astype(jnp.int32)
    position = lax.rem(dest_row // 2, gy_size)
    slot = iota((slots, entries), 0)
    choose[0] = (slot == dest_row).astype(F32).astype(BF16)
    choose[1] = ((slot == dest_row + 2) & (position < gy_size - 1)).astype(F32).astype(BF16)
    choose[2] = ((slot == dest_row - 2) & (position > 0)).astype(F32).astype(BF16)
    lane = iota((entries, LANES), 1)

    def digits(at):
        return jnp.where(lane == at, high, 0.0) + jnp.where(lane == at + 1, low, 0.0)

    own_head, above_head, below_head = digits(0), digits(BELOW), digits(ABOVE)
    group = iota((inter, inter * points), 0)
    column = iota((inter, inter * points), 1) // points

    @pl.loop(0, blocks)
    def _(b):
        stiffness = stiff[b]
        parts = []
        for c in range(3):
            row = (stiffness * force[c, pl.ds(b, 1), :]).astype(BF16).astype(F32)
            wide = jnp.concatenate([jnp.broadcast_to(row, (inter, points))] * inter, axis=1)
            parts.append(jnp.where(group == column, wide, 0.0))
        parts.append(jnp.zeros_like(parts[0]))
        pltpu.make_async_copy(dw_hbm.at[b], dw.at[b], sems.at[b]).wait()
        spread = dot(jnp.concatenate(parts, axis=0).astype(BF16), dw[b])
        for c in range(3):
            rows[c, pl.ds(pl.multiple_of(b * inter, inter), inter), :] = spread[c * inter : (c + 1) * inter]

    for c in range(3):
        tail = pltpu.roll(rows[c, :, patch - LANES :], BELOW + 4 + 2 * c, axis=1)
        at = BELOW + 2 + 2 * c
        above_head += jnp.where((lane == at) | (lane == at + 1), tail, 0.0)
        at = ABOVE + 2 + 2 * c
        start = pltpu.roll(rows[c, :, :LANES], at, axis=1)
        below_head += jnp.where((lane == at) | (lane == at + 1), start, 0.0)
        out[:, c * patch : (c + 1) * patch] = dot(choose[0], rows[c].astype(BF16)).astype(BF16)
    head = dot(choose[0], own_head.astype(BF16))
    head += dot(choose[1], above_head.astype(BF16))
    head += dot(choose[2], below_head.astype(BF16))
    out[:, 3 * patch :] = head.astype(BF16)


def edge_kernel(velocity, first, last, start, end, sems):
    patch = velocity.shape[2]
    loads = []
    for c in range(3):
        for i, (to, lane) in enumerate(((start, 0), (end, patch - LANES))):
            loads.append(pltpu.make_async_copy(velocity.at[c, :, pl.ds(lane, LANES)], to.at[c], sems.at[2 * c + i]))
    for load in loads:
        load.start()
    row, lane = iota((16, LANES), 0), iota((16, LANES), 1)
    across = (((1,), (1,)), ((), ()))
    sums = [0.0, 0.0]
    for c in range(3):
        for i, (tile, at) in enumerate(((start, 0), (end, LANES - 2))):
            loads[2 * c + i].wait()
            pick = ((row - 2 * c == lane - at) & (lane >= at) & (lane < at + 2)).astype(F32).astype(BF16)
            sums[i] += lax.dot_general(pick, tile[c].astype(BF16), across, preferred_element_type=F32)
    first[...] = sums[0][:8]
    last[...] = sums[1][:8]


def line_kernel(velocity, out, lines, sems):
    layers, rows, patch = velocity.shape[1:]
    loads = []
    for i, x in enumerate((0, rows - 8)):
        for t in range(patch // LANES):
            part = velocity.at[:, :, pl.ds(x, 8), pl.ds(t * LANES, LANES)]
            loads.append(pltpu.make_async_copy(part, lines.at[i, t], sems.at[len(loads)]))
    for load in loads:
        load.start()
    for i in range(2):
        for t in range(patch // LANES):
            loads[i * (patch // LANES) + t].wait()
            for c in range(3):
                for j in range(2):
                    at = (2 * i + j) * layers
                    out[c, at : at + layers, t * LANES : (t + 1) * LANES] = lines[i, t, c, :, 6 * i + j, :]


class Arrived:
    def __init__(self, received, patch):
        self.received, self.patch = received, patch
        slots = received.shape[0]
        head = received[:, 3 * patch :].astype(F32)
        head_t = jnp.transpose(head)
        lane = iota((slots, LANES), 1)
        self.tails, self.starts = [], []
        for c in range(3):
            tail = pltpu.roll(head, LANES - 4 - BELOW - 2 * c, axis=1)
            self.tails.append(jnp.where(lane >= LANES - 2, tail, 0.0).astype(BF16))
            start = pltpu.roll(head, LANES - (ABOVE + 2 + 2 * c), axis=1)
            self.starts.append(jnp.where(lane < 2, start, 0.0).astype(BF16))
        self.slots = [
            (head_t[at : at + 1] * 32.0 + head_t[at + 1 : at + 2] - 1.0).astype(jnp.int32) for at in (0, BELOW, ABOVE)
        ]

    def choose(self, row):
        return [(row == slot).astype(F32).astype(BF16) for slot in self.slots]

    def force(self, chosen, c):
        return force_step * dot(chosen[0], self.received[:, c * self.patch : (c + 1) * self.patch])

    def edges(self, chosen):
        tails, starts = jnp.concatenate(self.tails, axis=1), jnp.concatenate(self.starts, axis=1)
        both = jnp.concatenate([tails, starts], axis=0)
        return force_step * dot(jnp.concatenate([chosen[1], chosen[2]], axis=1), both)


def rim_kernel(layer_rows, velocity, ahead, behind, received, low_rows, high_rows, rim, edges):
    layers, patch = low_rows.shape[1], velocity.shape[2]
    slots, cells, tiles = received.shape[0], ahead.shape[1], patch // LANES
    corners = [0.0, 0.0]
    z_lane = iota((layers, LANES), 1)

    sides = beside()
    from_ahead = jnp.where(sides[3] > 0.0, ahead[...], 0.0)
    from_behind = jnp.where(sides[2] > 0.0, behind[...], 0.0)
    turned = jnp.transpose(jnp.concatenate([from_ahead, from_behind, jnp.zeros((LANES - 16, cells), F32)], axis=0))
    turned = turned.astype(BF16)
    row, lane = iota((LANES, LANES), 0), iota((LANES, LANES), 1)
    for c in range(3):
        put = ((lane < 2) & (row == lane + 2 * c)) | ((lane >= LANES - 2) & (row == lane - (LANES - 2) + 8 + 2 * c))
        edges[c] = dot(turned, put.astype(F32).astype(BF16))

    arrived = Arrived(received, patch)
    row = iota((4 * layers, slots), 0)
    line, z = row // layers, lax.rem(row, layers)
    chosen = arrived.choose(z * layer_rows + jnp.where(line < 2, line, layer_rows - 4 + line))
    from_edges = arrived.edges(chosen)
    for c in range(3):
        main = velocity[c] + arrived.force(chosen, c)
        edge = from_edges[:, c * LANES : (c + 1) * LANES]
        for j in range(4):
            at = slice(j * layers, (j + 1) * layers)
            x = j if j < 2 else layer_rows - 4 + j
            side = edges[c, pl.ds(x, layers, stride=layer_rows), :] + edge[at]
            to = low_rows if j < 2 else high_rows
            for t in range(tiles):
                to[(c * 2 + j % 2) * tiles + t] = main[at, t * LANES : (t + 1) * LANES].astype(BF16)
            if j in (0, 3):
                for t in range(tiles):
                    rim[j // 3, c, t] = main[at, t * LANES : (t + 1) * LANES]
                rim[j // 3, c, tiles] = side
                corners[j // 3] += jnp.where(z_lane == 2 * c, pltpu.roll(side, 2 * c, axis=1), 0.0)
                corners[j // 3] += jnp.where(z_lane == 2 * c + 1, pltpu.roll(side, 2 * c + 2, axis=1), 0.0)
    low_rows[6 * tiles] = corners[0].astype(BF16)
    high_rows[6 * tiles] = corners[1].astype(BF16)


def update(centre, weights, c, east, west, north, south, up, down):
    (px, mx), (py, my), (pz, mz) = weights
    keep = 1.0 - 6.0 * viscosity
    return keep * centre[c] + px * east + mx * west + py * north + my * south + pz * up + mz * down


def mix(centre):
    return [(viscosity - transport_rate * v, viscosity + transport_rate * v) for v in centre]


def beside():
    flags = []
    for axis in ("gx", "gy"):
        at, size = lax.axis_index(axis), lax.axis_size(axis)
        flags += [jnp.where(at > 0, 1.0, 0.0).astype(F32), jnp.where(at < size - 1, 1.0, 0.0).astype(F32)]
    return flags


def edge_mask(sides):
    lane = iota((8, LANES), 1)
    return jnp.where(lane == 0, sides[3], 0.0) + jnp.where(lane == LANES - 1, sides[2], 0.0)


def rows_at(z, x, rows):
    return pl.ds(pl.multiple_of(z * rows + x, 8), 8)


def shifted(v, ahead, behind, axis):
    size = v.shape[axis]
    at = iota(v.shape, axis)
    return (
        pltpu.roll(jnp.where(at == 0, ahead, v), size - 1, axis=axis),
        pltpu.roll(jnp.where(at == size - 1, behind, v), 1, axis=axis),
    )


def sweep_pair(source, layers, z, low_row, high_row, store, tiles):
    count, rows = source.shape[1], source.shape[2] // layers
    z1 = lax.rem(z + 1, layers)
    for z, up, down in ((z, z1, lax.rem(z + layers - 1, layers)), (z1, lax.rem(z + 2, layers), z)):
        for x in range(0, rows, 8):
            for t in range(tiles):
                here = rows_at(z, x, rows)
                centre = [source[c, t, here, :] for c in range(3)]
                weights = mix(centre)
                for c in range(3):
                    v = centre[c]
                    ahead = source[c, t, rows_at(z, x + 8, rows), :] if x + 8 < rows else high_row(c, t, z)
                    behind = source[c, t, rows_at(z, x - 8, rows), :] if x > 0 else low_row(c, t, z)
                    east, west = shifted(v, ahead, behind, 0)
                    north, south = shifted(v, source[c, (t + 1) % count, here, :], source[c, (t - 1) % count, here, :], 1)
                    above, below = source[c, t, rows_at(up, x, rows), :], source[c, t, rows_at(down, x, rows), :]
                    store(c, t, here, update(centre, weights, c, east, west, north, south, above, below))


def first_kernel(layers, velocity, edges, received, u1, u0, sems):
    count, cells = u0.shape[1:3]
    rows, tiles = cells // layers, count - 1
    depth, slots = 8, received.shape[0]
    part, steps = depth * rows, layers // depth

    def load(step, t):
        at = pl.ds(pl.multiple_of(step * part, part), part)
        return pltpu.make_async_copy(
            velocity.at[:, at, pl.ds(t * LANES, LANES)], u0.at[:, t, at], sems.at[step * tiles + t]
        )

    for step in range(steps):
        for t in range(tiles):
            load(step, t).start()
    arrived = Arrived(received, tiles * LANES)
    mask = edge_mask(beside())

    def store(c, t, here, new):
        u1[c, t, here, :] = new * mask if t == tiles else new

    def nothing(c, t, z):
        return 0.0

    @pl.loop(0, steps)
    def _(step):
        at = pl.ds(pl.multiple_of(step * part, part), part)
        chosen = arrived.choose(iota((part, slots), 0) + step * part)
        for t in range(tiles):
            load(step, t).wait()
        from_edges = arrived.edges(chosen)
        for c in range(3):
            main = arrived.force(chosen, c)
            for t in range(tiles):
                u0[c, t, at, :] += main[:, t * LANES : (t + 1) * LANES]
            u0[c, tiles, at, :] = edges[c, at, :] + from_edges[:, c * LANES : (c + 1) * LANES]

        @pl.loop(jnp.where(step == 0, 1, 0), jnp.where(step == steps - 1, depth // 2 + 1, depth // 2))
        def _(i):
            sweep_pair(u0, layers, step * depth - 1 + 2 * i, nothing, nothing, store, count)


def last_kernel(
    layers, u1_in, rim, below_x, above_x, received, dw_hbm, fluid_hbm, replies, u1, near_dw, mid, halo, fluid, pick, sems
):
    count, cells = u1.shape[1:3]
    rows, tiles = cells // layers, count - 1
    patch, slots = tiles * LANES, received.shape[0]
    sides = beside()
    mask = edge_mask(sides)
    ahead = pltpu.make_async_copy(dw_hbm.at[pl.ds(0, near_dw.shape[0])], near_dw, sems.at[layers // 4])
    ahead.start()

    heads = received[:, 3 * patch :].astype(F32)
    slot = (heads[:, 0:1] * 32.0 + heads[:, 1:2] - 1.0).astype(jnp.int32)
    for first in range(0, cells, 256):
        pick[:, first : first + 256] = (iota((slots, 256), 1) + first == slot).astype(F32).astype(BF16)

    for side, source in enumerate((below_x, above_x)):
        for c in range(3):
            for j in range(2):
                for t in range(count):
                    if t < tiles:
                        arrived = source[(c * 2 + j) * tiles + t].astype(F32)
                    elif j == 1 - side:
                        corner = source[6 * tiles].astype(F32)
                        lane = iota(corner.shape, 1)
                        arrived = jnp.where(lane == 0, pltpu.roll(corner, (LANES - 2 * c) % LANES, axis=1), 0.0)
                        arrived += jnp.where(lane == LANES - 1, pltpu.roll(corner, LANES - 2 - 2 * c, axis=1), 0.0)
                    else:
                        continue
                    halo[side, c, j, t] = jnp.where(sides[side] > 0.0, arrived, 0.0)
    for side in range(2):
        near, row = 1 - side, (rows - 1) * side
        slope = -transport_rate if side else transport_rate
        for t in range(count):
            for g in range(0, layers, 8):
                at = slice(g, g + 8)
                after, before = (g + 8) % layers, (g - 8) % layers
                centre = [halo[side, c, near, t, at, :] for c in range(3)]
                weights = mix(centre)
                own = viscosity + slope * rim[side, 0, t, at, :]
                for c in range(3):
                    v = centre[c]
                    if t < tiles:
                        plane = halo.at[side, c, near]
                        inner, outer = rim[side, c, t, at, :], halo[side, c, side, t, at, :]
                        east, west = (outer, inner) if side else (inner, outer)
                        north, south = shifted(v, plane[(t + 1) % count, at, :], plane[(t - 1) % count, at, :], 1)
                        up, down = shifted(v, plane[t, after : after + 8, :], plane[t, before : before + 8, :], 0)
                        mid[side, c, t, at, :] = sides[side] * update(
                            centre, weights, c, east, west, north, south, up, down
                        )
                    term = own * v
                    strided = pl.ds(g * rows + row, 8, stride=rows)
                    u1[c, t, strided, :] += term * mask if t == tiles else term

    def store(c, t, here, new):
        fluid[c, here, t * LANES : (t + 1) * LANES] = new

    depth = 4

    def write(step):
        at = pl.ds(pl.multiple_of(step * depth * rows, depth * rows), depth * rows)
        return pltpu.make_async_copy(fluid.at[:, at], fluid_hbm.at[:, at], sems.at[step])

    @pl.loop(0, layers // depth)
    def _(step):
        for i in range(depth // 2):
            sweep_pair(
                u1,
                layers,
                step * depth + 2 * i,
                lambda c, t, z: mid[0, c, t, pl.ds(z, 1), :],
                lambda c, t, z: mid[1, c, t, pl.ds(z, 1), :],
                store,
                tiles,
            )

        write(step).start()

    for c in range(3):
        replies[:, c * patch : (c + 1) * patch] = dot(pick[...], fluid[c].astype(BF16)).astype(BF16)
    for step in range(layers // depth):
        write(step).wait()
    ahead.wait()


def gather_kernel(pts, dest, returned, near_dw, dw_hbm, out, dw, picked, moved, sems):
    entries, slots = dest.shape[0], returned.shape[0]
    near, blocks, patch, points = near_dw.shape[0], dw.shape[0], dw.shape[2], pts.shape[2]
    inter = entries // blocks
    for b in range(near, blocks):
        pltpu.make_async_copy(dw_hbm.at[b], dw.at[b], sems.at[b]).start()
    to = dest[:, 0:1].astype(jnp.int32)
    pick = (iota((entries, slots), 1) == to).astype(F32).astype(BF16)
    for c in range(3):
        picked[c] = dot(pick, returned[:, c * patch : (c + 1) * patch])
    group = iota((inter, inter * points), 0)
    column = iota((inter, inter * points), 1) // points

    def block(b, weights):
        at = pl.ds(pl.multiple_of(b * inter, inter), inter)
        parts = [picked[c, at, :] for c in range(3)]
        parts.append(jnp.zeros((inter, patch), F32))
        cells = jnp.concatenate(parts, axis=0).astype(BF16)
        every = lax.dot_general(cells, weights, (((1,), (1,)), ((), ())), preferred_element_type=F32)
        for c in range(3):
            own = jnp.where(group == column, every[c * inter : (c + 1) * inter], 0.0)
            folded = own[:, :points]
            for k in range(1, inter):
                folded = folded + own[:, k * points : (k + 1) * points]
            moved[c, pl.ds(b, 1), :] = jnp.sum(folded, axis=0, keepdims=True)

    @pl.loop(0, near)
    def _(b):
        block(b, near_dw[b])

    @pl.loop(near, blocks)
    def _(b):
        pltpu.make_async_copy(dw_hbm.at[b], dw.at[b], sems.at[b]).wait()
        block(b, dw[b])

    for c in range(3):
        out[c] = pts[c] + fiber_step * moved[c]


def in_hbm(x):
    return pltpu.with_memory_space_constraint(x, pltpu.HBM)


def params(limit):
    return pltpu.CompilerParams(vmem_limit_bytes=limit << 20)


def cost(flops, size):
    return pl.CostEstimate(flops=flops, bytes_accessed=size << 20, transcendentals=0)


VMEM = pl.BlockSpec(memory_space=pltpu.VMEM)
HBM = pl.BlockSpec(memory_space=pltpu.HBM)


def run_spread(gy_size, slots, pts, stiffness, links, owners, patch_slots, dw):
    blocks, points = links.shape
    inter, patch = owners.shape[1], dw.shape[2]
    entries = blocks * inter
    return pl.pallas_call(
        functools.partial(spread_kernel, gy_size, slots),
        in_specs=[HBM] * 6,
        out_specs=[VMEM, VMEM],
        out_shape=[
            jax.ShapeDtypeStruct((slots, 3 * patch + LANES), BF16),
            jax.ShapeDtypeStruct((entries, LANES), F32),
        ],
        scratch_shapes=[
            pltpu.VMEM(dw.shape, BF16),
            pltpu.VMEM((3, blocks, points), F32),
            pltpu.VMEM((3, entries, patch), F32),
            pltpu.VMEM((3, slots, entries), BF16),
            pltpu.VMEM((3, blocks, points), F32),
            pltpu.SMEM((blocks,), F32),
            pltpu.VMEM((blocks, points), jnp.int32),
            pltpu.VMEM((blocks, inter), jnp.int32),
            pltpu.VMEM((blocks, inter), jnp.int32),
            pltpu.SemaphoreType.DMA((blocks + 5,)),
        ],
        compiler_params=params(24),
        cost_estimate=cost(10**9, 9),
        name="spread",
    )(*[in_hbm(x) for x in (pts, stiffness, links, owners, patch_slots, dw)])


def run_edges(velocity):
    cells = velocity.shape[1]
    return pl.pallas_call(
        edge_kernel,
        in_specs=[HBM],
        out_specs=[VMEM, VMEM],
        out_shape=[jax.ShapeDtypeStruct((8, cells), F32)] * 2,
        scratch_shapes=[pltpu.VMEM((3, cells, LANES), F32)] * 2 + [pltpu.SemaphoreType.DMA((6,))],
        compiler_params=params(24),
        cost_estimate=cost(10**8, 3),
        name="edges",
    )(in_hbm(velocity))


def run_lines(velocity):
    layers, patch = velocity.shape[1], velocity.shape[3]
    tiles = patch // LANES
    return pl.pallas_call(
        line_kernel,
        in_specs=[HBM],
        out_specs=VMEM,
        out_shape=jax.ShapeDtypeStruct((3, 4 * layers, patch), F32),
        scratch_shapes=[pltpu.VMEM((2, tiles, 3, layers, 8, LANES), F32), pltpu.SemaphoreType.DMA((2 * tiles,))],
        compiler_params=params(24),
        cost_estimate=cost(10**8, 3),
        name="lines",
    )(in_hbm(velocity))


def run_rim(layer_rows, layers, rim_velocity, ahead, behind, received):
    patch, cells = rim_velocity.shape[2], ahead.shape[1]
    side = (6 * (patch // LANES) + 1, layers, LANES)
    return pl.pallas_call(
        functools.partial(rim_kernel, layer_rows),
        in_specs=[VMEM] * 4,
        out_specs=[VMEM] * 4,
        out_shape=[
            jax.ShapeDtypeStruct(side, BF16),
            jax.ShapeDtypeStruct(side, BF16),
            jax.ShapeDtypeStruct((2, 3, patch // LANES + 1, layers, LANES), F32),
            jax.ShapeDtypeStruct((3, cells, LANES), F32),
        ],
        compiler_params=params(24),
        cost_estimate=cost(10**8, 3),
        name="rim",
    )(rim_velocity, ahead, behind, received)


def run_first(layers, velocity, edge, received):
    cells, patch = velocity.shape[1:]
    block = (3, patch // LANES + 1, cells, LANES)
    return pl.pallas_call(
        functools.partial(first_kernel, layers),
        in_specs=[HBM, VMEM, VMEM],
        out_specs=VMEM,
        out_shape=jax.ShapeDtypeStruct(block, F32),
        scratch_shapes=[pltpu.VMEM(block, F32), pltpu.SemaphoreType.DMA((layers // 8 * (patch // LANES),))],
        compiler_params=params(24),
        cost_estimate=cost(2 * 10**9, 24),
        name="sweep_first",
    )(in_hbm(velocity), edge, received)


def run_last(layers, near, u1, rim, below_x, above_x, received, dw):
    count, cells = u1.shape[1:3]
    patch, slots = (count - 1) * LANES, received.shape[0]
    return pl.pallas_call(
        functools.partial(last_kernel, layers),
        in_specs=[VMEM] * 5 + [HBM],
        out_specs=[HBM, VMEM, VMEM, VMEM],
        out_shape=[
            jax.ShapeDtypeStruct((3, cells, patch), F32),
            jax.ShapeDtypeStruct((slots, 3 * patch), BF16),
            jax.ShapeDtypeStruct(u1.shape, F32),
            jax.ShapeDtypeStruct((near, *dw.shape[1:]), BF16),
        ],
        scratch_shapes=[
            pltpu.VMEM((2, 3, count - 1, layers, LANES), F32),
            pltpu.VMEM((2, 3, 2, count, layers, LANES), F32),
            pltpu.VMEM((3, cells, patch), F32),
            pltpu.VMEM((slots, cells), BF16),
            pltpu.SemaphoreType.DMA((layers // 4 + 1,)),
        ],
        input_output_aliases={0: 2},
        compiler_params=params(34),
        cost_estimate=cost(2 * 10**9, 16),
        name="sweep_last",
    )(u1, rim, below_x, above_x, received, in_hbm(dw))


def run_gather(pts, dest, returned, near_dw, dw):
    blocks, patch = dw.shape[0], dw.shape[2]
    return pl.pallas_call(
        gather_kernel,
        in_specs=[VMEM] * 4 + [HBM],
        out_specs=VMEM,
        out_shape=jax.ShapeDtypeStruct(pts.shape, F32),
        scratch_shapes=[
            pltpu.VMEM(dw.shape, BF16),
            pltpu.VMEM((3, dest.shape[0], patch), F32),
            pltpu.VMEM(pts.shape, F32),
            pltpu.SemaphoreType.DMA((blocks,)),
        ],
        compiler_params=params(24),
        cost_estimate=cost(10**9, 9),
        name="interp",
    )(pts, dest, returned, near_dw, in_hbm(dw))


def shards(velocity, fiber_points, stiffness, links, delta_weights, owners, patch_slots):
    blocks, inter, points, patch = delta_weights.shape
    layers, rows, columns = velocity.shape[1:]
    gx_size, gy_size = lax.axis_size("gx"), lax.axis_size("gy")
    devices = gx_size * gy_size
    slots, cells = devices * 2, layers * rows
    pts = fiber_points.transpose(1, 0, 2)
    dw = delta_weights.reshape(blocks, inter * points, patch)
    outgoing, dest = run_spread(
        gy_size, slots, pts, stiffness, links, owners.reshape(blocks, inter), patch_slots, dw
    )

    def exchange(rows_out):
        size = rows_out.shape[1]
        return lax.all_to_all(
            rows_out.reshape(devices, 2, size), ("gx", "gy"), split_axis=0, concat_axis=0, tiled=True
        ).reshape(slots, size)

    received = exchange(outgoing)

    flat = velocity.reshape(3, cells, columns)
    first, last = run_edges(flat)
    ahead = lax.ppermute(first, "gy", [((i + 1) % gy_size, i) for i in range(gy_size)])
    behind = lax.ppermute(last, "gy", [(i, (i + 1) % gy_size) for i in range(gy_size)])
    low_rows, high_rows, rim, edge = run_rim(rows, layers, run_lines(velocity), ahead, behind, received)

    up = [(i, (i + 1) % gx_size) for i in range(gx_size)]
    below_x = lax.ppermute(high_rows, "gx", up)
    above_x = lax.ppermute(low_rows, "gx", [(b, a) for a, b in up])
    u1 = run_first(layers, flat, edge, received)
    fluid, replies, _, near_dw = run_last(layers, NEAR, u1, rim, below_x, above_x, received, dw)
    moved = run_gather(pts, dest, exchange(replies), near_dw, dw)
    return fluid.reshape(3, layers, rows, columns), moved.transpose(1, 0, 2)


def solution(mesh):
    placed = (
        P(None, None, "gx", "gy"),
        P(("gx", "gy"), None, None),
        P(("gx", "gy")),
        P(("gx", "gy"), None),
        P(("gx", "gy"), None, None, None),
        P(("gx", "gy"), None, None),
        P(("gx", "gy"), None),
    )
    return jax.shard_map(
        shards,
        mesh=mesh,
        in_specs=placed,
        out_specs=(P(None, None, "gx", "gy"), P(("gx", "gy"), None, None)),
        check_vma=False,
    )
```
